32 devices in a mesh: groups: 2 (over y), ctx: 4 (over z), exp: 2 (over x), tp: 2 (over core).
Axes of the slice: x: 2, y: 2, z: 4, core: 2. Of those that a mesh axis runs over, the one named last changes fastest.
Arguments:
- queries: bfloat16 [4, 512, 20, 128], P(('groups', 'exp'), 'ctx', 'tp'), parts along dimension 0, may hold values from -9 to 9
- key_states: bfloat16 [4, 512, 4, 128], P(('groups', 'exp'), 'ctx', 'tp'), parts along dimension 0, may hold values from -9 to 9
- values: bfloat16 [4, 512, 4, 128], P(('groups', 'exp'), 'ctx', 'tp'), parts along dimension 0, may hold values from -6 to 6
- doc_ids: int32 [4, 512], P(('groups', 'exp'), 'ctx'), parts along dimension 0, may hold values from 0 to 3, never falling along the last dimension, each value on 1 to 256 neighbouring positions
- residual: bfloat16 [4, 512, 5120], P(('groups', 'exp'), ('ctx', 'tp')), parts along dimension 0, may hold values from -6 to 6
- out_proj: bfloat16 [2560, 5120], P('tp', 'ctx'), may hold values from -0.125 to 0.125
- norm_gain: bfloat16 [5120], replicated, may hold values from 0.5 to 1.5
- router: bfloat16 [5120, 64], P(None, 'exp'), may hold values from -0.078125 to 0.078125
- expert_ids: int32 [4, 512, 1], P(('groups', 'exp'), ('ctx', 'tp')), parts along dimension 0, may hold values from 0 to 63; in each aligned block of 64 rows (0 to 63, 64 to 127, ..., all dimensions but the last counted through in order) at most 2 rows name the same one
- keep_counts: int32 [128], P('groups'), parts along dimension 0, may hold values from 1 to 2
Outputs:
- expert_inputs: bfloat16 [32, 64, 2, 5120], P(('groups', 'ctx', 'tp'), 'exp'), parts along dimension 0
The draws below stay inside these ranges and needn't reach their ends.
There are 2 independent parts, one for each index of `groups`. The reference program is written for one: setup_inputs(seed, part) draws one part's arguments, and reference() takes and returns one part's arrays. A program takes and returns all parts, laid end to end along the dimension named above; an argument that names none is the same for every part. Nothing has to cross between parts.
Inputs may be any that keep to these rules, and one draw needn't show every extreme that they name: `doc_ids`: doc ids never fall along a request; a document holds at most 256 tokens, and some document holds exactly that many. `expert_ids`: in each aligned block of 64 tokens (the rows of one device) no expert is named more than 2 times, and in some blocks one expert is named exactly 2 times.
All inputs are finite; a program needn't handle non-finite values.
Results may differ from the reference program's by a relative error of at most 0.013.
Values may be sent and summed in bfloat16 or wider, within the bound.
No kernel may reach another device: no remote copies, remote signals or barrier semaphores. Data moves between devices by JAX's collectives and lax.ppermute only.
A program may use at most 64 MiB of HBM per device.

```python
import math
import jax
import jax.numpy as jnp
import numpy as np
from jax import lax

D = 5120
HEAD_DIMENSION = 128
EXPERTS = 64
QUERY_HEADS = 20
KEY_VALUE_HEADS = 4
CAP = 2
DOCS = 4
TOK_DEV = 128
REQUEST_COUNT = 2
REQUEST_TOKENS = 512
N_CTX = 4
N_TP = 2


def query_key_pair(key):
    folded = jax.random.fold_in(key, 5)
    query_key, state_random_key = jax.random.split(folded, 2)
    sampled_query = jnp.clip(jax.random.normal(query_key, (REQUEST_COUNT, REQUEST_TOKENS, QUERY_HEADS, HEAD_DIMENSION), jnp.float32), -4.0, 4.0)
    sampled_state = jnp.clip(jax.random.normal(state_random_key, (REQUEST_COUNT, REQUEST_TOKENS, KEY_VALUE_HEADS, HEAD_DIMENSION), jnp.float32), -4.0, 4.0)
    return (sampled_query, sampled_state)


def draw_queries(key, part):
    return query_key_pair(key)[0].astype(jnp.bfloat16)


def draw_key_states(key, part):
    return query_key_pair(key)[1].astype(jnp.bfloat16)


def draw_residual(key, part):
    folded = jax.random.fold_in(key, 11)
    noise_key, row_key, column_key = jax.random.split(folded, 3)
    row_scale = jnp.exp(jax.random.uniform(row_key, (REQUEST_COUNT, REQUEST_TOKENS, 1), jnp.float32, math.log(0.02), math.log(0.2)))
    column_scale = jnp.exp(jax.random.uniform(column_key, (1, 1, D), jnp.float32, math.log(0.33), math.log(3.3)))
    noise = jnp.clip(jax.random.normal(noise_key, (REQUEST_COUNT, REQUEST_TOKENS, D), jnp.float32), -4.0, 4.0)
    return (noise * row_scale * column_scale).astype(jnp.bfloat16)


def plant(result, own_key, least, largest):
    longest = result.shape.index(max(result.shape))
    spots = []
    for shift in (0, 1):
        where = [jax.random.randint(jax.random.fold_in(own_key, axis), (), 0, length) for axis, length in enumerate(result.shape)]
        where[longest] = (where[longest] + shift) % result.shape[longest]
        spots.append(tuple(where))
    return result.at[spots[0]].set(least).at[spots[1]].set(largest)


def level_of(key, dims, shards, smallest, top_value):
    level = 1.0
    for dim, shards_of in shards:
        steps = jax.random.uniform(jax.random.fold_in(jax.random.fold_in(key, 6), dim), (shards_of,), jnp.float32, smallest / len(shards), top_value / len(shards))
        level = level * jnp.repeat(jnp.exp(steps), dims[dim] // shards_of).reshape((-1,) + (1,) * (len(dims) - 1 - dim))
    return level


def length_profile(amount, total, most, skew):
    portions = [(1 << 20) // math.isqrt(rank ** skew) + 1 for rank in range(2, amount + 1)]
    spare, counts = total - most - (amount - 1), [1] * (amount - 1)
    while spare > 0:
        free = [i for i in range(amount - 1) if counts[i] < most]
        pool, left = sum([portions[i] for i in free]), spare
        for i in free:
            addition = min(most - counts[i], max(1, left * portions[i] // pool), spare)
            counts[i] = counts[i] + addition
            spare = spare - addition
    return np.array([most] + counts)


def uneven(key, count, total, most, lean):
    if count == 2:
        one = jax.random.randint(key, (), max(1, total - most), min(most, total - 1) + 1)
        return jnp.stack([one, total - one])
    tallies = jnp.asarray(length_profile(count, total, most, lean), jnp.int32)
    twos = (count - 1) // 2
    donor, receiver = tallies[1:1 + 2 * twos:2], tallies[2:2 + 2 * twos:2]
    room = jnp.minimum(donor - 1, most - receiver)
    shifted = jax.random.randint(jax.random.fold_in(key, 1), (twos,), 0, 1 << 20) % (room + 1)
    tallies = tallies.at[1:1 + 2 * twos:2].set(donor - shifted).at[2:2 + 2 * twos:2].set(receiver + shifted)
    return tallies[jax.random.permutation(jax.random.fold_in(key, 2), count)]


def assign_block(key, own, number, rows, number_of, top, reach, lean):
    order = jax.random.permutation(key, number_of)
    crowded, usual = load_shares(number_of, rows * top, reach, lean, True), load_shares(number_of, rows * top, reach, lean, False)
    places = jnp.arange(number_of)

    def named(lengths, rotation):
        used = int((lengths > 0).sum())
        fixed = max(1, used // 4)
        passed = fixed + (places - fixed + rotation * (used - fixed)) % max(1, number_of - fixed)
        return jnp.zeros((number_of,), jnp.int32).at[order[jnp.where(places < fixed, places, passed)]].set(jnp.asarray(lengths, jnp.int32))

    lengths = jnp.where(number % 4 == 0, named(crowded, number // 4), named(usual, number - number // 4 - 1))
    mixed = jax.random.permutation(jax.random.fold_in(own, 3), number_of)
    source_of, receiver = mixed[0:number_of // 2 * 2:2], mixed[1:number_of // 2 * 2:2]
    room = jnp.minimum(lengths[source_of] - 1, reach - lengths[receiver]) // 2
    room = jnp.where((source_of == order[0]) | (receiver == order[0]) | (lengths[receiver] == 0), 0, jnp.maximum(room, 0))
    passed = jax.random.randint(jax.random.fold_in(own, 4), (number_of // 2,), 0, 1 << 20) % (room + 1)
    lengths = lengths.at[source_of].add(-passed).at[receiver].add(passed)
    items = jnp.searchsorted(jnp.cumsum(lengths), jnp.arange(rows * top), side="right").astype(jnp.int32)
    listing = items.reshape(top, rows).T
    listing = listing[jax.random.permutation(jax.random.fold_in(own, 1), rows)]
    rotation = jax.random.randint(jax.random.fold_in(own, 2), (rows, 1), 0, top)
    return jnp.take_along_axis(listing, (jnp.arange(top)[None, :] + rotation) % top, axis=1)


def load_shares(amount, total, limit, skew, full):
    loads = [(1 << 20) // math.isqrt(rank ** skew) + 1 for rank in range(1, amount + 1)]
    largest = limit if full else min(limit, max(-(-total // amount), total * loads[0] // sum(loads)))
    least = 1 if total - largest >= amount - 1 else 0
    holding, spare = [largest] + [least] * (amount - 1), total - largest - least * (amount - 1)
    while spare > 0:
        movable = [i for i in range(1, amount) if holding[i] < largest] or [i for i in range(1, amount) if holding[i] < limit]
        pool, remaining = sum([loads[i] for i in movable]), spare
        for i in movable:
            more = min(limit - holding[i], max(1, remaining * loads[i] // pool), spare)
            holding[i] = holding[i] + more
            spare = spare - more
    return np.array(holding)


def scatter_about(own_key, shape, deviation, reach, cuts=(), kind=jnp.bfloat16):
    entries = jax.random.normal(own_key, shape, jnp.float32) * deviation
    if len(cuts) > 0:
        entries = level_of(own_key, shape, cuts, -0.22, 0.18) * entries
    return jnp.clip(entries, min=-reach, max=reach).astype(kind)


def setup_inputs(seed: int = 0, part: int = 0) -> dict:
    key_of = jax.random.split(jax.random.key(seed), 11)
    part_splits = jax.random.split(jax.random.fold_in(key_of[10], part), 11)
    queries = draw_queries(jax.random.fold_in(jax.random.fold_in(key_of[10], part), 71), part)
    key_states = draw_key_states(jax.random.fold_in(jax.random.fold_in(key_of[10], part), 71), part)
    values = scatter_about(part_splits[2], (REQUEST_COUNT, REQUEST_TOKENS, KEY_VALUE_HEADS, HEAD_DIMENSION), 1.0, 6.0, ((0, 2), (1, 4), (2, 2)))
    doc_ids = jax.vmap(lambda own: jnp.searchsorted(jnp.cumsum(uneven(own, DOCS, REQUEST_TOKENS, REQUEST_TOKENS // 2, 0)), jnp.arange(REQUEST_TOKENS), side="right"))(jax.random.split(part_splits[3], REQUEST_COUNT)).reshape((REQUEST_COUNT, REQUEST_TOKENS)).astype(jnp.int32)
    residual = draw_residual(jax.random.fold_in(jax.random.fold_in(key_of[10], part), 71), part)
    out_proj = scatter_about(key_of[5], (QUERY_HEADS * HEAD_DIMENSION, D), (QUERY_HEADS * HEAD_DIMENSION) ** -0.5, 0.125, ((0, 2), (1, 4)))
    norm_gain = jnp.clip(1.0 + 0.1 * jax.random.normal(key_of[6], (D,), jnp.float32), 0.5, 1.5).astype(jnp.bfloat16)
    router = scatter_about(key_of[7], (D, EXPERTS), D ** -0.5, 0.078125, ((1, 2),))
    expert_ids_keys = jax.random.split(jax.random.fold_in(part_splits[8], 1), REQUEST_COUNT * REQUEST_TOKENS // (TOK_DEV // N_TP))
    expert_ids_turns = jax.random.permutation(jax.random.fold_in(part_splits[8], 3), REQUEST_COUNT * REQUEST_TOKENS // (TOK_DEV // N_TP))
    expert_ids = jax.vmap(lambda own, number: assign_block(jax.random.fold_in(part_splits[8], 2), own, number, TOK_DEV // N_TP, EXPERTS, 1, CAP, 2))(expert_ids_keys, expert_ids_turns).reshape((REQUEST_COUNT, REQUEST_TOKENS, 1))
    keep_counts = plant(jax.random.randint(part_splits[9], (EXPERTS,), 1, CAP + 1), jax.random.fold_in(part_splits[9], 1), 1, CAP).astype(jnp.int32)
    return dict(queries=queries, key_states=key_states, values=values, doc_ids=doc_ids, residual=residual, out_proj=out_proj, norm_gain=norm_gain, router=router, expert_ids=expert_ids, keep_counts=keep_counts)


EPSILON = 1e-05

def reference(queries, key_states, values, doc_ids, residual, out_proj, norm_gain, router, expert_ids, keep_counts):
    mixing_ratio = QUERY_HEADS // KEY_VALUE_HEADS
    scale = 1.0 / math.sqrt(HEAD_DIMENSION)
    position = jnp.arange(REQUEST_TOKENS, dtype=jnp.int32)

    def attend_head_group(flattened_index):
        request_number = flattened_index // KEY_VALUE_HEADS
        head_group = flattened_index % KEY_VALUE_HEADS
        query_rows = lax.dynamic_index_in_dim(queries, request_number, 0, False)
        query_rows = lax.dynamic_slice_in_dim(query_rows, head_group * mixing_ratio, mixing_ratio, 1)
        key_rows = lax.dynamic_index_in_dim(lax.dynamic_index_in_dim(key_states, request_number, 0, False), head_group, 1, False)
        value_rows = lax.dynamic_index_in_dim(lax.dynamic_index_in_dim(values, request_number, 0, False), head_group, 1, False)
        documents = lax.dynamic_index_in_dim(doc_ids, request_number, 0, False)
        scores = jnp.einsum('qrd,kd->rqk', query_rows.astype(jnp.float32), key_rows.astype(jnp.float32)) * scale
        allowed = (position[None, :] <= position[:, None]) & (documents[None, :] == documents[:, None])
        masked = jnp.where(allowed[None], scores, -jnp.inf)
        highest = lax.optimization_barrier(jnp.max(masked, axis=2, keepdims=True))
        weights = jnp.where(allowed[None], jnp.exp(scores - highest), 0.0)
        totals = lax.optimization_barrier(jnp.sum(weights, axis=2, keepdims=True))
        rounded = weights.astype(jnp.bfloat16).astype(jnp.float32)
        summed = jnp.einsum('rqk,kd->rqd', rounded, value_rows.astype(jnp.float32))
        return (summed / totals).astype(jnp.bfloat16)
    head_list = lax.map(attend_head_group, jnp.arange(REQUEST_COUNT * KEY_VALUE_HEADS, dtype=jnp.int32))
    blended_output = head_list.reshape(REQUEST_COUNT, KEY_VALUE_HEADS, mixing_ratio, REQUEST_TOKENS, HEAD_DIMENSION).transpose(0, 3, 1, 2, 4).reshape(REQUEST_COUNT * REQUEST_TOKENS, QUERY_HEADS * HEAD_DIMENSION)
    projected = jnp.dot(blended_output, out_proj, preferred_element_type=jnp.float32).reshape(REQUEST_COUNT, REQUEST_TOKENS, D)
    hidden = residual.astype(jnp.float32) + projected
    power = lax.optimization_barrier(jnp.mean(hidden * hidden, axis=2, keepdims=True))
    normed = (hidden * lax.rsqrt(power + EPSILON) * norm_gain.astype(jnp.float32)).astype(jnp.bfloat16)
    blocks = N_CTX * N_TP
    block_rows = TOK_DEV // N_TP
    normed_blocks = normed.reshape(REQUEST_COUNT, blocks, block_rows, D)
    id_blocks = expert_ids.reshape(REQUEST_COUNT, blocks, block_rows)
    expert_iota = jnp.arange(EXPERTS, dtype=jnp.int32)
    slot_iota = jnp.arange(EXPERTS * CAP, dtype=jnp.int32)
    router_wide = router.astype(jnp.float32)

    def route_block(flattened_index):
        block = flattened_index // REQUEST_COUNT
        request_number = flattened_index % REQUEST_COUNT
        token_rows = lax.dynamic_index_in_dim(lax.dynamic_index_in_dim(normed_blocks, request_number, 0, False), block, 0, False)
        chosen = lax.dynamic_index_in_dim(lax.dynamic_index_in_dim(id_blocks, request_number, 0, False), block, 0, False)
        onehot = (chosen[:, None] == expert_iota[None, :]).astype(jnp.int32)
        earlier = jnp.cumsum(onehot, axis=0) - onehot
        ranking = lax.optimization_barrier(jnp.sum(onehot * earlier, axis=1))
        limits = lax.optimization_barrier(jnp.sum(onehot * keep_counts[None, :], axis=1))
        kept = ranking < limits
        target = chosen * CAP + ranking
        table = (slot_iota[:, None] == target[None, :]) & kept[None, :]
        slots = jnp.dot(table.astype(jnp.bfloat16), token_rows, preferred_element_type=jnp.float32)
        slots = slots.astype(jnp.bfloat16).astype(jnp.float32).reshape(EXPERTS, CAP, D)
        logits = jnp.einsum('ecd,de->ec', slots, router_wide)
        return (slots * jax.nn.sigmoid(logits)[..., None]).astype(jnp.bfloat16)
    return lax.map(route_block, jnp.arange(blocks * REQUEST_COUNT, dtype=jnp.int32))
```

```python
import functools
import math

import jax
import jax.numpy as jnp
from jax import lax
from jax.experimental import pallas as pl
from jax.experimental.pallas import tpu as pltpu
from jax.sharding import PartitionSpec as P

CAP = 2
EPSILON = 1e-05
DOC_ROWS = 16
VMEM_LIMIT = 40 * 1024 * 1024


def attention_kernel(ratio, pair, core_ref, query_ref, doc_ref, *refs):
    pack_refs, out_refs = refs[:-pair], refs[-pair:]
    heads, tokens, head_size = query_ref.shape
    groups = heads // ratio
    scale = 1.0 / math.sqrt(head_size)
    own_doc = doc_ref[...]
    rows = lax.broadcasted_iota(jnp.int32, (tokens, tokens), 0)
    columns = lax.broadcasted_iota(jnp.int32, (tokens, tokens), 1)
    allowed = []
    for place, ref in enumerate(pack_refs):
        docs = ref[2 * groups * tokens : 2 * groups * tokens + 1, :].astype(jnp.float32)
        same = own_doc == docs
        allowed.append(same & (columns <= rows) if place == 0 else same)
    allowed = jnp.concatenate(allowed, axis=1)
    core = core_ref[0]
    part_rows = tokens // pair
    for group in range(groups):
        first = group * tokens
        keys = jnp.concatenate([ref[first : first + tokens, :] for ref in pack_refs], axis=0)
        first = (groups + group) * tokens
        held = jnp.concatenate([ref[first : first + tokens, :] for ref in pack_refs], axis=0)
        for head in range(group * ratio, (group + 1) * ratio):
            scores = lax.dot_general(
                query_ref[head], keys, (((1,), (1,)), ((), ())), preferred_element_type=jnp.float32
            )
            scores = jnp.where(allowed, scores * scale, -1e30)
            weights = jnp.exp(scores - jnp.max(scores, axis=1, keepdims=True))
            totals = jnp.sum(weights, axis=1, keepdims=True)
            mixed = jnp.dot(
                weights.astype(jnp.bfloat16), held, preferred_element_type=jnp.float32
            )
            mixed = (mixed / totals).astype(jnp.bfloat16)
            parts = [mixed[i * part_rows : (i + 1) * part_rows] for i in range(pair)]
            for turn in range(pair):
                piece = parts[turn]
                for own in range(1, pair):
                    piece = jnp.where(core == own, parts[(own + turn) % pair], piece)
                out_refs[turn][:, head * head_size : (head + 1) * head_size] = piece


def finish_kernel(steps, exp_count, place_ref, *refs):
    chunk_refs = refs[: steps * exp_count]
    rest = refs[steps * exp_count :]
    residual_refs, id_refs = rest[:exp_count], rest[exp_count : 2 * exp_count]
    keep_ref, gain_ref, router_ref, out_ref, hidden_ref, normed_ref = rest[2 * exp_count :]
    rows, width = residual_refs[0].shape
    columns = chunk_refs[0].shape[1]
    experts = keep_ref.shape[1]
    here = router_ref.shape[0]
    ctx_index, exp_index = place_ref[0], place_ref[1]
    keep = keep_ref[...].astype(jnp.float32)
    upper = (
        lax.broadcasted_iota(jnp.int32, (rows, rows), 0)
        < lax.broadcasted_iota(jnp.int32, (rows, rows), 1)
    ).astype(jnp.bfloat16)
    for back in range(exp_count):
        power = jnp.zeros((rows, 1), jnp.float32)
        for step in range(steps):
            first = 0 if steps == 1 else lax.rem(ctx_index + step, steps) * columns
            part = pl.ds(pl.multiple_of(first, 128), columns)
            hidden = residual_refs[back][:, part].astype(jnp.float32) + chunk_refs[
                step * exp_count + back
            ][...].astype(jnp.float32)
            hidden_ref[:, part] = hidden
            power = power + jnp.sum(hidden * hidden, axis=1, keepdims=True)
        factor = lax.rsqrt(power / width + EPSILON)
        normed_ref[...] = (
            hidden_ref[...] * factor * gain_ref[...].astype(jnp.float32)
        ).astype(jnp.bfloat16)
        ids = id_refs[back][...]
        onehot = ids == lax.broadcasted_iota(jnp.int32, (experts, rows), 0)
        onehot_wide = onehot.astype(jnp.float32)
        earlier = jnp.dot(
            onehot_wide.astype(jnp.bfloat16), upper, preferred_element_type=jnp.float32
        )
        ranking = jnp.sum(onehot_wide * earlier, axis=0, keepdims=True)
        limits = jnp.dot(
            keep.astype(jnp.bfloat16),
            onehot_wide.astype(jnp.bfloat16),
            preferred_element_type=jnp.float32,
        )
        local = ids - exp_index * here
        logits = lax.dot_general(
            router_ref[...],
            normed_ref[...],
            (((1,), (1,)), ((), ())),
            preferred_element_type=jnp.float32,
        )
        chosen = local == lax.broadcasted_iota(jnp.int32, (here, rows), 0)
        gates = jax.nn.sigmoid(jnp.sum(jnp.where(chosen, logits, 0.0), axis=0, keepdims=True))
        target = local * CAP + ranking.astype(jnp.int32)
        target = jnp.where((ranking < limits) & (local >= 0) & (local < here), target, -1)
        table = lax.broadcasted_iota(jnp.int32, (here * CAP, rows), 0) == target
        slot_gates = jnp.sum(jnp.where(table, gates, 0.0), axis=1, keepdims=True)
        slots = jnp.dot(
            table.astype(jnp.bfloat16), normed_ref[...], preferred_element_type=jnp.float32
        )
        source = lax.rem(exp_index - back + exp_count, exp_count)
        out_ref[source] = (slots * slot_gates).astype(jnp.bfloat16)


def on_device(
    queries,
    key_states,
    values,
    doc_ids,
    residual,
    out_proj,
    norm_gain,
    router,
    expert_ids,
    keep_counts,
):
    _, tokens, heads, head_size = queries.shape
    groups = key_states.shape[2]
    ctx_count = lax.axis_size("ctx")
    pair = lax.axis_size("tp")
    exp_count = lax.axis_size("exp")
    part_rows = tokens // pair
    width = residual.shape[2]
    columns = out_proj.shape[1]
    ctx_index = lax.axis_index("ctx")
    core = lax.axis_index("tp")
    exp_index = lax.axis_index("exp")
    reach = -(-(ctx_count * tokens // 2 - 1) // tokens)

    docs = (doc_ids + 1).astype(jnp.bfloat16)
    pack = jnp.concatenate(
        [
            key_states[0].transpose(1, 0, 2).reshape(groups * tokens, head_size),
            values[0].transpose(1, 0, 2).reshape(groups * tokens, head_size),
            jnp.broadcast_to(docs, (DOC_ROWS, tokens)),
        ],
        axis=0,
    )
    packs = [pack] + [
        lax.ppermute(pack, "ctx", [(i, i + step) for i in range(ctx_count - step)])
        for step in range(1, reach + 1)
    ]
    weights = [out_proj] + [
        lax.ppermute(out_proj, "tp", [(i, (i + turn) % pair) for i in range(pair)])
        for turn in range(1, pair)
    ]

    def over_exp(array, back):
        if back == 0:
            return array
        return lax.ppermute(
            array, "exp", [(i, (i + back) % exp_count) for i in range(exp_count)]
        )

    ids = expert_ids[:, :, 0]
    all_ids = [over_exp(ids, back) for back in range(exp_count)]
    all_residual = [over_exp(residual[0], back) for back in range(exp_count)]

    vmem = pl.BlockSpec(memory_space=pltpu.VMEM)
    smem = pl.BlockSpec(memory_space=pltpu.SMEM)
    pieces = pl.pallas_call(
        functools.partial(attention_kernel, heads // groups, pair),
        out_shape=[jax.ShapeDtypeStruct((part_rows, heads * head_size), jnp.bfloat16)] * pair,
        in_specs=[smem] + [vmem] * (2 + len(packs)),
        out_specs=[vmem] * pair,
        compiler_params=pltpu.CompilerParams(vmem_limit_bytes=VMEM_LIMIT),
    )(
        core.reshape(1),
        queries[0].transpose(1, 0, 2),
        (doc_ids + 1).astype(jnp.float32).reshape(tokens, 1),
        *packs,
    )

    arrived = {}
    for step in range(ctx_count):
        for turn in range(pair):
            moves = [
                (z * pair + c, (z + step) % ctx_count * pair + (c + turn) % pair)
                for z in range(ctx_count)
                for c in range(pair)
            ]
            arrived[step, turn] = (
                pieces[0]
                if step == 0 and turn == 0
                else lax.ppermute(pieces[turn], ("ctx", "tp"), moves)
            )
    order = sorted(range(ctx_count), key=lambda step: min(step, ctx_count - step))
    chunks = {}
    for step in order:
        total = sum(
            jnp.dot(arrived[step, turn], weights[turn], preferred_element_type=jnp.float32)
            for turn in range(pair)
        ).astype(jnp.bfloat16)
        away = (ctx_count - step) % ctx_count
        if away:
            total = lax.ppermute(
                total, "ctx", [(z, (z + away) % ctx_count) for z in range(ctx_count)]
            )
        chunks[step] = total
    steps = ctx_count
    if columns % 128:
        steps = 1
        whole = jnp.roll(jnp.stack([chunks[step] for step in range(ctx_count)]), ctx_index, axis=0)
        chunks = {0: whole.transpose(1, 0, 2).reshape(part_rows, width)}
    flat = [over_exp(chunks[step], back) for step in range(steps) for back in range(exp_count)]
    out = pl.pallas_call(
        functools.partial(finish_kernel, steps, exp_count),
        out_shape=jax.ShapeDtypeStruct(
            (exp_count, router.shape[1] * CAP, width), jnp.bfloat16
        ),
        in_specs=[smem] + [vmem] * (len(flat) + 2 * exp_count + 3),
        out_specs=vmem,
        scratch_shapes=[
            pltpu.VMEM((part_rows, width), jnp.float32),
            pltpu.VMEM((part_rows, width), jnp.bfloat16),
        ],
        compiler_params=pltpu.CompilerParams(vmem_limit_bytes=VMEM_LIMIT),
    )(
        jnp.stack([ctx_index, exp_index]),
        *flat,
        *all_residual,
        *all_ids,
        keep_counts.reshape(1, -1),
        norm_gain.reshape(1, -1),
        router.T,
    )
    return out.reshape(exp_count, router.shape[1], CAP, width)


def solution(mesh):
    placed = (
        P(("groups", "exp"), "ctx", "tp", None),
        P(("groups", "exp"), "ctx", "tp", None),
        P(("groups", "exp"), "ctx", "tp", None),
        P(("groups", "exp"), "ctx"),
        P(("groups", "exp"), ("ctx", "tp"), None),
        P("tp", "ctx"),
        P(),
        P(None, "exp"),
        P(("groups", "exp"), ("ctx", "tp"), None),
        P("groups"),
    )
    return jax.shard_map(
        on_device,
        mesh=mesh,
        in_specs=placed,
        out_specs=P(("groups", "ctx", "tp"), "exp", None, None),
        check_vma=False,
    )
```

```python
import functools
import math

import jax
import jax.numpy as jnp
from jax import lax
from jax.experimental import pallas as pl
from jax.experimental.pallas import tpu as pltpu
from jax.sharding import PartitionSpec as P

CAP = 2
EPSILON = 1e-05
DOC_ROWS = 16
VMEM_LIMIT = 16 * 1024 * 1024


def attention_kernel(ratio, groups, pair, packs, place_ref, query_ref, *refs):
    pack_refs, out_refs = refs[:packs], refs[-pair:]
    heads, tokens, head_size = query_ref.shape
    scale = 1.0 / math.sqrt(head_size)
    ctx_index, core = place_ref[0], place_ref[1]
    rows = lax.broadcasted_iota(jnp.int32, (tokens, tokens), 0)
    columns = lax.broadcasted_iota(jnp.int32, (tokens, tokens), 1)
    held_rows = groups * tokens
    docs = [ref[2 * held_rows : 2 * held_rows + 1, :].astype(jnp.float32) for ref in pack_refs]
    own_doc = jnp.sum(jnp.where(rows == columns, docs[0], 0.0), axis=1, keepdims=True)
    allowed = [(own_doc == docs[0]) & (columns <= rows)]
    for step in range(1, len(pack_refs)):
        allowed.append((own_doc == docs[step]) & (ctx_index >= step))
    allowed = jnp.concatenate(allowed, axis=1)
    part_rows = tokens // pair
    token = lax.broadcasted_iota(jnp.int32, (tokens, held_rows), 0)
    row = lax.broadcasted_iota(jnp.int32, (tokens, held_rows), 1)

    def of_group(group, first):
        pick = (row == token * groups + group).astype(jnp.bfloat16)
        parts = [
            jnp.dot(pick, ref[first : first + held_rows, :], preferred_element_type=jnp.float32)
            for ref in pack_refs
        ]
        return jnp.concatenate(parts, axis=0).astype(jnp.bfloat16)

    for group in range(groups):
        keys, held = of_group(group, 0), of_group(group, held_rows)
        for head in range(group * ratio, (group + 1) * ratio):
            scores = lax.dot_general(
                query_ref[head], keys, (((1,), (1,)), ((), ())), preferred_element_type=jnp.float32
            )
            scores = jnp.where(allowed, scores * scale, -1e30)
            weights = jnp.exp(scores - jnp.max(scores, axis=1, keepdims=True))
            totals = jnp.sum(weights, axis=1, keepdims=True)
            mixed = jnp.dot(
                weights.astype(jnp.bfloat16), held, preferred_element_type=jnp.float32
            )
            mixed = (mixed / totals).astype(jnp.bfloat16)
            parts = [mixed[i * part_rows : (i + 1) * part_rows] for i in range(pair)]
            for turn in range(pair):
                piece = parts[turn]
                for own in range(1, pair):
                    piece = jnp.where(core == own, parts[(own + turn) % pair], piece)
                out_refs[turn][:, head * head_size : (head + 1) * head_size] = piece


def project_kernel(pair, block_ref, *refs):
    weight_refs, out_ref = refs[:pair], refs[pair]
    depth = weight_refs[0].shape[0]
    total = jnp.zeros(out_ref.shape, jnp.float32)
    for turn in range(pair):
        total = total + jnp.dot(
            block_ref[:, turn * depth : (turn + 1) * depth],
            weight_refs[turn][...],
            preferred_element_type=jnp.float32,
        )
    out_ref[...] = total.astype(out_ref.dtype)


def finish_kernel(steps, exp_count, place_ref, *refs):
    chunk_refs = refs[: steps * exp_count]
    rest = refs[steps * exp_count :]
    residual_refs, id_refs = rest[:exp_count], rest[exp_count : 2 * exp_count]
    keep_ref, gain_ref, router_ref, out_ref, hidden_ref, normed_ref = rest[2 * exp_count :]
    rows, width = residual_refs[0].shape
    columns = chunk_refs[0].shape[1]
    experts = keep_ref.shape[1]
    here = router_ref.shape[0]
    ctx_index, exp_index = place_ref[0], place_ref[1]
    keep = keep_ref[...].astype(jnp.float32)
    upper = (
        lax.broadcasted_iota(jnp.int32, (rows, rows), 0)
        < lax.broadcasted_iota(jnp.int32, (rows, rows), 1)
    ).astype(jnp.bfloat16)
    for back in range(exp_count):
        power = jnp.zeros((rows, 1), jnp.float32)
        for step in range(steps):
            first = 0 if steps == 1 else lax.rem(ctx_index + step, steps) * columns
            part = pl.ds(pl.multiple_of(first, 128), columns)
            hidden = residual_refs[back][:, part].astype(jnp.float32) + chunk_refs[
                step * exp_count + back
            ][...].astype(jnp.float32)
            hidden_ref[:, part] = hidden
            power = power + jnp.sum(hidden * hidden, axis=1, keepdims=True)
        factor = lax.rsqrt(power / width + EPSILON)
        normed_ref[...] = (
            hidden_ref[...] * factor * gain_ref[...].astype(jnp.float32)
        ).astype(jnp.bfloat16)
        ids = id_refs[back][...]
        onehot = ids == lax.broadcasted_iota(jnp.int32, (experts, rows), 0)
        onehot_wide = onehot.astype(jnp.float32)
        earlier = jnp.dot(
            onehot_wide.astype(jnp.bfloat16), upper, preferred_element_type=jnp.float32
        )
        ranking = jnp.sum(onehot_wide * earlier, axis=0, keepdims=True)
        limits = jnp.dot(
            keep.astype(jnp.bfloat16),
            onehot_wide.astype(jnp.bfloat16),
            preferred_element_type=jnp.float32,
        )
        local = ids - exp_index * here
        logits = lax.dot_general(
            router_ref[...],
            normed_ref[...],
            (((1,), (1,)), ((), ())),
            preferred_element_type=jnp.float32,
        )
        chosen = local == lax.broadcasted_iota(jnp.int32, (here, rows), 0)
        gates = jax.nn.sigmoid(jnp.sum(jnp.where(chosen, logits, 0.0), axis=0, keepdims=True))
        target = local * CAP + ranking.astype(jnp.int32)
        target = jnp.where((ranking < limits) & (local >= 0) & (local < here), target, -1)
        table = lax.broadcasted_iota(jnp.int32, (here * CAP, rows), 0) == target
        slot_gates = jnp.sum(jnp.where(table, gates, 0.0), axis=1, keepdims=True)
        slots = jnp.dot(
            table.astype(jnp.bfloat16), normed_ref[...], preferred_element_type=jnp.float32
        )
        source = lax.rem(exp_index - back + exp_count, exp_count)
        out_ref[source] = (slots * slot_gates).astype(jnp.bfloat16)


def on_device(
    queries,
    key_states,
    values,
    doc_ids,
    residual,
    out_proj,
    norm_gain,
    router,
    expert_ids,
    keep_counts,
):
    _, tokens, heads, head_size = queries.shape
    groups = key_states.shape[2]
    ctx_count = lax.axis_size("ctx")
    pair = lax.axis_size("tp")
    exp_count = lax.axis_size("exp")
    part_rows = tokens // pair
    width = residual.shape[2]
    columns = out_proj.shape[1]
    ctx_index = lax.axis_index("ctx")
    core = lax.axis_index("tp")
    exp_index = lax.axis_index("exp")
    reach = -(-(ctx_count * tokens // 2 - 1) // tokens)

    def over(array, axis, step):
        count = lax.axis_size(axis)
        if step % count == 0:
            return array
        return lax.ppermute(array, axis, [(i, (i + step) % count) for i in range(count)])

    pack = jnp.concatenate(
        [
            key_states.reshape(groups * tokens, head_size),
            values.reshape(groups * tokens, head_size),
            jnp.broadcast_to(doc_ids.astype(jnp.bfloat16), (DOC_ROWS, tokens)),
        ],
        axis=0,
    )
    packs = [over(pack, "ctx", step) for step in range(reach + 1)]
    weights = [over(out_proj, "tp", turn) for turn in range(pair)]
    ids = expert_ids[:, :, 0]
    all_ids = [over(ids, "exp", back) for back in range(exp_count)]
    all_residual = [over(residual[0], "exp", back) for back in range(exp_count)]

    vmem = pl.BlockSpec(memory_space=pltpu.VMEM)
    smem = pl.BlockSpec(memory_space=pltpu.SMEM)
    anywhere = pl.BlockSpec(memory_space=pl.ANY)
    early = weights[1:] + all_ids[1:] + all_residual[1:]
    pieces = pl.pallas_call(
        functools.partial(attention_kernel, heads // groups, groups, pair, len(packs)),
        out_shape=[jax.ShapeDtypeStruct((part_rows, heads * head_size), jnp.bfloat16)] * pair,
        in_specs=[smem] + [vmem] * (1 + len(packs)) + [anywhere] * len(early),
        out_specs=[vmem] * pair,
        compiler_params=pltpu.CompilerParams(vmem_limit_bytes=VMEM_LIMIT),
    )(
        jnp.stack([ctx_index, core]),
        queries[0].transpose(1, 0, 2),
        *packs,
        *early,
    )

    project = pl.pallas_call(
        functools.partial(project_kernel, pair),
        out_shape=jax.ShapeDtypeStruct((part_rows, columns), jnp.bfloat16),
        in_specs=[vmem] * (1 + pair),
        out_specs=vmem,
        cost_estimate=pl.CostEstimate(
            flops=2 * pair * part_rows * out_proj.size,
            bytes_accessed=2 * pair * out_proj.size,
            transcendentals=0,
        ),
        compiler_params=pltpu.CompilerParams(vmem_limit_bytes=VMEM_LIMIT),
    )
    block = jnp.concatenate([over(pieces[turn], "tp", turn) for turn in range(pair)], axis=1)
    aligned = columns % 128 == 0
    flat, chunks = [], []
    for step in range(ctx_count):
        following = over(block, "ctx", 1) if step < ctx_count - 1 else None
        if step >= 2 and aligned:
            block, flat[step - 2] = lax.optimization_barrier((block, flat[step - 2]))
        total = project(block, *weights)
        if following is not None:
            following, total = lax.optimization_barrier((following, total))
        chunk = over(total, "ctx", ctx_count - step)
        chunks.append(chunk)
        if aligned:
            flat.append([over(chunk, "exp", back) for back in range(exp_count)])
        block = following
    if not aligned:
        whole = jnp.roll(jnp.stack(chunks), ctx_index, axis=0)
        whole = whole.transpose(1, 0, 2).reshape(part_rows, width)
        flat = [[over(whole, "exp", back) for back in range(exp_count)]]
    steps = len(flat)
    flat = [array for arrays in flat for array in arrays]
    out = pl.pallas_call(
        functools.partial(finish_kernel, steps, exp_count),
        out_shape=jax.ShapeDtypeStruct(
            (exp_count, router.shape[1] * CAP, width), jnp.bfloat16
        ),
        in_specs=[smem] + [vmem] * (len(flat) + 2 * exp_count + 3),
        out_specs=vmem,
        scratch_shapes=[
            pltpu.VMEM((part_rows, width), jnp.float32),
            pltpu.VMEM((part_rows, width), jnp.bfloat16),
        ],
        compiler_params=pltpu.CompilerParams(vmem_limit_bytes=VMEM_LIMIT),
    )(
        jnp.stack([ctx_index, exp_index]),
        *flat,
        *all_residual,
        *all_ids,
        keep_counts.reshape(1, -1),
        norm_gain.reshape(1, -1),
        router.T,
    )
    return out.reshape(exp_count, router.shape[1], CAP, width)


def solution(mesh):
    placed = (
        P(("groups", "exp"), "ctx", "tp", None),
        P(("groups", "exp"), "ctx", "tp", None),
        P(("groups", "exp"), "ctx", "tp", None),
        P(("groups", "exp"), "ctx"),
        P(("groups", "exp"), ("ctx", "tp"), None),
        P("tp", "ctx"),
        P(),
        P(None, "exp"),
        P(("groups", "exp"), ("ctx", "tp"), None),
        P("groups"),
    )
    return jax.shard_map(
        on_device,
        mesh=mesh,
        in_specs=placed,
        out_specs=P(("groups", "ctx", "tp"), "exp", None, None),
        check_vma=False,
    )
```

```python
import functools
import math

import jax
import jax.numpy as jnp
from jax import lax
from jax.experimental import pallas as pl
from jax.experimental.pallas import tpu as pltpu
from jax.sharding import PartitionSpec as P

CAP = 2
EPSILON = 1e-05
DOC_ROWS = 16
VMEM_LIMIT = 28 * 1024 * 1024


def attention_kernel(ratio, groups, pair, packs, place_ref, query_ref, *refs):
    pack_refs, out_refs = refs[:packs], refs[-pair:]
    heads, tokens, head_size = query_ref.shape
    scale = 1.0 / math.sqrt(head_size)
    ctx_index, core = place_ref[0], place_ref[1]
    rows = lax.broadcasted_iota(jnp.int32, (tokens, tokens), 0)
    columns = lax.broadcasted_iota(jnp.int32, (tokens, tokens), 1)
    held_rows = groups * tokens
    docs = [ref[2 * held_rows : 2 * held_rows + 1, :].astype(jnp.float32) for ref in pack_refs]
    own_doc = jnp.sum(jnp.where(rows == columns, docs[0], 0.0), axis=1, keepdims=True)
    allowed = [(own_doc == docs[0]) & (columns <= rows)]
    for step in range(1, len(pack_refs)):
        allowed.append((own_doc == docs[step]) & (ctx_index >= step))
    allowed = jnp.concatenate(allowed, axis=1)
    part_rows = tokens // pair
    token = lax.broadcasted_iota(jnp.int32, (tokens, held_rows), 0)
    row = lax.broadcasted_iota(jnp.int32, (tokens, held_rows), 1)

    def of_group(group, first):
        pick = (row == token * groups + group).astype(jnp.bfloat16)
        parts = [
            jnp.dot(pick, ref[first : first + held_rows, :], preferred_element_type=jnp.float32)
            for ref in pack_refs
        ]
        return jnp.concatenate(parts, axis=0).astype(jnp.bfloat16)

    for group in range(groups):
        keys, held = of_group(group, 0), of_group(group, held_rows)
        for head in range(group * ratio, (group + 1) * ratio):
            scores = lax.dot_general(
                query_ref[head], keys, (((1,), (1,)), ((), ())), preferred_element_type=jnp.float32
            )
            scores = jnp.where(allowed, scores * scale, -1e30)
            weights = jnp.exp(scores - jnp.max(scores, axis=1, keepdims=True))
            totals = jnp.sum(weights, axis=1, keepdims=True)
            mixed = jnp.dot(
                weights.astype(jnp.bfloat16), held, preferred_element_type=jnp.float32
            )
            mixed = (mixed / totals).astype(jnp.bfloat16)
            parts = [mixed[i * part_rows : (i + 1) * part_rows] for i in range(pair)]
            for turn in range(pair):
                piece = parts[turn]
                for own in range(1, pair):
                    piece = jnp.where(core == own, parts[(own + turn) % pair], piece)
                out_refs[turn][:, head * head_size : (head + 1) * head_size] = piece


def project_kernel(pair, blocks, either, place_ref, *refs):
    block_refs, weight_refs, out_refs = refs[:blocks], refs[blocks : blocks + pair], refs[-1:]
    if not either:
        out_refs = refs[blocks + pair :]
    depth = weight_refs[0].shape[0]
    rows = block_refs[0].shape[0]
    total = None
    for turn in range(pair):
        parts = [ref[:, turn * depth : (turn + 1) * depth] for ref in block_refs]
        if either:
            parts = [jnp.where(place_ref[0] >= either, parts[0], parts[1])]
        product = jnp.dot(
            jnp.concatenate(parts, axis=0) if len(parts) > 1 else parts[0],
            weight_refs[turn][...],
            preferred_element_type=jnp.float32,
        )
        total = product if total is None else total + product
    for number, ref in enumerate(out_refs):
        ref[...] = total[number * rows : (number + 1) * rows].astype(ref.dtype)


def column_of(kind, distance, ctx_index, ctx_count):
    if kind == "own":
        return ctx_index, ctx_index >= 0
    above, below = ctx_index + distance, ctx_index - distance
    if kind == "above":
        return jnp.minimum(above, ctx_count - 1), above < ctx_count
    if kind == "below":
        return jnp.maximum(below, 0), below >= 0
    place = jnp.where(above < ctx_count, above, jnp.maximum(below, 0))
    return place, (above < ctx_count) | (below >= 0)


def finish_kernel(chunk_kinds, ctx_count, exp_count, place_ref, *refs):
    count = len(chunk_kinds)
    chunk_refs = refs[: count * exp_count]
    rest = refs[count * exp_count :]
    residual_refs, id_refs = rest[:exp_count], rest[exp_count : 2 * exp_count]
    keep_ref, gain_ref, router_ref, out_ref = rest[2 * exp_count : 2 * exp_count + 4]
    chunk_buffer, residual_buffer, hidden_ref, normed_ref, chunk_sems, residual_sems = rest[
        2 * exp_count + 4 :
    ]
    rows, width = residual_refs[0].shape
    columns = chunk_refs[0].shape[1]
    experts = keep_ref.shape[1]
    here = router_ref.shape[0]
    ctx_index, exp_index = place_ref[0], place_ref[1]
    chunk_copies = [
        pltpu.make_async_copy(ref, chunk_buffer.at[number], chunk_sems.at[number])
        for number, ref in enumerate(chunk_refs)
    ]
    residual_copies = [
        pltpu.make_async_copy(ref, residual_buffer.at[back], residual_sems.at[back])
        for back, ref in enumerate(residual_refs)
    ]
    for back in range(exp_count):
        residual_copies[back].start()
        for number in range(count):
            chunk_copies[number * exp_count + back].start()
    keep = keep_ref[...].astype(jnp.float32)
    upper = (
        lax.broadcasted_iota(jnp.int32, (rows, rows), 0)
        < lax.broadcasted_iota(jnp.int32, (rows, rows), 1)
    ).astype(jnp.bfloat16)
    for back in range(exp_count):
        residual_copies[back].wait()
        for number, (kind, distance) in enumerate(chunk_kinds):
            chunk_copies[number * exp_count + back].wait()
            place, valid = column_of(kind, distance, ctx_index, ctx_count)
            if columns == width:
                place, valid = 0, ctx_index >= 0

            @pl.when(valid)
            def _(number=number, place=place):
                part = pl.ds(pl.multiple_of(place * columns, 128), columns)
                hidden_ref[:, part] = residual_buffer[back, :, part].astype(
                    jnp.float32
                ) + chunk_buffer[number * exp_count + back].astype(jnp.float32)

        hidden = hidden_ref[...]
        power = jnp.sum(hidden * hidden, axis=1, keepdims=True)
        factor = lax.rsqrt(power / width + EPSILON)
        normed_ref[...] = (hidden * factor * gain_ref[...].astype(jnp.float32)).astype(
            jnp.bfloat16
        )
        ids = id_refs[back][...]
        onehot = ids == lax.broadcasted_iota(jnp.int32, (experts, rows), 0)
        onehot_wide = onehot.astype(jnp.float32)
        earlier = jnp.dot(
            onehot_wide.astype(jnp.bfloat16), upper, preferred_element_type=jnp.float32
        )
        ranking = jnp.sum(onehot_wide * earlier, axis=0, keepdims=True)
        limits = jnp.dot(
            keep.astype(jnp.bfloat16),
            onehot_wide.astype(jnp.bfloat16),
            preferred_element_type=jnp.float32,
        )
        local = ids - exp_index * here
        logits = lax.dot_general(
            router_ref[...],
            normed_ref[...],
            (((1,), (1,)), ((), ())),
            preferred_element_type=jnp.float32,
        )
        chosen = local == lax.broadcasted_iota(jnp.int32, (here, rows), 0)
        gates = jax.nn.sigmoid(jnp.sum(jnp.where(chosen, logits, 0.0), axis=0, keepdims=True))
        target = local * CAP + ranking.astype(jnp.int32)
        target = jnp.where((ranking < limits) & (local >= 0) & (local < here), target, -1)
        table = lax.broadcasted_iota(jnp.int32, (here * CAP, rows), 0) == target
        slot_gates = jnp.sum(jnp.where(table, gates, 0.0), axis=1, keepdims=True)
        slots = jnp.dot(
            table.astype(jnp.bfloat16), normed_ref[...], preferred_element_type=jnp.float32
        )
        source = lax.rem(exp_index - back + exp_count, exp_count)
        out_ref[source] = (slots * slot_gates).astype(jnp.bfloat16)


def on_device(
    queries,
    key_states,
    values,
    doc_ids,
    residual,
    out_proj,
    norm_gain,
    router,
    expert_ids,
    keep_counts,
):
    _, tokens, heads, head_size = queries.shape
    groups = key_states.shape[2]
    ctx_count = lax.axis_size("ctx")
    pair = lax.axis_size("tp")
    exp_count = lax.axis_size("exp")
    part_rows = tokens // pair
    width = residual.shape[2]
    columns = out_proj.shape[1]
    ctx_index = lax.axis_index("ctx")
    core = lax.axis_index("tp")
    exp_index = lax.axis_index("exp")
    reach = -(-(ctx_count * tokens // 2 - 1) // tokens)

    def over(array, axis, step):
        count = lax.axis_size(axis)
        if step % count == 0:
            return array
        return lax.ppermute(array, axis, [(i, (i + step) % count) for i in range(count)])

    pack = jnp.concatenate(
        [
            key_states.reshape(groups * tokens, head_size),
            values.reshape(groups * tokens, head_size),
            jnp.broadcast_to(doc_ids.astype(jnp.bfloat16), (DOC_ROWS, tokens)),
        ],
        axis=0,
    )
    packs = [over(pack, "ctx", step) for step in range(reach + 1)]
    weights = [over(out_proj, "tp", turn) for turn in range(pair)]
    ids = expert_ids[:, :, 0]
    all_ids = [over(ids, "exp", back) for back in range(exp_count)]
    all_residual = [over(residual[0], "exp", back) for back in range(exp_count)]

    vmem = pl.BlockSpec(memory_space=pltpu.VMEM)
    smem = pl.BlockSpec(memory_space=pltpu.SMEM)
    anywhere = pl.BlockSpec(memory_space=pl.ANY)
    pieces = pl.pallas_call(
        functools.partial(attention_kernel, heads // groups, groups, pair, len(packs)),
        out_shape=[jax.ShapeDtypeStruct((part_rows, heads * head_size), jnp.bfloat16)] * pair,
        in_specs=[smem] + [vmem] * (1 + len(packs)),
        out_specs=[vmem] * pair,
        compiler_params=pltpu.CompilerParams(vmem_limit_bytes=VMEM_LIMIT),
    )(
        jnp.stack([ctx_index, core]),
        queries[0].transpose(1, 0, 2),
        *packs,
    )

    def project(blocks, either=0):
        outputs = 1 if either else len(blocks)
        return pl.pallas_call(
            functools.partial(project_kernel, pair, len(blocks), either),
            out_shape=[jax.ShapeDtypeStruct((part_rows, columns), jnp.bfloat16)] * outputs,
            in_specs=[smem] + [vmem] * (len(blocks) + pair),
            out_specs=[vmem] * outputs,
            compiler_params=pltpu.CompilerParams(vmem_limit_bytes=VMEM_LIMIT),
            cost_estimate=pl.CostEstimate(
                flops=2 * pair * outputs * part_rows * out_proj.size,
                bytes_accessed=2 * pair * out_proj.size,
                transcendentals=0,
            ),
        )(ctx_index.reshape(1), *blocks, *weights)

    def along(array, moves):
        return lax.ppermute(array, "ctx", moves)

    block = jnp.concatenate([over(pieces[turn], "tp", turn) for turn in range(pair)], axis=1)
    block, weights, all_ids, all_residual = lax.optimization_barrier(
        (block, weights, all_ids, all_residual)
    )
    aligned = columns % 128 == 0

    def forward(chunk):
        return [over(chunk, "exp", back) for back in range(1, exp_count if aligned else 1)]

    kinds, chunks, sent = [], [], []
    rising = falling = block
    for distance in range(1, ctx_count + 1):
        last = distance == ctx_count
        if not last:
            coming = (
                along(rising, [(i, i + 1) for i in range(distance - 1, ctx_count - 1)]),
                along(falling, [(i, i - 1) for i in range(1, ctx_count - distance + 1)]),
            )
        held = distance - 1
        blocks = (rising, falling)
        if held >= 2:
            blocks, chunks[held - 1], sent[held - 2] = lax.optimization_barrier(
                (blocks, chunks[held - 1], sent[held - 2])
            )
        if held == 0:
            totals = project((block,))
        else:
            totals = project(blocks, either=held if 2 * held >= ctx_count else 0)
        if not last:
            (rising, falling), _ = lax.optimization_barrier((coming, totals))
        to_lower = [(i, i - held) for i in range(held, ctx_count)]
        to_upper = [(i, i + held) for i in range(ctx_count - held)]
        if held == 0:
            arrived = [("own", totals[0])]
        elif 2 * held >= ctx_count:
            arrived = [("either", along(totals[0], to_lower + to_upper))]
        else:
            arrived = [
                ("above", along(totals[0], to_lower)),
                ("below", along(totals[1], to_upper)),
            ]
        kinds += [(kind, held) for kind, _ in arrived]
        chunks.append([chunk for _, chunk in arrived])
        sent.append([forward(chunk) for _, chunk in arrived])
    flat = [
        [chunk] + others
        for group, others_of in zip(chunks, sent)
        for chunk, others in zip(group, others_of)
    ]
    if aligned:
        flat = [array for arrays in flat for array in arrays]
    else:
        whole = jnp.zeros((ctx_count, part_rows, columns), jnp.bfloat16)
        for (kind, distance), (chunk,) in zip(kinds, flat):
            place, valid = column_of(kind, distance, ctx_index, ctx_count)
            whole = whole.at[place].add(jnp.where(valid, chunk, 0))
        whole = whole.transpose(1, 0, 2).reshape(part_rows, width)
        flat = [over(whole, "exp", back) for back in range(exp_count)]
        kinds = [("own", 0)]
    out = pl.pallas_call(
        functools.partial(finish_kernel, kinds, ctx_count, exp_count),
        out_shape=jax.ShapeDtypeStruct(
            (exp_count, router.shape[1] * CAP, width), jnp.bfloat16
        ),
        in_specs=[smem] + [anywhere] * (len(flat) + exp_count) + [vmem] * (exp_count + 3),
        out_specs=vmem,
        scratch_shapes=[
            pltpu.VMEM((len(flat),) + flat[0].shape, jnp.bfloat16),
            pltpu.VMEM((exp_count, part_rows, width), jnp.bfloat16),
            pltpu.VMEM((part_rows, width), jnp.float32),
            pltpu.VMEM((part_rows, width), jnp.bfloat16),
            pltpu.SemaphoreType.DMA((len(flat),)),
            pltpu.SemaphoreType.DMA((exp_count,)),
        ],
        compiler_params=pltpu.CompilerParams(vmem_limit_bytes=VMEM_LIMIT),
    )(
        jnp.stack([ctx_index, exp_index]),
        *flat,
        *all_residual,
        *all_ids,
        keep_counts.reshape(1, -1),
        norm_gain.reshape(1, -1),
        router.T,
    )
    return out.reshape(exp_count, router.shape[1], CAP, width)


def solution(mesh):
    placed = (
        P(("groups", "exp"), "ctx", "tp", None),
        P(("groups", "exp"), "ctx", "tp", None),
        P(("groups", "exp"), "ctx", "tp", None),
        P(("groups", "exp"), "ctx"),
        P(("groups", "exp"), ("ctx", "tp"), None),
        P("tp", "ctx"),
        P(),
        P(None, "exp"),
        P(("groups", "exp"), ("ctx", "tp"), None),
        P("groups"),
    )
    return jax.shard_map(
        on_device,
        mesh=mesh,
        in_specs=placed,
        out_specs=P(("groups", "ctx", "tp"), "exp", None, None),
        check_vma=False,
    )
```

```python
import functools
import math

import jax
import jax.numpy as jnp
from jax import lax
from jax.experimental import pallas as pl
from jax.experimental.pallas import tpu as pltpu
from jax.sharding import PartitionSpec as P

CAP = 2
EPSILON = 1e-05
DOC_ROWS = 16
VMEM_LIMIT = 56 * 1024 * 1024


def fetch(refs, buffers, sems):
    copies = [
        pltpu.make_async_copy(ref, buffer, sems.at[number])
        for number, (ref, buffer) in enumerate(zip(refs, buffers))
    ]
    for copy in copies:
        copy.start()
    return [copy.wait for copy in copies]


def pack_kernel(groups, key_ref, value_ref, doc_ref, out_ref, *scratch):
    buffers, sems = scratch[:-1], scratch[-1]
    for wait in fetch((key_ref, value_ref, doc_ref), buffers, sems):
        wait()
    key_ref, value_ref, doc_ref = buffers
    rows, head_size = key_ref.shape
    tokens = rows // groups
    token = lax.broadcasted_iota(jnp.int32, (tokens, rows), 0)
    row = lax.broadcasted_iota(jnp.int32, (tokens, rows), 1)
    for group in range(groups):
        pick = (row == token * groups + group).astype(jnp.bfloat16)
        for place, ref in enumerate((key_ref, value_ref)):
            first = (place * groups + group) * tokens
            out_ref[first : first + tokens, :] = jnp.dot(
                pick, ref[...], preferred_element_type=jnp.float32
            ).astype(jnp.bfloat16)
    out_ref[2 * rows :, :] = jnp.broadcast_to(
        doc_ref[...].astype(jnp.float32), (DOC_ROWS, tokens)
    ).astype(jnp.bfloat16)


def block_kernel(ratio, groups, pair, reach, ctx_count, shifts, place_ref, *refs):
    count = len(shifts)
    operands = count + ctx_count + 1
    same_ref, cross_ref, mixed_ref = refs[operands : operands + 3]
    buffers, sems = refs[operands + 3 : -1], refs[-1]
    waits = fetch(refs[:operands], buffers, sems)
    for wait in waits[:-1]:
        wait()
    query_refs, pack_refs, weight_buffer = buffers[:count], buffers[count:-1], buffers[-1]
    heads, tokens, head_size = query_refs[0].shape
    scale = 1.0 / math.sqrt(head_size)
    ctx_index, core = place_ref[0], place_ref[1]
    part_rows = tokens // pair
    rows = lax.broadcasted_iota(jnp.int32, (tokens, tokens), 0)
    columns = lax.broadcasted_iota(jnp.int32, (tokens, tokens), 1)
    held_rows = groups * tokens

    def docs_of(ref):
        return ref[2 * held_rows : 2 * held_rows + 1, :].astype(jnp.float32)

    def attend(number, shift, spot):
        block_place = lax.rem(ctx_index - shift + ctx_count, ctx_count)
        packs = [pack_refs[(shift + step) % ctx_count] for step in range(reach + 1)]
        docs = docs_of(packs[0])
        own_doc = jnp.sum(jnp.where(rows == columns, docs, 0.0), axis=1, keepdims=True)
        allowed = [(own_doc == docs) & (columns <= rows)]
        for step in range(1, reach + 1):
            allowed.append((own_doc == docs_of(packs[step])) & (block_place >= step))
        allowed = jnp.concatenate(allowed, axis=1)
        for group in range(groups):
            first = group * tokens
            keys = jnp.concatenate([ref[first : first + tokens, :] for ref in packs], axis=0)
            first = held_rows + group * tokens
            held = jnp.concatenate([ref[first : first + tokens, :] for ref in packs], axis=0)
            for head in range(group * ratio, (group + 1) * ratio):
                scores = lax.dot_general(
                    query_refs[number][head],
                    keys,
                    (((1,), (1,)), ((), ())),
                    preferred_element_type=jnp.float32,
                )
                scores = jnp.where(allowed, scores * scale, -1e30)
                weights = jnp.exp(scores - jnp.max(scores, axis=1, keepdims=True))
                totals = jnp.sum(weights, axis=1, keepdims=True)
                mixed = jnp.dot(
                    weights.astype(jnp.bfloat16), held, preferred_element_type=jnp.float32
                )
                mixed_ref[spot, :, head * head_size : (head + 1) * head_size] = (
                    mixed / totals
                ).astype(jnp.bfloat16)

    def multiply(spot):
        product = jnp.dot(
            mixed_ref[spot], weight_buffer[...], preferred_element_type=jnp.float32
        )
        parts = [product[i * part_rows : (i + 1) * part_rows] for i in range(pair)]
        for turn in range(pair):
            piece = parts[turn]
            for own in range(1, pair):
                piece = jnp.where(core == own, parts[(own + turn) % pair], piece)
            if turn == 0:
                same_ref[spot] = piece
            else:
                cross_ref[turn - 1, spot] = piece.astype(jnp.bfloat16)

    outputs = same_ref.shape[0]
    valid = [
        ctx_index >= shift if number == 0 else ctx_index < shift
        for number, shift in enumerate(shifts)
    ]
    for number, shift in enumerate(shifts):
        pl.when(valid[number])(
            functools.partial(attend, number, shift, min(number, outputs - 1))
        )
    waits[-1]()
    if outputs < count:
        valid = [functools.reduce(jnp.logical_or, valid)]
    for spot in range(outputs):
        pl.when(valid[spot])(functools.partial(multiply, spot))


def column_of(kind, distance, ctx_index, ctx_count):
    if kind == "own":
        return ctx_index, ctx_index >= 0
    above, below = ctx_index + distance, ctx_index - distance
    if kind == "above":
        return jnp.minimum(above, ctx_count - 1), above < ctx_count
    if kind == "below":
        return jnp.maximum(below, 0), below >= 0
    place = jnp.where(above < ctx_count, above, jnp.maximum(below, 0))
    return place, (above < ctx_count) | (below >= 0)


def finish_kernel(kinds, back, ctx_count, exp_count, place_ref, *refs):
    count = len(kinds)
    operands = count + 2
    id_ref, keep_ref, gain_ref = refs[operands : operands + 3]
    out_ref, hidden_ref, normed_ref, result_ref = refs[-5 - operands - 1 :][:4]
    out_sem, buffers, sems = refs[-2 - operands], refs[-1 - operands : -1], refs[-1]
    waits = fetch(refs[:operands], buffers, sems)
    residual_ref, chunk_refs, router_ref = buffers[0], buffers[1:-1], buffers[-1]
    rows, width = residual_ref.shape
    experts = keep_ref.shape[1]
    here = router_ref.shape[0]
    ctx_index, exp_index = place_ref[0], place_ref[1]
    keep = keep_ref[...].astype(jnp.float32)
    upper = (
        lax.broadcasted_iota(jnp.int32, (rows, rows), 0)
        < lax.broadcasted_iota(jnp.int32, (rows, rows), 1)
    ).astype(jnp.bfloat16)
    ids = id_ref[...]
    onehot = (ids == lax.broadcasted_iota(jnp.int32, (experts, rows), 0)).astype(jnp.float32)
    earlier = jnp.dot(onehot.astype(jnp.bfloat16), upper, preferred_element_type=jnp.float32)
    ranking = jnp.sum(onehot * earlier, axis=0, keepdims=True)
    limits = jnp.dot(
        keep.astype(jnp.bfloat16),
        onehot.astype(jnp.bfloat16),
        preferred_element_type=jnp.float32,
    )
    local = ids - exp_index * here
    chosen = local == lax.broadcasted_iota(jnp.int32, (here, rows), 0)
    target = local * CAP + ranking.astype(jnp.int32)
    target = jnp.where((ranking < limits) & (local >= 0) & (local < here), target, -1)
    table = lax.broadcasted_iota(jnp.int32, (here * CAP, rows), 0) == target
    waits[0]()
    for number, (kind, distance) in enumerate(kinds):
        waits[1 + number]()
        chunk_ref = chunk_refs[number]
        columns = chunk_ref.shape[1]
        place, valid = column_of(kind, distance, ctx_index, ctx_count)
        if columns == width:
            place, valid = 0, ctx_index >= 0

        @pl.when(valid)
        def _(chunk_ref=chunk_ref, place=place, columns=columns):
            part = pl.ds(pl.multiple_of(place * columns, 128), columns)
            hidden_ref[:, part] = residual_ref[:, part].astype(jnp.float32) + chunk_ref[
                ...
            ].astype(jnp.float32)

    hidden = hidden_ref[...]
    power = jnp.sum(hidden * hidden, axis=1, keepdims=True)
    factor = lax.rsqrt(power / width + EPSILON)
    normed_ref[...] = (hidden * factor * gain_ref[...].astype(jnp.float32)).astype(jnp.bfloat16)
    waits[-1]()
    logits = lax.dot_general(
        router_ref[...],
        normed_ref[...],
        (((1,), (1,)), ((), ())),
        preferred_element_type=jnp.float32,
    )
    gates = jax.nn.sigmoid(jnp.sum(jnp.where(chosen, logits, 0.0), axis=0, keepdims=True))
    slot_gates = jnp.sum(jnp.where(table, gates, 0.0), axis=1, keepdims=True)
    slots = jnp.dot(
        table.astype(jnp.bfloat16), normed_ref[...], preferred_element_type=jnp.float32
    )
    result_ref[...] = (slots * slot_gates).astype(jnp.bfloat16)
    source = lax.rem(exp_index - back + exp_count, exp_count)
    copy = pltpu.make_async_copy(result_ref, out_ref.at[source], out_sem)
    copy.start()
    copy.wait()


def on_device(
    queries,
    key_states,
    values,
    doc_ids,
    residual,
    out_proj,
    norm_gain,
    router,
    expert_ids,
    keep_counts,
):
    _, tokens, heads, head_size = queries.shape
    groups = key_states.shape[2]
    ctx_count = lax.axis_size("ctx")
    pair = lax.axis_size("tp")
    exp_count = lax.axis_size("exp")
    part_rows = tokens // pair
    width = residual.shape[2]
    columns = out_proj.shape[1]
    experts_here = router.shape[1]
    ctx_index = lax.axis_index("ctx")
    core = lax.axis_index("tp")
    exp_index = lax.axis_index("exp")
    reach = -(-(ctx_count * tokens // 2 - 1) // tokens)
    vmem = pl.BlockSpec(memory_space=pltpu.VMEM)
    smem = pl.BlockSpec(memory_space=pltpu.SMEM)
    anywhere = pl.BlockSpec(memory_space=pl.ANY)
    params = pltpu.CompilerParams(vmem_limit_bytes=VMEM_LIMIT)
    bf16, f32 = jnp.bfloat16, jnp.float32

    def over(array, axis, step):
        count = lax.axis_size(axis)
        if step % count == 0:
            return array
        return lax.ppermute(array, axis, [(i, (i + step) % count) for i in range(count)])

    def along(array, moves):
        return lax.ppermute(array, "ctx", moves)

    pack = pl.pallas_call(
        functools.partial(pack_kernel, groups),
        out_shape=jax.ShapeDtypeStruct((2 * groups * tokens + DOC_ROWS, head_size), bf16),
        in_specs=[anywhere] * 3,
        out_specs=vmem,
        scratch_shapes=[pltpu.VMEM((groups * tokens, head_size), bf16)] * 2
        + [pltpu.VMEM(doc_ids.shape, doc_ids.dtype), pltpu.SemaphoreType.DMA((3,))],
        compiler_params=params,
    )(
        key_states.reshape(groups * tokens, head_size),
        values.reshape(groups * tokens, head_size),
        doc_ids,
    )
    packs = [over(pack, "ctx", step) for step in range(ctx_count)]
    rising = falling = queries[0].transpose(1, 0, 2)
    place = jnp.stack([ctx_index, core])

    def project(blocks, shifts, outputs, coming=None):
        operands = [*blocks, *packs, out_proj]
        same, cross = pl.pallas_call(
            functools.partial(
                block_kernel, heads // groups, groups, pair, reach, ctx_count, shifts
            ),
            out_shape=[
                jax.ShapeDtypeStruct((outputs, part_rows, columns), f32),
                jax.ShapeDtypeStruct((pair - 1, outputs, part_rows, columns), bf16),
            ],
            in_specs=[smem] + [anywhere] * len(operands),
            out_specs=[vmem] * 2,
            scratch_shapes=[pltpu.VMEM((outputs, tokens, heads * head_size), bf16)]
            + [pltpu.VMEM(array.shape, array.dtype) for array in operands]
            + [pltpu.SemaphoreType.DMA((len(operands),))],
            compiler_params=params,
            cost_estimate=pl.CostEstimate(
                flops=outputs
                * (4 * blocks[0].size * (reach + 1) * tokens + 2 * tokens * out_proj.size),
                bytes_accessed=2 * (out_proj.size + len(blocks) * blocks[0].size),
                transcendentals=outputs * heads * tokens * (reach + 1) * tokens,
            ),
        )(place, *operands)
        if coming is not None:
            coming, cross = lax.optimization_barrier((coming, cross))
        crossed = [over(cross[turn - 1], "tp", turn) for turn in range(1, pair)]
        return [
            sum((other[number].astype(f32) for other in crossed), same[number]).astype(bf16)
            for number in range(outputs)
        ], coming

    aligned = columns % 128 == 0

    def forward(chunk):
        return [over(chunk, "exp", back) for back in range(1, exp_count if aligned else 1)]

    ids = expert_ids[:, :, 0]
    all_ids, all_residual = [ids], [residual[0]]
    kinds, chunks, sent = [], [], []
    for distance in range(1, ctx_count + 1):
        last = distance == ctx_count
        if not last:
            coming = (
                along(rising, [(i, i + 1) for i in range(distance - 1, ctx_count - 1)]),
                along(falling, [(i, i - 1) for i in range(1, ctx_count - distance + 1)]),
            )
        held = distance - 1
        blocks = (rising, falling)
        if held >= 2:
            blocks, sent[held - 2], all_ids, all_residual = lax.optimization_barrier(
                (blocks, sent[held - 2], all_ids, all_residual)
            )
        if last:
            coming = None
        if held == 0:
            totals, coming = project((rising,), (0,), 1, coming)
        else:
            both = 1 if 2 * held >= ctx_count else 2
            totals, coming = project(blocks, (held, ctx_count - held), both, coming)
        if not last:
            rising, falling = coming
        to_lower = [(i, i - held) for i in range(held, ctx_count)]
        to_upper = [(i, i + held) for i in range(ctx_count - held)]
        if held == 0:
            arrived = [("own", totals[0])]
            early_ids, early_residual, _ = lax.optimization_barrier((ids, residual[0], packs))
            all_ids += [over(early_ids, "exp", back) for back in range(1, exp_count)]
            all_residual += [over(early_residual, "exp", back) for back in range(1, exp_count)]
        elif 2 * held >= ctx_count:
            arrived = [("either", along(totals[0], to_lower + to_upper))]
        else:
            arrived = [
                ("above", along(totals[0], to_lower)),
                ("below", along(totals[1], to_upper)),
            ]
        kinds.append([(kind, held) for kind, _ in arrived])
        chunks.append([chunk for _, chunk in arrived])
        sent.append([forward(chunk) for _, chunk in arrived])
    groups_of = [
        [[chunk] + others for chunk, others in zip(group, others_of)]
        for group, others_of in zip(chunks, sent)
    ]
    if aligned:
        kinds = [kind for group in kinds for kind in group]
        flat = [arrays for group in groups_of for arrays in group]
    else:
        whole = jnp.zeros((ctx_count, part_rows, columns), bf16)
        for group, arrays in zip(kinds, chunks):
            for (kind, distance), chunk in zip(group, arrays):
                spot, valid = column_of(kind, distance, ctx_index, ctx_count)
                whole = whole.at[spot].add(jnp.where(valid, chunk, 0))
        whole = whole.transpose(1, 0, 2).reshape(part_rows, width)
        kinds = [("own", 0)]
        flat = [[over(whole, "exp", back) for back in range(exp_count)]]
    out = None
    for back in range(exp_count):
        fetched = [all_residual[back]] + [arrays[back] for arrays in flat] + [router.T]
        others = [all_ids[back], keep_counts.reshape(1, -1), norm_gain.reshape(1, -1)]
        kept = [] if out is None else [out]
        out = pl.pallas_call(
            functools.partial(finish_kernel, kinds, back, ctx_count, exp_count),
            out_shape=jax.ShapeDtypeStruct((exp_count, experts_here * CAP, width), bf16),
            in_specs=[smem]
            + [anywhere] * len(fetched)
            + [vmem] * len(others)
            + [anywhere] * len(kept),
            out_specs=anywhere,
            scratch_shapes=[
                pltpu.VMEM((part_rows, width), f32),
                pltpu.VMEM((part_rows, width), bf16),
                pltpu.VMEM((experts_here * CAP, width), bf16),
                pltpu.SemaphoreType.DMA,
            ]
            + [pltpu.VMEM(array.shape, array.dtype) for array in fetched]
            + [pltpu.SemaphoreType.DMA((len(fetched),))],
            input_output_aliases={1 + len(fetched) + len(others): 0} if kept else {},
            compiler_params=params,
        )(jnp.stack([ctx_index, exp_index]), *fetched, *others, *kept)
    return out.reshape(exp_count, experts_here, CAP, width)


def solution(mesh):
    placed = (
        P(("groups", "exp"), "ctx", "tp", None),
        P(("groups", "exp"), "ctx", "tp", None),
        P(("groups", "exp"), "ctx", "tp", None),
        P(("groups", "exp"), "ctx"),
        P(("groups", "exp"), ("ctx", "tp"), None),
        P("tp", "ctx"),
        P(),
        P(None, "exp"),
        P(("groups", "exp"), ("ctx", "tp"), None),
        P("groups"),
    )
    return jax.shard_map(
        on_device,
        mesh=mesh,
        in_specs=placed,
        out_specs=P(("groups", "ctx", "tp"), "exp", None, None),
        check_vma=False,
    )
```

```python
import functools
import math

import jax
import jax.numpy as jnp
from jax import lax
from jax.experimental import pallas as pl
from jax.experimental.pallas import tpu as pltpu
from jax.sharding import PartitionSpec as P

CAP = 2
EPSILON = 1e-05
DOC_ROWS = 16
VMEM_LIMIT = 16 * 1024 * 1024
VMEM_MOST = 56 * 1024 * 1024


def fetch(refs, buffers, sems):
    copies = [
        pltpu.make_async_copy(ref, buffer, sems.at[number])
        for number, (ref, buffer) in enumerate(zip(refs, buffers))
    ]
    for copy in copies:
        copy.start()
    return [copy.wait for copy in copies]


def pack_kernel(groups, key_ref, value_ref, doc_ref, out_ref, *scratch):
    buffers, sems = scratch[:-1], scratch[-1]
    for wait in fetch((key_ref, value_ref, doc_ref), buffers, sems):
        wait()
    key_ref, value_ref, doc_ref = buffers
    rows, head_size = key_ref.shape
    tokens = rows // groups
    token = lax.broadcasted_iota(jnp.int32, (tokens, rows), 0)
    row = lax.broadcasted_iota(jnp.int32, (tokens, rows), 1)
    for group in range(groups):
        pick = (row == token * groups + group).astype(jnp.bfloat16)
        for place, ref in enumerate((key_ref, value_ref)):
            first = (place * groups + group) * tokens
            out_ref[first : first + tokens, :] = jnp.dot(
                pick, ref[...], preferred_element_type=jnp.float32
            ).astype(jnp.bfloat16)
    out_ref[2 * rows :, :] = jnp.broadcast_to(
        (doc_ref[...] + 1).astype(jnp.float32), (DOC_ROWS, tokens)
    ).astype(jnp.bfloat16)


def stage_kernel(in_ref, out_ref, sem):
    copy = pltpu.make_async_copy(in_ref, out_ref, sem)
    copy.start()
    copy.wait()


def attention_kernel(ratio, groups, pair, place_ref, query_ref, *refs):
    pack_refs, out_refs = refs[:-pair], refs[-pair:]
    heads, tokens, head_size = query_ref.shape
    scale = 1.0 / math.sqrt(head_size)
    core = place_ref[0]
    part_rows = tokens // pair
    held_rows = groups * tokens
    rows = lax.broadcasted_iota(jnp.int32, (tokens, tokens), 0)
    columns = lax.broadcasted_iota(jnp.int32, (tokens, tokens), 1)
    docs = [ref[2 * held_rows : 2 * held_rows + 1, :].astype(jnp.float32) for ref in pack_refs]
    own_doc = jnp.sum(jnp.where(rows == columns, docs[0], 0.0), axis=1, keepdims=True)
    allowed = [(own_doc == docs[0]) & (columns <= rows)] + [own_doc == doc for doc in docs[1:]]
    allowed = jnp.concatenate(allowed, axis=1)
    for group in range(groups):
        first = group * tokens
        keys = jnp.concatenate([ref[first : first + tokens, :] for ref in pack_refs], axis=0)
        first = held_rows + group * tokens
        held = jnp.concatenate([ref[first : first + tokens, :] for ref in pack_refs], axis=0)
        for head in range(group * ratio, (group + 1) * ratio):
            scores = lax.dot_general(
                query_ref[head], keys, (((1,), (1,)), ((), ())), preferred_element_type=jnp.float32
            )
            scores = jnp.where(allowed, scores * scale, -1e30)
            weights = jnp.exp(scores - jnp.max(scores, axis=1, keepdims=True))
            totals = jnp.sum(weights, axis=1, keepdims=True)
            mixed = jnp.dot(
                weights.astype(jnp.bfloat16), held, preferred_element_type=jnp.float32
            )
            mixed = (mixed / totals).astype(jnp.bfloat16)
            parts = [mixed[i * part_rows : (i + 1) * part_rows] for i in range(pair)]
            for turn in range(pair):
                piece = parts[turn]
                for own in range(1, pair):
                    piece = jnp.where(core == own, parts[(own + turn) % pair], piece)
                out_refs[turn][:, head * head_size : (head + 1) * head_size] = piece


def project_kernel(pair, block_ref, *refs):
    weight_refs, out_ref = refs[:pair], refs[pair]
    depth = weight_refs[0].shape[0]
    total = jnp.zeros(out_ref.shape, jnp.float32)
    for turn in range(pair):
        total = total + jnp.dot(
            block_ref[:, turn * depth : (turn + 1) * depth],
            weight_refs[turn][...],
            preferred_element_type=jnp.float32,
        )
    out_ref[...] = total.astype(out_ref.dtype)


def add_chunks(out_ref, base, chunk_refs, steps, spots, ctx_index):
    for step, chunk_ref in zip(steps, chunk_refs):
        columns = chunk_ref.shape[1]
        first = 0 if spots == 1 else lax.rem(ctx_index + step, spots) * columns
        part = pl.ds(pl.multiple_of(first, 128), columns)
        out_ref[:, part] = base[:, part].astype(jnp.float32) + chunk_ref[...].astype(jnp.float32)


def collect_kernel(steps, spots, exp_count, place_ref, *refs):
    count = len(steps)
    residual_refs, chunk_refs = refs[:exp_count], refs[exp_count:-exp_count]
    for back, out_ref in enumerate(refs[-exp_count:]):
        out_ref[...] = residual_refs[back][...].astype(jnp.float32)
        add_chunks(
            out_ref,
            residual_refs[back],
            chunk_refs[back * count : (back + 1) * count],
            steps,
            spots,
            place_ref[0],
        )


def finish_kernel(steps, spots, back, exp_count, place_ref, *refs):
    chunk_refs = refs[: len(steps)]
    hidden_ref, id_ref, keep_ref, gain_ref, router_ref = refs[len(steps) :][:5]
    kept_refs = refs[len(steps) + 5 : -3]
    out_ref, total_ref, normed_ref = refs[-3:]
    rows, width = hidden_ref.shape
    experts = keep_ref.shape[1]
    here = router_ref.shape[0]
    ctx_index, exp_index = place_ref[0], place_ref[1]
    keep = keep_ref[...].astype(jnp.float32)
    upper = (
        lax.broadcasted_iota(jnp.int32, (rows, rows), 0)
        < lax.broadcasted_iota(jnp.int32, (rows, rows), 1)
    ).astype(jnp.bfloat16)
    total_ref[...] = hidden_ref[...]
    add_chunks(total_ref, hidden_ref, chunk_refs, steps, spots, ctx_index)
    hidden = total_ref[...]
    power = jnp.sum(hidden * hidden, axis=1, keepdims=True)
    factor = lax.rsqrt(power / width + EPSILON)
    normed_ref[...] = (hidden * factor * gain_ref[...].astype(jnp.float32)).astype(jnp.bfloat16)
    ids = id_ref[...]
    onehot = (ids == lax.broadcasted_iota(jnp.int32, (experts, rows), 0)).astype(jnp.float32)
    earlier = jnp.dot(onehot.astype(jnp.bfloat16), upper, preferred_element_type=jnp.float32)
    ranking = jnp.sum(onehot * earlier, axis=0, keepdims=True)
    limits = jnp.dot(
        keep.astype(jnp.bfloat16),
        onehot.astype(jnp.bfloat16),
        preferred_element_type=jnp.float32,
    )
    local = ids - exp_index * here
    logits = lax.dot_general(
        router_ref[...],
        normed_ref[...],
        (((1,), (1,)), ((), ())),
        preferred_element_type=jnp.float32,
    )
    chosen = local == lax.broadcasted_iota(jnp.int32, (here, rows), 0)
    gates = jax.nn.sigmoid(jnp.sum(jnp.where(chosen, logits, 0.0), axis=0, keepdims=True))
    target = local * CAP + ranking.astype(jnp.int32)
    target = jnp.where((ranking < limits) & (local >= 0) & (local < here), target, -1)
    table = lax.broadcasted_iota(jnp.int32, (here * CAP, rows), 0) == target
    slot_gates = jnp.sum(jnp.where(table, gates, 0.0), axis=1, keepdims=True)
    slots = jnp.dot(
        table.astype(jnp.bfloat16), normed_ref[...], preferred_element_type=jnp.float32
    )
    result = (slots * slot_gates).astype(jnp.bfloat16)
    if back < exp_count - 1:
        out_ref[...] = result
        return
    for number, ref in enumerate(kept_refs):
        out_ref[lax.rem(exp_index - number + exp_count, exp_count)] = ref[...]
    out_ref[lax.rem(exp_index - back + exp_count, exp_count)] = result


def on_device(
    queries,
    key_states,
    values,
    doc_ids,
    residual,
    out_proj,
    norm_gain,
    router,
    expert_ids,
    keep_counts,
):
    _, tokens, heads, head_size = queries.shape
    groups = key_states.shape[2]
    ctx_count = lax.axis_size("ctx")
    pair = lax.axis_size("tp")
    exp_count = lax.axis_size("exp")
    part_rows = tokens // pair
    width = residual.shape[2]
    columns = out_proj.shape[1]
    experts_here = router.shape[1]
    ctx_index = lax.axis_index("ctx")
    core = lax.axis_index("tp")
    exp_index = lax.axis_index("exp")
    reach = -(-(ctx_count * tokens // 2 - 1) // tokens)
    vmem = pl.BlockSpec(memory_space=pltpu.VMEM)
    smem = pl.BlockSpec(memory_space=pltpu.SMEM)
    anywhere = pl.BlockSpec(memory_space=pl.ANY)
    params = pltpu.CompilerParams(vmem_limit_bytes=VMEM_LIMIT)
    bf16, f32 = jnp.bfloat16, jnp.float32

    def over(array, axis, step):
        count = lax.axis_size(axis)
        if step % count == 0:
            return array
        return lax.ppermute(array, axis, [(i, (i + step) % count) for i in range(count)])

    def along(array, moves):
        return lax.ppermute(array, "ctx", moves)

    pack = pl.pallas_call(
        functools.partial(pack_kernel, groups),
        out_shape=jax.ShapeDtypeStruct((2 * groups * tokens + DOC_ROWS, head_size), bf16),
        in_specs=[anywhere] * 3,
        out_specs=vmem,
        scratch_shapes=[pltpu.VMEM((groups * tokens, head_size), bf16)] * 2
        + [pltpu.VMEM(doc_ids.shape, doc_ids.dtype), pltpu.SemaphoreType.DMA((3,))],
        compiler_params=pltpu.CompilerParams(vmem_limit_bytes=VMEM_MOST),
    )(
        key_states.reshape(groups * tokens, head_size),
        values.reshape(groups * tokens, head_size),
        doc_ids,
    )
    packs = [pack] + [
        lax.ppermute(pack, "ctx", [(i, i + step) for i in range(ctx_count - step)])
        for step in range(1, reach + 1)
    ]
    own_weights, own_queries, pack = lax.optimization_barrier(
        (out_proj, queries[0].transpose(1, 0, 2), pack)
    )
    packs[0] = pack
    weights = [out_proj] + [over(own_weights, "tp", turn) for turn in range(1, pair)]
    staged = pl.pallas_call(
        stage_kernel,
        out_shape=jax.ShapeDtypeStruct(own_queries.shape, bf16),
        in_specs=[anywhere],
        out_specs=vmem,
        scratch_shapes=[pltpu.SemaphoreType.DMA],
        compiler_params=params,
    )(own_queries)
    pieces = pl.pallas_call(
        functools.partial(attention_kernel, heads // groups, groups, pair),
        out_shape=[jax.ShapeDtypeStruct((part_rows, heads * head_size), bf16)] * pair,
        in_specs=[smem] + [vmem] * (1 + len(packs)),
        out_specs=[vmem] * pair,
        compiler_params=params,
    )(core.reshape(1), staged, *packs)

    project = pl.pallas_call(
        functools.partial(project_kernel, pair),
        out_shape=jax.ShapeDtypeStruct((part_rows, columns), bf16),
        in_specs=[vmem] * (1 + pair),
        out_specs=vmem,
        compiler_params=params,
        cost_estimate=pl.CostEstimate(
            flops=2 * pair * part_rows * out_proj.size,
            bytes_accessed=2 * pair * out_proj.size,
            transcendentals=0,
        ),
    )
    block = jnp.concatenate([over(pieces[turn], "tp", turn) for turn in range(pair)], axis=1)
    ids, own_residual = expert_ids[:, :, 0], residual[0]
    block, early_ids, early_residual = lax.optimization_barrier((block, ids, own_residual))
    all_ids = [ids] + [over(early_ids, "exp", back) for back in range(1, exp_count)]
    all_residual = [own_residual] + [
        over(early_residual, "exp", back) for back in range(1, exp_count)
    ]

    aligned = columns % 128 == 0
    hidden = None

    def forward(chunk):
        return [over(chunk, "exp", back) for back in range(1, exp_count if aligned else 1)]

    def collect(arrays, steps, spots):
        return pl.pallas_call(
            functools.partial(collect_kernel, steps, spots, exp_count),
            out_shape=[jax.ShapeDtypeStruct((part_rows, width), f32)] * exp_count,
            in_specs=[smem] + [vmem] * (exp_count + len(arrays)),
            out_specs=[vmem] * exp_count,
            compiler_params=params,
        )(ctx_index.reshape(1), *all_residual, *arrays)

    flat = []
    for step in range(ctx_count):
        last = step == ctx_count - 1
        following = None if last else over(block, "ctx", 1)
        if step >= 2 and aligned:
            block, flat[step - 2] = lax.optimization_barrier((block, flat[step - 2]))
        if step == 2:
            block, flat[1][0] = lax.optimization_barrier((block, flat[1][0]))
        total = project(block, *weights)
        chunk = over(total, "ctx", ctx_count - step)
        if not last:
            block, _ = lax.optimization_barrier((following, total))
        if last and aligned:
            steps = list(range(step))
            hidden = collect(
                [flat[number][back] for back in range(exp_count) for number in steps],
                steps,
                ctx_count,
            )
            chunk, hidden, all_ids = lax.optimization_barrier((chunk, hidden, all_ids))
        flat.append([chunk] + forward(chunk))
    if aligned:
        late_steps, late, spots = [ctx_count - 1], [flat[-1]], ctx_count
    else:
        whole = jnp.roll(jnp.stack([arrays[0] for arrays in flat]), ctx_index, axis=0)
        whole = whole.transpose(1, 0, 2).reshape(part_rows, width)
        hidden = collect([over(whole, "exp", back) for back in range(exp_count)], [0], 1)
        late_steps, late, spots = [], [], 1
    places = jnp.stack([ctx_index, exp_index])
    results = []
    for back in range(exp_count):
        operands = (
            [places]
            + [arrays[back] for arrays in late]
            + [hidden[back], all_ids[back], keep_counts.reshape(1, -1)]
            + [norm_gain.reshape(1, -1), router.T]
        )
        shape = (experts_here * CAP, width)
        if back == exp_count - 1:
            operands += results
            shape = (exp_count,) + shape
        out = pl.pallas_call(
            functools.partial(finish_kernel, late_steps, spots, back, exp_count),
            out_shape=jax.ShapeDtypeStruct(shape, bf16),
            in_specs=[smem] + [vmem] * (len(operands) - 1),
            out_specs=vmem,
            scratch_shapes=[
                pltpu.VMEM((part_rows, width), f32),
                pltpu.VMEM((part_rows, width), bf16),
            ],
            compiler_params=params,
        )(*operands)
        results.append(out)
    return out.reshape(exp_count, experts_here, CAP, width)


def solution(mesh):
    placed = (
        P(("groups", "exp"), "ctx", "tp", None),
        P(("groups", "exp"), "ctx", "tp", None),
        P(("groups", "exp"), "ctx", "tp", None),
        P(("groups", "exp"), "ctx"),
        P(("groups", "exp"), ("ctx", "tp"), None),
        P("tp", "ctx"),
        P(),
        P(None, "exp"),
        P(("groups", "exp"), ("ctx", "tp"), None),
        P("groups"),
    )
    return jax.shard_map(
        on_device,
        mesh=mesh,
        in_specs=placed,
        out_specs=P(("groups", "ctx", "tp"), "exp", None, None),
        check_vma=False,
    )
```

```python
import functools
import math

import jax
import jax.numpy as jnp
from jax import lax
from jax.experimental import pallas as pl
from jax.experimental.pallas import tpu as pltpu
from jax.sharding import PartitionSpec as P

CAP = 2
EPSILON = 1e-05
DOC_ROWS = 16
VMEM_LIMIT = 16 * 1024 * 1024
VMEM_MOST = 56 * 1024 * 1024


def fetch(refs, buffers, sems):
    copies = [
        pltpu.make_async_copy(ref, buffer, sems.at[number])
        for number, (ref, buffer) in enumerate(zip(refs, buffers))
    ]
    for copy in copies:
        copy.start()
    return [copy.wait for copy in copies]


def pack_kernel(groups, key_ref, value_ref, doc_ref, out_ref, *scratch):
    buffers, sems = scratch[:-1], scratch[-1]
    for wait in fetch((key_ref, value_ref, doc_ref), buffers, sems):
        wait()
    key_ref, value_ref, doc_ref = buffers
    rows, head_size = key_ref.shape
    tokens = rows // groups
    token = lax.broadcasted_iota(jnp.int32, (tokens, rows), 0)
    row = lax.broadcasted_iota(jnp.int32, (tokens, rows), 1)
    for group in range(groups):
        pick = (row == token * groups + group).astype(jnp.bfloat16)
        for place, ref in enumerate((key_ref, value_ref)):
            first = (place * groups + group) * tokens
            out_ref[first : first + tokens, :] = jnp.dot(
                pick, ref[...], preferred_element_type=jnp.float32
            ).astype(jnp.bfloat16)
    out_ref[2 * rows :, :] = jnp.broadcast_to(
        (doc_ref[...] + 1).astype(jnp.float32), (DOC_ROWS, tokens)
    ).astype(jnp.bfloat16)


def stage_kernel(count, *refs):
    for wait in fetch(refs[:count], refs[count:-1], refs[-1]):
        wait()


def attention_kernel(ratio, groups, pair, place_ref, query_ref, *refs):
    pack_refs, out_refs = refs[:-pair], refs[-pair:]
    heads, tokens, head_size = query_ref.shape
    scale = 1.0 / math.sqrt(head_size)
    core = place_ref[0]
    part_rows = tokens // pair
    held_rows = groups * tokens
    rows = lax.broadcasted_iota(jnp.int32, (tokens, tokens), 0)
    columns = lax.broadcasted_iota(jnp.int32, (tokens, tokens), 1)
    docs = [ref[2 * held_rows : 2 * held_rows + 1, :].astype(jnp.float32) for ref in pack_refs]
    own_doc = jnp.sum(jnp.where(rows == columns, docs[0], 0.0), axis=1, keepdims=True)
    allowed = [(own_doc == docs[0]) & (columns <= rows)] + [own_doc == doc for doc in docs[1:]]
    allowed = jnp.concatenate(allowed, axis=1)
    for group in range(groups):
        first = group * tokens
        keys = jnp.concatenate([ref[first : first + tokens, :] for ref in pack_refs], axis=0)
        first = held_rows + group * tokens
        held = jnp.concatenate([ref[first : first + tokens, :] for ref in pack_refs], axis=0)
        for head in range(group * ratio, (group + 1) * ratio):
            scores = lax.dot_general(
                query_ref[head], keys, (((1,), (1,)), ((), ())), preferred_element_type=jnp.float32
            )
            scores = jnp.where(allowed, scores * scale, -1e30)
            weights = jnp.exp(scores - jnp.max(scores, axis=1, keepdims=True))
            totals = jnp.sum(weights, axis=1, keepdims=True)
            mixed = jnp.dot(
                weights.astype(jnp.bfloat16), held, preferred_element_type=jnp.float32
            )
            mixed = (mixed / totals).astype(jnp.bfloat16)
            parts = [mixed[i * part_rows : (i + 1) * part_rows] for i in range(pair)]
            for turn in range(pair):
                piece = parts[turn]
                for own in range(1, pair):
                    piece = jnp.where(core == own, parts[(own + turn) % pair], piece)
                out_refs[turn][:, head * head_size : (head + 1) * head_size] = piece


def project_kernel(pair, *refs):
    block_refs, weight_refs, out_ref = refs[:pair], refs[pair : 2 * pair], refs[2 * pair]
    total = jnp.zeros(out_ref.shape, jnp.float32)
    for block_ref, weight_ref in zip(block_refs, weight_refs):
        total = total + jnp.dot(
            block_ref[...], weight_ref[...], preferred_element_type=jnp.float32
        )
    out_ref[...] = total.astype(out_ref.dtype)


def columns_of(chunk_ref, step, spots, ctx_index):
    columns = chunk_ref.shape[1]
    first = 0 if spots == 1 else lax.rem(ctx_index + step, spots) * columns
    return pl.ds(pl.multiple_of(first, 128), columns)


def hidden_kernel(step, spots, place_ref, residual_ref, chunk_ref, out_ref):
    part = columns_of(chunk_ref, step, spots, place_ref[0])
    out_ref[...] = (
        residual_ref[:, part].astype(jnp.float32) + chunk_ref[...].astype(jnp.float32)
    ).astype(out_ref.dtype)


def collect_kernel(steps, spots, exp_count, place_ref, residual_ref, *refs):
    count = len(steps)
    chunk_refs, out_refs = refs[:-exp_count], refs[-exp_count:]
    out_refs[0][...] = residual_ref[...].astype(jnp.float32)
    for back, out_ref in enumerate(out_refs):
        for step, chunk_ref in zip(steps, chunk_refs[back * count : (back + 1) * count]):
            part = columns_of(chunk_ref, step, spots, place_ref[0])
            hidden = chunk_ref[...].astype(jnp.float32)
            if back == 0:
                hidden = hidden + residual_ref[:, part].astype(jnp.float32)
            out_ref[:, part] = hidden


def finish_kernel(steps, spots, back, exp_count, place_ref, *refs):
    chunk_refs = refs[: len(steps)]
    hidden_ref, id_ref, keep_ref, gain_ref, router_ref = refs[len(steps) :][:5]
    kept_refs = refs[len(steps) + 5 : -3]
    out_ref, total_ref, normed_ref = refs[-3:]
    rows, width = hidden_ref.shape
    experts = keep_ref.shape[1]
    here = router_ref.shape[0]
    ctx_index, exp_index = place_ref[0], place_ref[1]
    keep = keep_ref[...].astype(jnp.float32)
    upper = (
        lax.broadcasted_iota(jnp.int32, (rows, rows), 0)
        < lax.broadcasted_iota(jnp.int32, (rows, rows), 1)
    ).astype(jnp.bfloat16)
    total_ref[...] = hidden_ref[...]
    for step, chunk_ref in zip(steps, chunk_refs):
        part = columns_of(chunk_ref, step, spots, ctx_index)
        late = chunk_ref[...].astype(jnp.float32)
        if back == 0:
            late = late + hidden_ref[:, part]
        total_ref[:, part] = late
    hidden = total_ref[...]
    power = jnp.sum(hidden * hidden, axis=1, keepdims=True)
    factor = lax.rsqrt(power / width + EPSILON)
    normed_ref[...] = (hidden * factor * gain_ref[...].astype(jnp.float32)).astype(jnp.bfloat16)
    ids = id_ref[...]
    onehot = (ids == lax.broadcasted_iota(jnp.int32, (experts, rows), 0)).astype(jnp.float32)
    earlier = jnp.dot(onehot.astype(jnp.bfloat16), upper, preferred_element_type=jnp.float32)
    ranking = jnp.sum(onehot * earlier, axis=0, keepdims=True)
    limits = jnp.dot(
        keep.astype(jnp.bfloat16),
        onehot.astype(jnp.bfloat16),
        preferred_element_type=jnp.float32,
    )
    local = ids - exp_index * here
    logits = lax.dot_general(
        router_ref[...],
        normed_ref[...],
        (((1,), (1,)), ((), ())),
        preferred_element_type=jnp.float32,
    )
    chosen = local == lax.broadcasted_iota(jnp.int32, (here, rows), 0)
    gates = jax.nn.sigmoid(jnp.sum(jnp.where(chosen, logits, 0.0), axis=0, keepdims=True))
    target = local * CAP + ranking.astype(jnp.int32)
    target = jnp.where((ranking < limits) & (local >= 0) & (local < here), target, -1)
    table = lax.broadcasted_iota(jnp.int32, (here * CAP, rows), 0) == target
    slot_gates = jnp.sum(jnp.where(table, gates, 0.0), axis=1, keepdims=True)
    slots = jnp.dot(
        table.astype(jnp.bfloat16), normed_ref[...], preferred_element_type=jnp.float32
    )
    result = (slots * slot_gates).astype(jnp.bfloat16)
    if back < exp_count - 1:
        out_ref[...] = result
        return
    for number, ref in enumerate(kept_refs):
        out_ref[lax.rem(exp_index - number + exp_count, exp_count)] = ref[...]
    out_ref[lax.rem(exp_index - back + exp_count, exp_count)] = result


def on_device(
    queries,
    key_states,
    values,
    doc_ids,
    residual,
    out_proj,
    norm_gain,
    router,
    expert_ids,
    keep_counts,
):
    _, tokens, heads, head_size = queries.shape
    groups = key_states.shape[2]
    ctx_count = lax.axis_size("ctx")
    pair = lax.axis_size("tp")
    exp_count = lax.axis_size("exp")
    part_rows = tokens // pair
    width = residual.shape[2]
    columns = out_proj.shape[1]
    experts_here = router.shape[1]
    ctx_index = lax.axis_index("ctx")
    core = lax.axis_index("tp")
    exp_index = lax.axis_index("exp")
    reach = -(-(ctx_count * tokens // 2 - 1) // tokens)
    vmem = pl.BlockSpec(memory_space=pltpu.VMEM)
    smem = pl.BlockSpec(memory_space=pltpu.SMEM)
    anywhere = pl.BlockSpec(memory_space=pl.ANY)
    params = pltpu.CompilerParams(vmem_limit_bytes=VMEM_LIMIT)
    bf16, f32 = jnp.bfloat16, jnp.float32

    def over(array, axis, step):
        count = lax.axis_size(axis)
        if step % count == 0:
            return array
        return lax.ppermute(array, axis, [(i, (i + step) % count) for i in range(count)])

    def along(array, moves):
        return lax.ppermute(array, "ctx", moves)

    pack = pl.pallas_call(
        functools.partial(pack_kernel, groups),
        out_shape=jax.ShapeDtypeStruct((2 * groups * tokens + DOC_ROWS, head_size), bf16),
        in_specs=[anywhere] * 3,
        out_specs=vmem,
        scratch_shapes=[pltpu.VMEM((groups * tokens, head_size), bf16)] * 2
        + [pltpu.VMEM(doc_ids.shape, doc_ids.dtype), pltpu.SemaphoreType.DMA((3,))],
        compiler_params=pltpu.CompilerParams(vmem_limit_bytes=VMEM_MOST),
    )(
        key_states.reshape(groups * tokens, head_size),
        values.reshape(groups * tokens, head_size),
        doc_ids,
    )
    packs = [pack] + [
        lax.ppermute(pack, "ctx", [(i, i + step) for i in range(ctx_count - step)])
        for step in range(1, reach + 1)
    ]
    ids, own_residual = expert_ids[:, :, 0], residual[0]
    pack, own_queries, early_weights = lax.optimization_barrier(
        (pack, queries[0].transpose(1, 0, 2), out_proj)
    )
    weights = [out_proj] + [over(early_weights, "tp", turn) for turn in range(1, pair)]
    staged_queries, packs[0] = pl.pallas_call(
        functools.partial(stage_kernel, 2),
        out_shape=[
            jax.ShapeDtypeStruct(own_queries.shape, bf16),
            jax.ShapeDtypeStruct(pack.shape, bf16),
        ],
        in_specs=[anywhere] * 2,
        out_specs=[vmem] * 2,
        scratch_shapes=[pltpu.SemaphoreType.DMA((2,))],
        compiler_params=params,
    )(own_queries, pack)
    all_ids = [ids] + [over(ids, "exp", back) for back in range(1, exp_count)]
    pieces = pl.pallas_call(
        functools.partial(attention_kernel, heads // groups, groups, pair),
        out_shape=[jax.ShapeDtypeStruct((part_rows, heads * head_size), bf16)] * pair,
        in_specs=[smem] + [vmem] * (1 + len(packs)),
        out_specs=[vmem] * pair,
        compiler_params=params,
    )(core.reshape(1), staged_queries, *packs)

    project = pl.pallas_call(
        functools.partial(project_kernel, pair),
        out_shape=jax.ShapeDtypeStruct((part_rows, columns), bf16),
        in_specs=[vmem] * (2 * pair),
        out_specs=vmem,
        compiler_params=params,
        cost_estimate=pl.CostEstimate(
            flops=2 * pair * part_rows * out_proj.size,
            bytes_accessed=2 * pair * out_proj.size,
            transcendentals=0,
        ),
    )
    block = [over(pieces[turn], "tp", turn) for turn in range(pair)]

    aligned = columns % 128 == 0
    hidden = None

    def forward(chunk, step, spots):
        if exp_count == 1:
            return []
        hidden = pl.pallas_call(
            functools.partial(hidden_kernel, step, spots),
            out_shape=jax.ShapeDtypeStruct(chunk.shape, bf16),
            in_specs=[smem] + [vmem] * 2,
            out_specs=vmem,
            compiler_params=params,
        )(ctx_index.reshape(1), own_residual, chunk)
        return [over(hidden, "exp", back) for back in range(1, exp_count)]

    def collect(arrays, steps, spots):
        return pl.pallas_call(
            functools.partial(collect_kernel, steps, spots, exp_count),
            out_shape=[jax.ShapeDtypeStruct((part_rows, width), f32)] * exp_count,
            in_specs=[smem] + [vmem] * (1 + len(arrays)),
            out_specs=[vmem] * exp_count,
            compiler_params=params,
        )(ctx_index.reshape(1), own_residual, *arrays)

    flat = []
    for step in range(ctx_count):
        last = step == ctx_count - 1
        following = None if last else [over(array, "ctx", 1) for array in block]
        if step == 1:
            block, all_ids = lax.optimization_barrier((block, all_ids))
        if step == 2:
            block, flat[1][0] = lax.optimization_barrier((block, flat[1][0]))
        if step >= 3 and aligned:
            block, flat[step - 3], flat[step - 2] = lax.optimization_barrier(
                (block, flat[step - 3], flat[step - 2])
            )
        total = project(*block, *weights)
        chunk = over(total, "ctx", ctx_count - step)
        if not last:
            block = [lax.optimization_barrier((array, total))[0] for array in following]
        if last and aligned:
            steps = list(range(step))
            hidden = collect(
                [flat[number][back] for back in range(exp_count) for number in steps],
                steps,
                ctx_count,
            )
        flat.append([chunk] + (forward(chunk, step, ctx_count) if aligned else []))
    if aligned:
        late_steps, late, spots = [ctx_count - 1], [flat[-1]], ctx_count
    else:
        whole = jnp.roll(jnp.stack([arrays[0] for arrays in flat]), ctx_index, axis=0)
        whole = whole.transpose(1, 0, 2).reshape(part_rows, width)
        hidden = collect([whole] + forward(whole, 0, 1), [0], 1)
        late_steps, late, spots = [], [], 1
    places = jnp.stack([ctx_index, exp_index])
    results = []
    for back in range(exp_count):
        operands = (
            [places]
            + [arrays[back] for arrays in late]
            + [hidden[back], all_ids[back], keep_counts.reshape(1, -1)]
            + [norm_gain.reshape(1, -1), router.T]
        )
        shape = (experts_here * CAP, width)
        if back == exp_count - 1:
            operands += results
            shape = (exp_count,) + shape
        out = pl.pallas_call(
            functools.partial(finish_kernel, late_steps, spots, back, exp_count),
            out_shape=jax.ShapeDtypeStruct(shape, bf16),
            in_specs=[smem] + [vmem] * (len(operands) - 1),
            out_specs=vmem,
            scratch_shapes=[
                pltpu.VMEM((part_rows, width), f32),
                pltpu.VMEM((part_rows, width), bf16),
            ],
            compiler_params=params,
        )(*operands)
        results.append(out)
    return out.reshape(exp_count, experts_here, CAP, width)


def solution(mesh):
    placed = (
        P(("groups", "exp"), "ctx", "tp", None),
        P(("groups", "exp"), "ctx", "tp", None),
        P(("groups", "exp"), "ctx", "tp", None),
        P(("groups", "exp"), "ctx"),
        P(("groups", "exp"), ("ctx", "tp"), None),
        P("tp", "ctx"),
        P(),
        P(None, "exp"),
        P(("groups", "exp"), ("ctx", "tp"), None),
        P("groups"),
    )
    return jax.shard_map(
        on_device,
        mesh=mesh,
        in_specs=placed,
        out_specs=P(("groups", "ctx", "tp"), "exp", None, None),
        check_vma=False,
    )
```

```python
import functools
import math

import jax
import jax.numpy as jnp
from jax import lax
from jax.experimental import pallas as pl
from jax.experimental.pallas import tpu as pltpu
from jax.sharding import PartitionSpec as P

CAP = 2
EPSILON = 1e-05
DOC_ROWS = 16
VMEM_LIMIT = 16 * 1024 * 1024
VMEM_MOST = 61 * 1024 * 1024
VMEM_MUCH = 52 * 1024 * 1024
PIECE = 256


def fetch(refs, buffers, sems):
    copies = [
        pltpu.make_async_copy(ref, buffer, sems.at[number])
        for number, (ref, buffer) in enumerate(zip(refs, buffers))
    ]
    for copy in copies:
        copy.start()
    return [copy.wait for copy in copies]


def pack_kernel(groups, key_ref, value_ref, doc_ref, out_ref, *scratch):
    buffers, sems = scratch[:-1], scratch[-1]
    for wait in fetch((key_ref, value_ref, doc_ref), buffers, sems):
        wait()
    key_ref, value_ref, doc_ref = buffers
    rows, head_size = key_ref.shape
    tokens = rows // groups
    token = lax.broadcasted_iota(jnp.int32, (tokens, rows), 0)
    row = lax.broadcasted_iota(jnp.int32, (tokens, rows), 1)
    for group in range(groups):
        pick = (row == token * groups + group).astype(jnp.bfloat16)
        for place, ref in enumerate((key_ref, value_ref)):
            first = (place * groups + group) * tokens
            out_ref[first : first + tokens, :] = jnp.dot(
                pick, ref[...], preferred_element_type=jnp.float32
            ).astype(jnp.bfloat16)
    out_ref[2 * rows :, :] = jnp.broadcast_to(
        (doc_ref[...] + 1).astype(jnp.float32), (DOC_ROWS, tokens)
    ).astype(jnp.bfloat16)


def stage_kernel(count, *refs):
    for wait in fetch(refs[:count], refs[count:-1], refs[-1]):
        wait()


def attention_kernel(ratio, groups, pair, place_ref, query_ref, *refs):
    pack_refs, out_refs = refs[:-pair], refs[-pair:]
    heads, tokens, head_size = query_ref.shape
    scale = 1.0 / math.sqrt(head_size)
    core = place_ref[0]
    part_rows = tokens // pair
    held_rows = groups * tokens
    rows = lax.broadcasted_iota(jnp.int32, (tokens, tokens), 0)
    columns = lax.broadcasted_iota(jnp.int32, (tokens, tokens), 1)
    docs = [ref[2 * held_rows : 2 * held_rows + 1, :].astype(jnp.float32) for ref in pack_refs]
    own_doc = jnp.sum(jnp.where(rows == columns, docs[0], 0.0), axis=1, keepdims=True)
    allowed = [(own_doc == docs[0]) & (columns <= rows)] + [own_doc == doc for doc in docs[1:]]
    allowed = jnp.concatenate(allowed, axis=1)
    for group in range(groups):
        first = group * tokens
        keys = jnp.concatenate([ref[first : first + tokens, :] for ref in pack_refs], axis=0)
        first = held_rows + group * tokens
        held = jnp.concatenate([ref[first : first + tokens, :] for ref in pack_refs], axis=0)
        for head in range(group * ratio, (group + 1) * ratio):
            scores = lax.dot_general(
                query_ref[head], keys, (((1,), (1,)), ((), ())), preferred_element_type=jnp.float32
            )
            scores = jnp.where(allowed, scores * scale, -1e30)
            weights = jnp.exp(scores - jnp.max(scores, axis=1, keepdims=True))
            totals = jnp.sum(weights, axis=1, keepdims=True)
            mixed = jnp.dot(
                weights.astype(jnp.bfloat16), held, preferred_element_type=jnp.float32
            )
            mixed = (mixed / totals).astype(jnp.bfloat16)
            parts = [mixed[i * part_rows : (i + 1) * part_rows] for i in range(pair)]
            for turn in range(pair):
                piece = parts[turn]
                for own in range(1, pair):
                    piece = jnp.where(core == own, parts[(own + turn) % pair], piece)
                out_refs[turn][:, head * head_size : (head + 1) * head_size] = piece


def project_kernel(pair, *refs):
    block_refs, weight_refs, out_ref = refs[:pair], refs[pair : 2 * pair], refs[2 * pair]
    buffers, sems = refs[2 * pair + 1 : 3 * pair + 1], refs[3 * pair + 1]
    columns = out_ref.shape[1]
    piece = PIECE if columns % PIECE == 0 else columns
    parts = [pl.ds(first, piece) for first in range(0, columns, piece)]
    copies = [
        [
            pltpu.make_async_copy(
                weight_refs[turn].at[:, part], buffers[turn].at[:, part], sems.at[turn, number]
            )
            for turn in range(pair)
        ]
        for number, part in enumerate(parts)
    ]
    for group in copies:
        for copy in group:
            copy.start()
    for group, part in zip(copies, parts):
        total = None
        for turn in range(pair):
            group[turn].wait()
            product = jnp.dot(
                block_refs[turn][...],
                buffers[turn][:, part],
                preferred_element_type=jnp.float32,
            )
            total = product if total is None else total + product
        out_ref[:, part] = total.astype(out_ref.dtype)


def columns_of(chunk_ref, step, spots, ctx_index):
    columns = chunk_ref.shape[1]
    first = 0 if spots == 1 else lax.rem(ctx_index + step, spots) * columns
    return pl.ds(pl.multiple_of(first, 128), columns)


def hidden_kernel(step, spots, place_ref, residual_ref, chunk_ref, out_ref):
    part = columns_of(chunk_ref, step, spots, place_ref[0])
    out_ref[...] = (
        residual_ref[:, part].astype(jnp.float32) + chunk_ref[...].astype(jnp.float32)
    ).astype(out_ref.dtype)


def collect_kernel(steps, spots, exp_count, place_ref, *refs):
    count = len(steps)
    chunk_refs, out_refs = refs[:-exp_count], refs[-exp_count:]
    for back, out_ref in enumerate(out_refs):
        for step, chunk_ref in zip(steps, chunk_refs[back * count : (back + 1) * count]):
            out_ref[:, columns_of(chunk_ref, step, spots, place_ref[0])] = chunk_ref[...]


def finish_kernel(steps, spots, back, exp_count, place_ref, *refs):
    count = len(steps)
    chunk_refs = refs[:count]
    hidden_ref, id_ref, keep_ref, gain_ref, router_ref = refs[count : count + 5]
    out_ref, total_ref, normed_ref, result_ref, out_sem = refs[-5:]
    rows, width = hidden_ref.shape
    experts = keep_ref.shape[1]
    here = router_ref.shape[0]
    ctx_index, exp_index = place_ref[0], place_ref[1]
    keep = keep_ref[...].astype(jnp.float32)
    upper = (
        lax.broadcasted_iota(jnp.int32, (rows, rows), 0)
        < lax.broadcasted_iota(jnp.int32, (rows, rows), 1)
    ).astype(jnp.bfloat16)
    total_ref[...] = hidden_ref[...].astype(jnp.float32)
    for step, chunk_ref in zip(steps, chunk_refs):
        part = columns_of(chunk_ref, step, spots, ctx_index)
        total_ref[:, part] = chunk_ref[...].astype(jnp.float32)
    hidden = total_ref[...]
    power = jnp.sum(hidden * hidden, axis=1, keepdims=True)
    factor = lax.rsqrt(power / width + EPSILON)
    normed_ref[...] = (hidden * factor * gain_ref[...].astype(jnp.float32)).astype(jnp.bfloat16)
    ids = id_ref[...]
    onehot = (ids == lax.broadcasted_iota(jnp.int32, (experts, rows), 0)).astype(jnp.float32)
    earlier = jnp.dot(onehot.astype(jnp.bfloat16), upper, preferred_element_type=jnp.float32)
    ranking = jnp.sum(onehot * earlier, axis=0, keepdims=True)
    limits = jnp.dot(
        keep.astype(jnp.bfloat16),
        onehot.astype(jnp.bfloat16),
        preferred_element_type=jnp.float32,
    )
    local = ids - exp_index * here
    logits = lax.dot_general(
        router_ref[...],
        normed_ref[...],
        (((1,), (1,)), ((), ())),
        preferred_element_type=jnp.float32,
    )
    chosen = local == lax.broadcasted_iota(jnp.int32, (here, rows), 0)
    gates = jax.nn.sigmoid(jnp.sum(jnp.where(chosen, logits, 0.0), axis=0, keepdims=True))
    target = local * CAP + ranking.astype(jnp.int32)
    target = jnp.where((ranking < limits) & (local >= 0) & (local < here), target, -1)
    table = lax.broadcasted_iota(jnp.int32, (here * CAP, rows), 0) == target
    slot_gates = jnp.sum(jnp.where(table, gates, 0.0), axis=1, keepdims=True)
    slots = jnp.dot(
        table.astype(jnp.bfloat16), normed_ref[...], preferred_element_type=jnp.float32
    )
    result_ref[...] = (slots * slot_gates).astype(jnp.bfloat16).reshape(result_ref.shape)
    source = lax.rem(exp_index - back + exp_count, exp_count)
    copy = pltpu.make_async_copy(result_ref, out_ref.at[source], out_sem)
    copy.start()
    copy.wait()


def on_device(
    queries,
    key_states,
    values,
    doc_ids,
    residual,
    out_proj,
    norm_gain,
    router,
    expert_ids,
    keep_counts,
):
    _, tokens, heads, head_size = queries.shape
    groups = key_states.shape[2]
    ctx_count = lax.axis_size("ctx")
    pair = lax.axis_size("tp")
    exp_count = lax.axis_size("exp")
    part_rows = tokens // pair
    width = residual.shape[2]
    columns = out_proj.shape[1]
    experts_here = router.shape[1]
    ctx_index = lax.axis_index("ctx")
    core = lax.axis_index("tp")
    exp_index = lax.axis_index("exp")
    reach = -(-(ctx_count * tokens // 2 - 1) // tokens)
    vmem = pl.BlockSpec(memory_space=pltpu.VMEM)
    smem = pl.BlockSpec(memory_space=pltpu.SMEM)
    anywhere = pl.BlockSpec(memory_space=pl.ANY)
    params = pltpu.CompilerParams(vmem_limit_bytes=VMEM_LIMIT)
    most = pltpu.CompilerParams(vmem_limit_bytes=VMEM_MOST)
    much = pltpu.CompilerParams(vmem_limit_bytes=VMEM_MUCH)
    bf16, f32 = jnp.bfloat16, jnp.float32

    def over(array, axis, step):
        count = lax.axis_size(axis)
        if step % count == 0:
            return array
        return lax.ppermute(array, axis, [(i, (i + step) % count) for i in range(count)])

    def along(array, moves):
        return lax.ppermute(array, "ctx", moves)

    pack = pl.pallas_call(
        functools.partial(pack_kernel, groups),
        out_shape=jax.ShapeDtypeStruct((2 * groups * tokens + DOC_ROWS, head_size), bf16),
        in_specs=[anywhere] * 3,
        out_specs=vmem,
        scratch_shapes=[pltpu.VMEM((groups * tokens, head_size), bf16)] * 2
        + [pltpu.VMEM(doc_ids.shape, doc_ids.dtype), pltpu.SemaphoreType.DMA((3,))],
        compiler_params=most,
    )(
        key_states.reshape(groups * tokens, head_size),
        values.reshape(groups * tokens, head_size),
        doc_ids,
    )
    packs = [pack] + [
        lax.ppermute(pack, "ctx", [(i, i + step) for i in range(ctx_count - step)])
        for step in range(1, reach + 1)
    ]
    ids, own_residual = expert_ids[:, :, 0], residual[0]
    pack, own_queries, early_weights = lax.optimization_barrier(
        (pack, queries[0].transpose(1, 0, 2), out_proj)
    )
    weights = [out_proj] + [over(early_weights, "tp", turn) for turn in range(1, pair)]
    staged_queries, packs[0] = pl.pallas_call(
        functools.partial(stage_kernel, 2),
        out_shape=[
            jax.ShapeDtypeStruct(own_queries.shape, bf16),
            jax.ShapeDtypeStruct(pack.shape, bf16),
        ],
        in_specs=[anywhere] * 2,
        out_specs=[vmem] * 2,
        scratch_shapes=[pltpu.SemaphoreType.DMA((2,))],
        compiler_params=much,
    )(own_queries, pack)
    all_ids = [ids] + [over(ids, "exp", back) for back in range(1, exp_count)]
    pieces = pl.pallas_call(
        functools.partial(attention_kernel, heads // groups, groups, pair),
        out_shape=[jax.ShapeDtypeStruct((part_rows, heads * head_size), bf16)] * pair,
        in_specs=[smem] + [vmem] * (1 + len(packs)),
        out_specs=[vmem] * pair,
        compiler_params=params,
    )(core.reshape(1), staged_queries, *packs)

    project = pl.pallas_call(
        functools.partial(project_kernel, pair),
        out_shape=jax.ShapeDtypeStruct((part_rows, columns), bf16),
        in_specs=[vmem] * pair + [anywhere] * pair,
        out_specs=vmem,
        scratch_shapes=[pltpu.VMEM(out_proj.shape, bf16)] * pair
        + [pltpu.SemaphoreType.DMA((pair, max(1, columns // PIECE)))],
        compiler_params=much,
        cost_estimate=pl.CostEstimate(
            flops=2 * pair * part_rows * out_proj.size,
            bytes_accessed=2 * pair * out_proj.size,
            transcendentals=0,
        ),
    )
    block = [over(pieces[turn], "tp", turn) for turn in range(pair)]

    aligned = columns % 128 == 0
    hidden = None

    def forward(chunk, step, spots):
        hidden = pl.pallas_call(
            functools.partial(hidden_kernel, step, spots),
            out_shape=jax.ShapeDtypeStruct(chunk.shape, bf16),
            in_specs=[smem] + [vmem] * 2,
            out_specs=vmem,
            compiler_params=params,
        )(ctx_index.reshape(1), own_residual, chunk)
        return [over(hidden, "exp", back) for back in range(exp_count)]

    def collect(steps, spots):
        arrays = [flat[step][back] for back in range(exp_count) for step in steps]
        return pl.pallas_call(
            functools.partial(collect_kernel, steps, spots, exp_count),
            out_shape=[jax.ShapeDtypeStruct((part_rows, width), bf16)] * exp_count,
            in_specs=[smem] + [vmem] * len(arrays),
            out_specs=[vmem] * exp_count,
            compiler_params=params,
        )(ctx_index.reshape(1), *arrays)

    chunks, flat = [], []
    late_from = max(1, ctx_count - 2)
    for step in range(ctx_count):
        last = step == ctx_count - 1
        following = None if last else [over(array, "ctx", 1) for array in block]
        if step == 1:
            block, all_ids = lax.optimization_barrier((block, all_ids))
        if step == 2:
            block, chunks[1] = lax.optimization_barrier((block, chunks[1]))
        if last and aligned:
            hidden = collect(list(range(late_from)), ctx_count)
            block, hidden = lax.optimization_barrier((block, hidden))
        total = project(*block, *weights)
        chunk = over(total, "ctx", ctx_count - step)
        if not last:
            block = [lax.optimization_barrier((array, total))[0] for array in following]
        chunks.append(chunk)
        if aligned:
            flat.append(forward(chunk, step, ctx_count))
    if aligned:
        late_steps, spots = list(range(late_from, ctx_count)), ctx_count
    else:
        whole = jnp.roll(jnp.stack(chunks), ctx_index, axis=0)
        whole = whole.transpose(1, 0, 2).reshape(part_rows, width)
        flat.append(forward(whole, 0, 1))
        hidden = collect([0], 1)
        late_steps, spots = [], 1
    places = jnp.stack([ctx_index, exp_index])
    out = None
    for back in range(exp_count):
        operands = (
            [places]
            + [flat[step][back] for step in late_steps]
            + [hidden[back], all_ids[back], keep_counts.reshape(1, -1)]
            + [norm_gain.reshape(1, -1), router.T]
        )
        kept = [] if out is None else [out]
        out = pl.pallas_call(
            functools.partial(finish_kernel, late_steps, spots, back, exp_count),
            out_shape=jax.ShapeDtypeStruct((exp_count, experts_here, CAP, width), bf16),
            in_specs=[smem] + [vmem] * (len(operands) - 1) + [anywhere] * len(kept),
            out_specs=anywhere,
            scratch_shapes=[
                pltpu.VMEM((part_rows, width), f32),
                pltpu.VMEM((part_rows, width), bf16),
                pltpu.VMEM((experts_here, CAP, width), bf16),
                pltpu.SemaphoreType.DMA,
            ],
            input_output_aliases={len(operands): 0} if kept else {},
            compiler_params=params,
        )(*operands, *kept)
    return out


def solution(mesh):
    placed = (
        P(("groups", "exp"), "ctx", "tp", None),
        P(("groups", "exp"), "ctx", "tp", None),
        P(("groups", "exp"), "ctx", "tp", None),
        P(("groups", "exp"), "ctx"),
        P(("groups", "exp"), ("ctx", "tp"), None),
        P("tp", "ctx"),
        P(),
        P(None, "exp"),
        P(("groups", "exp"), ("ctx", "tp"), None),
        P("groups"),
    )
    return jax.shard_map(
        on_device,
        mesh=mesh,
        in_specs=placed,
        out_specs=P(("groups", "ctx", "tp"), "exp", None, None),
        check_vma=False,
    )
```

```python
import functools
import math

import jax
import jax.numpy as jnp
from jax import lax
from jax.experimental import pallas as pl
from jax.experimental.pallas import tpu as pltpu
from jax.sharding import PartitionSpec as P

CAP = 2
EPSILON = 1e-05
DOC_ROWS = 16
VMEM_LIMIT = 12 * 1024 * 1024
VMEM_MOST = 61 * 1024 * 1024
VMEM_MUCH = 52 * 1024 * 1024


def fetch(refs, buffers, sems):
    copies = [
        pltpu.make_async_copy(ref, buffer, sems.at[number])
        for number, (ref, buffer) in enumerate(zip(refs, buffers))
    ]
    for copy in copies:
        copy.start()
    return [copy.wait for copy in copies]


def pack_kernel(groups, key_ref, value_ref, doc_ref, out_ref, *scratch):
    buffers, sems = scratch[:-1], scratch[-1]
    for wait in fetch((key_ref, value_ref, doc_ref), buffers, sems):
        wait()
    key_ref, value_ref, doc_ref = buffers
    rows, head_size = key_ref.shape
    tokens = rows // groups
    token = lax.broadcasted_iota(jnp.int32, (tokens, rows), 0)
    row = lax.broadcasted_iota(jnp.int32, (tokens, rows), 1)
    for group in range(groups):
        pick = (row == token * groups + group).astype(jnp.bfloat16)
        for place, ref in enumerate((key_ref, value_ref)):
            first = (place * groups + group) * tokens
            out_ref[first : first + tokens, :] = jnp.dot(
                pick, ref[...], preferred_element_type=jnp.float32
            ).astype(jnp.bfloat16)
    out_ref[2 * rows :, :] = jnp.broadcast_to(
        (doc_ref[...] + 1).astype(jnp.float32), (DOC_ROWS, tokens)
    ).astype(jnp.bfloat16)


def stage_kernel(count, *refs):
    for wait in fetch(refs[:count], refs[count:-1], refs[-1]):
        wait()


def attention_kernel(ratio, groups, pair, place_ref, query_ref, *refs):
    pack_refs, out_refs = refs[:-pair], refs[-pair:]
    heads, tokens, head_size = query_ref.shape
    scale = 1.0 / math.sqrt(head_size)
    core = place_ref[0]
    part_rows = tokens // pair
    held_rows = groups * tokens
    rows = lax.broadcasted_iota(jnp.int32, (tokens, tokens), 0)
    columns = lax.broadcasted_iota(jnp.int32, (tokens, tokens), 1)
    docs = [ref[2 * held_rows : 2 * held_rows + 1, :].astype(jnp.float32) for ref in pack_refs]
    own_doc = jnp.sum(jnp.where(rows == columns, docs[0], 0.0), axis=1, keepdims=True)
    allowed = [(own_doc == docs[0]) & (columns <= rows)] + [own_doc == doc for doc in docs[1:]]
    allowed = jnp.concatenate(allowed, axis=1)
    for group in range(groups):
        first = group * tokens
        keys = jnp.concatenate([ref[first : first + tokens, :] for ref in pack_refs], axis=0)
        first = held_rows + group * tokens
        held = jnp.concatenate([ref[first : first + tokens, :] for ref in pack_refs], axis=0)
        for head in range(group * ratio, (group + 1) * ratio):
            scores = lax.dot_general(
                query_ref[head], keys, (((1,), (1,)), ((), ())), preferred_element_type=jnp.float32
            )
            scores = jnp.where(allowed, scores * scale, -1e30)
            weights = jnp.exp(scores - jnp.max(scores, axis=1, keepdims=True))
            totals = jnp.sum(weights, axis=1, keepdims=True)
            mixed = jnp.dot(
                weights.astype(jnp.bfloat16), held, preferred_element_type=jnp.float32
            )
            mixed = (mixed / totals).astype(jnp.bfloat16)
            parts = [mixed[i * part_rows : (i + 1) * part_rows] for i in range(pair)]
            for turn in range(pair):
                piece = parts[turn]
                for own in range(1, pair):
                    piece = jnp.where(core == own, parts[(own + turn) % pair], piece)
                out_refs[turn][:, head * head_size : (head + 1) * head_size] = piece


def project_kernel(pair, *refs):
    block_refs, weight_refs, out_ref = refs[:pair], refs[pair : 2 * pair], refs[2 * pair]
    total = None
    for block_ref, weight_ref in zip(block_refs, weight_refs):
        product = jnp.dot(block_ref[...], weight_ref[...], preferred_element_type=jnp.float32)
        total = product if total is None else total + product
    out_ref[...] = total.astype(out_ref.dtype)


def columns_of(chunk_ref, step, spots, ctx_index):
    columns = chunk_ref.shape[1]
    first = 0 if spots == 1 else lax.rem(ctx_index + step, spots) * columns
    return pl.ds(pl.multiple_of(first, 128), columns)


def hidden_kernel(step, spots, place_ref, residual_ref, chunk_ref, out_ref):
    part = columns_of(chunk_ref, step, spots, place_ref[0])
    out_ref[...] = (
        residual_ref[:, part].astype(jnp.float32) + chunk_ref[...].astype(jnp.float32)
    ).astype(out_ref.dtype)


def collect_kernel(steps, spots, exp_count, place_ref, *refs):
    count = len(steps)
    chunk_refs, out_refs = refs[:-exp_count], refs[-exp_count:]
    for back, out_ref in enumerate(out_refs):
        for step, chunk_ref in zip(steps, chunk_refs[back * count : (back + 1) * count]):
            out_ref[:, columns_of(chunk_ref, step, spots, place_ref[0])] = chunk_ref[...]


def finish_kernel(steps, spots, back, exp_count, place_ref, *refs):
    count = len(steps)
    chunk_refs = refs[:count]
    hidden_ref, id_ref, keep_ref, gain_ref, router_ref = refs[count : count + 5]
    out_ref, total_ref, normed_ref, result_ref, out_sem = refs[-5:]
    rows, width = hidden_ref.shape
    experts = keep_ref.shape[1]
    here = router_ref.shape[0]
    ctx_index, exp_index = place_ref[0], place_ref[1]
    keep = keep_ref[...].astype(jnp.float32)
    upper = (
        lax.broadcasted_iota(jnp.int32, (rows, rows), 0)
        < lax.broadcasted_iota(jnp.int32, (rows, rows), 1)
    ).astype(jnp.bfloat16)
    total_ref[...] = hidden_ref[...].astype(jnp.float32)
    for step, chunk_ref in zip(steps, chunk_refs):
        part = columns_of(chunk_ref, step, spots, ctx_index)
        total_ref[:, part] = chunk_ref[...].astype(jnp.float32)
    hidden = total_ref[...]
    power = jnp.sum(hidden * hidden, axis=1, keepdims=True)
    factor = lax.rsqrt(power / width + EPSILON)
    normed_ref[...] = (hidden * factor * gain_ref[...].astype(jnp.float32)).astype(jnp.bfloat16)
    ids = id_ref[...]
    onehot = (ids == lax.broadcasted_iota(jnp.int32, (experts, rows), 0)).astype(jnp.float32)
    earlier = jnp.dot(onehot.astype(jnp.bfloat16), upper, preferred_element_type=jnp.float32)
    ranking = jnp.sum(onehot * earlier, axis=0, keepdims=True)
    limits = jnp.dot(
        keep.astype(jnp.bfloat16),
        onehot.astype(jnp.bfloat16),
        preferred_element_type=jnp.float32,
    )
    local = ids - exp_index * here
    logits = lax.dot_general(
        router_ref[...],
        normed_ref[...],
        (((1,), (1,)), ((), ())),
        preferred_element_type=jnp.float32,
    )
    chosen = local == lax.broadcasted_iota(jnp.int32, (here, rows), 0)
    gates = jax.nn.sigmoid(jnp.sum(jnp.where(chosen, logits, 0.0), axis=0, keepdims=True))
    target = local * CAP + ranking.astype(jnp.int32)
    target = jnp.where((ranking < limits) & (local >= 0) & (local < here), target, -1)
    table = lax.broadcasted_iota(jnp.int32, (here * CAP, rows), 0) == target
    slot_gates = jnp.sum(jnp.where(table, gates, 0.0), axis=1, keepdims=True)
    slots = jnp.dot(
        table.astype(jnp.bfloat16), normed_ref[...], preferred_element_type=jnp.float32
    )
    result_ref[...] = (slots * slot_gates).astype(jnp.bfloat16).reshape(result_ref.shape)
    source = lax.rem(exp_index - back + exp_count, exp_count)
    copy = pltpu.make_async_copy(result_ref, out_ref.at[source], out_sem)
    copy.start()
    copy.wait()


def on_device(
    queries,
    key_states,
    values,
    doc_ids,
    residual,
    out_proj,
    norm_gain,
    router,
    expert_ids,
    keep_counts,
):
    _, tokens, heads, head_size = queries.shape
    groups = key_states.shape[2]
    ctx_count = lax.axis_size("ctx")
    pair = lax.axis_size("tp")
    exp_count = lax.axis_size("exp")
    part_rows = tokens // pair
    width = residual.shape[2]
    columns = out_proj.shape[1]
    experts_here = router.shape[1]
    ctx_index = lax.axis_index("ctx")
    core = lax.axis_index("tp")
    exp_index = lax.axis_index("exp")
    reach = -(-(ctx_count * tokens // 2 - 1) // tokens)
    vmem = pl.BlockSpec(memory_space=pltpu.VMEM)
    smem = pl.BlockSpec(memory_space=pltpu.SMEM)
    anywhere = pl.BlockSpec(memory_space=pl.ANY)
    params = pltpu.CompilerParams(vmem_limit_bytes=VMEM_LIMIT)
    most = pltpu.CompilerParams(vmem_limit_bytes=VMEM_MOST)
    much = pltpu.CompilerParams(vmem_limit_bytes=VMEM_MUCH)
    bf16, f32 = jnp.bfloat16, jnp.float32

    def over(array, axis, step):
        count = lax.axis_size(axis)
        if step % count == 0:
            return array
        return lax.ppermute(array, axis, [(i, (i + step) % count) for i in range(count)])

    def along(array, moves):
        return lax.ppermute(array, "ctx", moves)

    pack = pl.pallas_call(
        functools.partial(pack_kernel, groups),
        out_shape=jax.ShapeDtypeStruct((2 * groups * tokens + DOC_ROWS, head_size), bf16),
        in_specs=[anywhere] * 3,
        out_specs=vmem,
        scratch_shapes=[pltpu.VMEM((groups * tokens, head_size), bf16)] * 2
        + [pltpu.VMEM(doc_ids.shape, doc_ids.dtype), pltpu.SemaphoreType.DMA((3,))],
        compiler_params=most,
    )(
        key_states.reshape(groups * tokens, head_size),
        values.reshape(groups * tokens, head_size),
        doc_ids,
    )
    packs = [pack] + [
        lax.ppermute(pack, "ctx", [(i, i + step) for i in range(ctx_count - step)])
        for step in range(1, reach + 1)
    ]
    ids, own_residual = expert_ids[:, :, 0], residual[0]
    pack, own_queries, early_weights = lax.optimization_barrier(
        (pack, queries[0].transpose(1, 0, 2), out_proj)
    )
    weights = [out_proj] + [over(early_weights, "tp", turn) for turn in range(1, pair)]
    staged_queries, packs[0] = pl.pallas_call(
        functools.partial(stage_kernel, 2),
        out_shape=[
            jax.ShapeDtypeStruct(own_queries.shape, bf16),
            jax.ShapeDtypeStruct(pack.shape, bf16),
        ],
        in_specs=[anywhere] * 2,
        out_specs=[vmem] * 2,
        scratch_shapes=[pltpu.SemaphoreType.DMA((2,))],
        compiler_params=much,
    )(own_queries, pack)
    all_ids = [ids] + [over(ids, "exp", back) for back in range(1, exp_count)]
    pieces = pl.pallas_call(
        functools.partial(attention_kernel, heads // groups, groups, pair),
        out_shape=[jax.ShapeDtypeStruct((part_rows, heads * head_size), bf16)] * pair,
        in_specs=[smem] + [vmem] * (1 + len(packs)),
        out_specs=[vmem] * pair,
        compiler_params=params,
    )(core.reshape(1), staged_queries, *packs)

    project = pl.pallas_call(
        functools.partial(project_kernel, pair),
        out_shape=jax.ShapeDtypeStruct((part_rows, columns), bf16),
        in_specs=[vmem] * (2 * pair),
        out_specs=vmem,
        compiler_params=params,
        cost_estimate=pl.CostEstimate(
            flops=2 * pair * part_rows * out_proj.size,
            bytes_accessed=2 * pair * out_proj.size,
            transcendentals=0,
        ),
    )
    block = [over(pieces[turn], "tp", turn) for turn in range(pair)]
    block[-1], swapped = lax.optimization_barrier((block[-1], weights[1:]))
    weights = weights[:1] + [*pl.pallas_call(
        functools.partial(stage_kernel, pair - 1),
        out_shape=[jax.ShapeDtypeStruct(out_proj.shape, bf16)] * (pair - 1),
        in_specs=[anywhere] * (pair - 1),
        out_specs=[vmem] * (pair - 1),
        scratch_shapes=[pltpu.SemaphoreType.DMA((pair - 1,))],
        compiler_params=params,
    )(*swapped)]

    aligned = columns % 128 == 0
    hidden = None

    def forward(chunk, step, spots):
        hidden = pl.pallas_call(
            functools.partial(hidden_kernel, step, spots),
            out_shape=jax.ShapeDtypeStruct(chunk.shape, bf16),
            in_specs=[smem] + [vmem] * 2,
            out_specs=vmem,
            compiler_params=params,
        )(ctx_index.reshape(1), own_residual, chunk)
        return [over(hidden, "exp", back) for back in range(exp_count)]

    def collect(steps, spots):
        arrays = [flat[step][back] for back in range(exp_count) for step in steps]
        return pl.pallas_call(
            functools.partial(collect_kernel, steps, spots, exp_count),
            out_shape=[jax.ShapeDtypeStruct((part_rows, width), bf16)] * exp_count,
            in_specs=[smem] + [vmem] * len(arrays),
            out_specs=[vmem] * exp_count,
            compiler_params=params,
        )(ctx_index.reshape(1), *arrays)

    chunks, flat = [], []
    late_from = max(1, ctx_count - 2)
    for step in range(ctx_count):
        last = step == ctx_count - 1
        following = None if last else [over(array, "ctx", 1) for array in block]
        if step == 1:
            block, all_ids = lax.optimization_barrier((block, all_ids))
        if step == 2:
            block, chunks[1], flat[:1] = lax.optimization_barrier((block, chunks[1], flat[:1]))
        if last and aligned:
            hidden = collect(list(range(late_from)), ctx_count)
            block, hidden = lax.optimization_barrier((block, hidden))
        total = project(*block, *weights)
        chunk = over(total, "ctx", ctx_count - step)
        if not last:
            block = [lax.optimization_barrier((array, total))[0] for array in following]
        chunks.append(chunk)
        if aligned:
            if step == 2:
                first, _ = lax.optimization_barrier((chunks[1], total))
                flat[1] = forward(first, 1, ctx_count)
            flat.append(forward(chunk, step, ctx_count) if step != 1 else None)
    if aligned:
        late_steps, spots = list(range(late_from, ctx_count)), ctx_count
    else:
        whole = jnp.roll(jnp.stack(chunks), ctx_index, axis=0)
        whole = whole.transpose(1, 0, 2).reshape(part_rows, width)
        flat.append(forward(whole, 0, 1))
        hidden = collect([0], 1)
        late_steps, spots = [], 1
    places = jnp.stack([ctx_index, exp_index])
    out = None
    for back in range(exp_count):
        operands = (
            [places]
            + [flat[step][back] for step in late_steps]
            + [hidden[back], all_ids[back], keep_counts.reshape(1, -1)]
            + [norm_gain.reshape(1, -1), router.T]
        )
        kept = [] if out is None else [out]
        out = pl.pallas_call(
            functools.partial(finish_kernel, late_steps, spots, back, exp_count),
            out_shape=jax.ShapeDtypeStruct((exp_count, experts_here, CAP, width), bf16),
            in_specs=[smem] + [vmem] * (len(operands) - 1) + [anywhere] * len(kept),
            out_specs=anywhere,
            scratch_shapes=[
                pltpu.VMEM((part_rows, width), f32),
                pltpu.VMEM((part_rows, width), bf16),
                pltpu.VMEM((experts_here, CAP, width), bf16),
                pltpu.SemaphoreType.DMA,
            ],
            input_output_aliases={len(operands): 0} if kept else {},
            compiler_params=params,
        )(*operands, *kept)
    return out


def solution(mesh):
    placed = (
        P(("groups", "exp"), "ctx", "tp", None),
        P(("groups", "exp"), "ctx", "tp", None),
        P(("groups", "exp"), "ctx", "tp", None),
        P(("groups", "exp"), "ctx"),
        P(("groups", "exp"), ("ctx", "tp"), None),
        P("tp", "ctx"),
        P(),
        P(None, "exp"),
        P(("groups", "exp"), ("ctx", "tp"), None),
        P("groups"),
    )
    return jax.shard_map(
        on_device,
        mesh=mesh,
        in_specs=placed,
        out_specs=P(("groups", "ctx", "tp"), "exp", None, None),
        check_vma=False,
    )
```

```python
import functools
import math

import jax
import jax.numpy as jnp
from jax import lax
from jax.experimental import pallas as pl
from jax.experimental.pallas import tpu as pltpu
from jax.sharding import PartitionSpec as P

CAP = 2
EPSILON = 1e-05
DOC_ROWS = 16
VMEM_LIMIT = 12 * 1024 * 1024
VMEM_MORE = 16 * 1024 * 1024
VMEM_MOST = 61 * 1024 * 1024
VMEM_MUCH = 52 * 1024 * 1024


def fetch(refs, buffers, sems):
    copies = [
        pltpu.make_async_copy(ref, buffer, sems.at[number])
        for number, (ref, buffer) in enumerate(zip(refs, buffers))
    ]
    for copy in copies:
        copy.start()
    return [copy.wait for copy in copies]


def pack_kernel(groups, key_ref, value_ref, doc_ref, out_ref, *scratch):
    buffers, sems = scratch[:-1], scratch[-1]
    for wait in fetch((key_ref, value_ref, doc_ref), buffers, sems):
        wait()
    key_ref, value_ref, doc_ref = buffers
    rows, head_size = key_ref.shape
    tokens = rows // groups
    token = lax.broadcasted_iota(jnp.int32, (tokens, rows), 0)
    row = lax.broadcasted_iota(jnp.int32, (tokens, rows), 1)
    for group in range(groups):
        pick = (row == token * groups + group).astype(jnp.bfloat16)
        for place, ref in enumerate((key_ref, value_ref)):
            first = (place * groups + group) * tokens
            out_ref[first : first + tokens, :] = jnp.dot(
                pick, ref[...], preferred_element_type=jnp.float32
            ).astype(jnp.bfloat16)
    out_ref[2 * rows :, :] = jnp.broadcast_to(
        (doc_ref[...] + 1).astype(jnp.float32), (DOC_ROWS, tokens)
    ).astype(jnp.bfloat16)


def stage_kernel(count, *refs):
    for wait in fetch(refs[:count], refs[count:-1], refs[-1]):
        wait()


def attention_kernel(ratio, groups, pair, place_ref, query_ref, *refs):
    pack_refs, out_refs = refs[:-pair], refs[-pair:]
    heads, tokens, head_size = query_ref.shape
    scale = 1.0 / math.sqrt(head_size)
    core = place_ref[0]
    part_rows = tokens // pair
    held_rows = groups * tokens
    rows = lax.broadcasted_iota(jnp.int32, (tokens, tokens), 0)
    columns = lax.broadcasted_iota(jnp.int32, (tokens, tokens), 1)
    docs = [ref[2 * held_rows : 2 * held_rows + 1, :].astype(jnp.float32) for ref in pack_refs]
    own_doc = jnp.sum(jnp.where(rows == columns, docs[0], 0.0), axis=1, keepdims=True)
    allowed = [(own_doc == docs[0]) & (columns <= rows)] + [own_doc == doc for doc in docs[1:]]
    allowed = jnp.concatenate(allowed, axis=1)
    for group in range(groups):
        first = group * tokens
        keys = jnp.concatenate([ref[first : first + tokens, :] for ref in pack_refs], axis=0)
        first = held_rows + group * tokens
        held = jnp.concatenate([ref[first : first + tokens, :] for ref in pack_refs], axis=0)
        for head in range(group * ratio, (group + 1) * ratio):
            scores = lax.dot_general(
                query_ref[head], keys, (((1,), (1,)), ((), ())), preferred_element_type=jnp.float32
            )
            scores = jnp.where(allowed, scores * scale, -1e30)
            weights = jnp.exp(scores - jnp.max(scores, axis=1, keepdims=True))
            totals = jnp.sum(weights, axis=1, keepdims=True)
            mixed = jnp.dot(
                weights.astype(jnp.bfloat16), held, preferred_element_type=jnp.float32
            )
            mixed = (mixed / totals).astype(jnp.bfloat16)
            parts = [mixed[i * part_rows : (i + 1) * part_rows] for i in range(pair)]
            for turn in range(pair):
                piece = parts[turn]
                for own in range(1, pair):
                    piece = jnp.where(core == own, parts[(own + turn) % pair], piece)
                out_refs[turn][:, head * head_size : (head + 1) * head_size] = piece


def project_kernel(pair, *refs):
    block_refs, weight_refs, out_ref = refs[:pair], refs[pair : 2 * pair], refs[2 * pair]
    total = None
    for block_ref, weight_ref in zip(block_refs, weight_refs):
        product = jnp.dot(block_ref[...], weight_ref[...], preferred_element_type=jnp.float32)
        total = product if total is None else total + product
    out_ref[...] = total.astype(out_ref.dtype)


def columns_of(chunk_ref, step, spots, ctx_index):
    columns = chunk_ref.shape[1]
    first = 0 if spots == 1 else lax.rem(ctx_index + step, spots) * columns
    return pl.ds(pl.multiple_of(first, 128), columns)


def hidden_kernel(step, spots, place_ref, residual_ref, chunk_ref, out_ref):
    part = columns_of(chunk_ref, step, spots, place_ref[0])
    out_ref[...] = (
        residual_ref[:, part].astype(jnp.float32) + chunk_ref[...].astype(jnp.float32)
    ).astype(out_ref.dtype)


def collect_kernel(steps, spots, exp_count, place_ref, *refs):
    count = len(steps)
    chunk_refs, out_refs = refs[:-exp_count], refs[-exp_count:]
    for back, out_ref in enumerate(out_refs):
        for step, chunk_ref in zip(steps, chunk_refs[back * count : (back + 1) * count]):
            out_ref[:, columns_of(chunk_ref, step, spots, place_ref[0])] = chunk_ref[...]


def finish_kernel(steps, spots, back, exp_count, place_ref, *refs):
    count = len(steps)
    chunk_refs = refs[:count]
    hidden_ref, id_ref, keep_ref, gain_ref, router_ref = refs[count : count + 5]
    out_ref, total_ref, normed_ref, result_ref, out_sem = refs[-5:]
    rows, width = hidden_ref.shape
    experts = keep_ref.shape[1]
    here = router_ref.shape[0]
    ctx_index, exp_index = place_ref[0], place_ref[1]
    keep = keep_ref[...].astype(jnp.float32)
    upper = (
        lax.broadcasted_iota(jnp.int32, (rows, rows), 0)
        < lax.broadcasted_iota(jnp.int32, (rows, rows), 1)
    ).astype(jnp.bfloat16)
    total_ref[...] = hidden_ref[...].astype(jnp.float32)
    for step, chunk_ref in zip(steps, chunk_refs):
        part = columns_of(chunk_ref, step, spots, ctx_index)
        total_ref[:, part] = chunk_ref[...].astype(jnp.float32)
    hidden = total_ref[...]
    power = jnp.sum(hidden * hidden, axis=1, keepdims=True)
    factor = lax.rsqrt(power / width + EPSILON)
    normed_ref[...] = (hidden * factor * gain_ref[...].astype(jnp.float32)).astype(jnp.bfloat16)
    ids = id_ref[...]
    onehot = (ids == lax.broadcasted_iota(jnp.int32, (experts, rows), 0)).astype(jnp.float32)
    earlier = jnp.dot(onehot.astype(jnp.bfloat16), upper, preferred_element_type=jnp.float32)
    ranking = jnp.sum(onehot * earlier, axis=0, keepdims=True)
    limits = jnp.dot(
        keep.astype(jnp.bfloat16),
        onehot.astype(jnp.bfloat16),
        preferred_element_type=jnp.float32,
    )
    local = ids - exp_index * here
    logits = lax.dot_general(
        router_ref[...],
        normed_ref[...],
        (((1,), (1,)), ((), ())),
        preferred_element_type=jnp.float32,
    )
    chosen = local == lax.broadcasted_iota(jnp.int32, (here, rows), 0)
    gates = jax.nn.sigmoid(jnp.sum(jnp.where(chosen, logits, 0.0), axis=0, keepdims=True))
    target = local * CAP + ranking.astype(jnp.int32)
    target = jnp.where((ranking < limits) & (local >= 0) & (local < here), target, -1)
    table = lax.broadcasted_iota(jnp.int32, (here * CAP, rows), 0) == target
    slot_gates = jnp.sum(jnp.where(table, gates, 0.0), axis=1, keepdims=True)
    slots = jnp.dot(
        table.astype(jnp.bfloat16), normed_ref[...], preferred_element_type=jnp.float32
    )
    result_ref[...] = (slots * slot_gates).astype(jnp.bfloat16).reshape(result_ref.shape)
    source = lax.rem(exp_index - back + exp_count, exp_count)
    copy = pltpu.make_async_copy(result_ref, out_ref.at[source], out_sem)
    copy.start()
    copy.wait()


def on_device(
    queries,
    key_states,
    values,
    doc_ids,
    residual,
    out_proj,
    norm_gain,
    router,
    expert_ids,
    keep_counts,
):
    _, tokens, heads, head_size = queries.shape
    groups = key_states.shape[2]
    ctx_count = lax.axis_size("ctx")
    pair = lax.axis_size("tp")
    exp_count = lax.axis_size("exp")
    part_rows = tokens // pair
    width = residual.shape[2]
    columns = out_proj.shape[1]
    experts_here = router.shape[1]
    ctx_index = lax.axis_index("ctx")
    core = lax.axis_index("tp")
    exp_index = lax.axis_index("exp")
    reach = -(-(ctx_count * tokens // 2 - 1) // tokens)
    vmem = pl.BlockSpec(memory_space=pltpu.VMEM)
    smem = pl.BlockSpec(memory_space=pltpu.SMEM)
    anywhere = pl.BlockSpec(memory_space=pl.ANY)
    params = pltpu.CompilerParams(vmem_limit_bytes=VMEM_LIMIT)
    more = pltpu.CompilerParams(vmem_limit_bytes=VMEM_MORE)
    most = pltpu.CompilerParams(vmem_limit_bytes=VMEM_MOST)
    much = pltpu.CompilerParams(vmem_limit_bytes=VMEM_MUCH)
    bf16, f32 = jnp.bfloat16, jnp.float32

    def over(array, axis, step):
        count = lax.axis_size(axis)
        if step % count == 0:
            return array
        return lax.ppermute(array, axis, [(i, (i + step) % count) for i in range(count)])

    def along(array, moves):
        return lax.ppermute(array, "ctx", moves)

    pack = pl.pallas_call(
        functools.partial(pack_kernel, groups),
        out_shape=jax.ShapeDtypeStruct((2 * groups * tokens + DOC_ROWS, head_size), bf16),
        in_specs=[anywhere] * 3,
        out_specs=vmem,
        scratch_shapes=[pltpu.VMEM((groups * tokens, head_size), bf16)] * 2
        + [pltpu.VMEM(doc_ids.shape, doc_ids.dtype), pltpu.SemaphoreType.DMA((3,))],
        compiler_params=most,
    )(
        key_states.reshape(groups * tokens, head_size),
        values.reshape(groups * tokens, head_size),
        doc_ids,
    )
    packs = [pack] + [
        lax.ppermute(pack, "ctx", [(i, i + step) for i in range(ctx_count - step)])
        for step in range(1, reach + 1)
    ]
    ids, own_residual = expert_ids[:, :, 0], residual[0]
    pack, own_queries, early_weights = lax.optimization_barrier(
        (pack, queries[0].transpose(1, 0, 2), out_proj)
    )
    weights = [out_proj] + [over(early_weights, "tp", turn) for turn in range(1, pair)]
    staged_queries, packs[0] = pl.pallas_call(
        functools.partial(stage_kernel, 2),
        out_shape=[
            jax.ShapeDtypeStruct(own_queries.shape, bf16),
            jax.ShapeDtypeStruct(pack.shape, bf16),
        ],
        in_specs=[anywhere] * 2,
        out_specs=[vmem] * 2,
        scratch_shapes=[pltpu.SemaphoreType.DMA((2,))],
        compiler_params=much,
    )(own_queries, pack)
    all_ids = [ids] + [over(ids, "exp", back) for back in range(1, exp_count)]
    pieces = pl.pallas_call(
        functools.partial(attention_kernel, heads // groups, groups, pair),
        out_shape=[jax.ShapeDtypeStruct((part_rows, heads * head_size), bf16)] * pair,
        in_specs=[smem] + [vmem] * (1 + len(packs)),
        out_specs=[vmem] * pair,
        compiler_params=more,
    )(core.reshape(1), staged_queries, *packs)

    project = pl.pallas_call(
        functools.partial(project_kernel, pair),
        out_shape=jax.ShapeDtypeStruct((part_rows, columns), bf16),
        in_specs=[vmem] * (2 * pair),
        out_specs=vmem,
        compiler_params=params,
        cost_estimate=pl.CostEstimate(
            flops=2 * pair * part_rows * out_proj.size,
            bytes_accessed=2 * pair * out_proj.size,
            transcendentals=0,
        ),
    )
    block = [over(pieces[turn], "tp", turn) for turn in range(pair)]
    block[-1], swapped = lax.optimization_barrier((block[-1], weights[1:]))
    weights = weights[:1] + [*pl.pallas_call(
        functools.partial(stage_kernel, pair - 1),
        out_shape=[jax.ShapeDtypeStruct(out_proj.shape, bf16)] * (pair - 1),
        in_specs=[anywhere] * (pair - 1),
        out_specs=[vmem] * (pair - 1),
        scratch_shapes=[pltpu.SemaphoreType.DMA((pair - 1,))],
        compiler_params=params,
    )(*swapped)]

    aligned = columns % 128 == 0
    hidden = None

    def forward(chunk, step, spots):
        hidden = pl.pallas_call(
            functools.partial(hidden_kernel, step, spots),
            out_shape=jax.ShapeDtypeStruct(chunk.shape, bf16),
            in_specs=[smem] + [vmem] * 2,
            out_specs=vmem,
            compiler_params=params,
        )(ctx_index.reshape(1), own_residual, chunk)
        return [over(hidden, "exp", back) for back in range(exp_count)]

    def collect(steps, spots):
        arrays = [flat[step][back] for back in range(exp_count) for step in steps]
        return pl.pallas_call(
            functools.partial(collect_kernel, steps, spots, exp_count),
            out_shape=[jax.ShapeDtypeStruct((part_rows, width), bf16)] * exp_count,
            in_specs=[smem] + [vmem] * len(arrays),
            out_specs=[vmem] * exp_count,
            compiler_params=params,
        )(ctx_index.reshape(1), *arrays)

    chunks, flat = [], []
    late_from = max(1, ctx_count - 2)
    for step in range(ctx_count):
        last = step == ctx_count - 1
        following = None if last else [over(array, "ctx", 1) for array in block]
        if step == 1:
            block, all_ids = lax.optimization_barrier((block, all_ids))
        if step == 2:
            block, flat[:1] = lax.optimization_barrier((block, flat[:1]))
        if last and aligned:
            hidden = collect(list(range(late_from)), ctx_count)
        total = project(*block, *weights)
        chunk = over(total, "ctx", ctx_count - step)
        if not last:
            block = [lax.optimization_barrier((array, total))[0] for array in following]
        if last and aligned:
            chunk, hidden = lax.optimization_barrier((chunk, hidden))
        chunks.append(chunk)
        if aligned:
            if step == 2:
                first, _ = lax.optimization_barrier((chunks[1], [total] + following[:1]))
                flat[1] = forward(first, 1, ctx_count)
            flat.append(forward(chunk, step, ctx_count) if step != 1 else None)
    if aligned:
        late_steps, spots = list(range(late_from, ctx_count)), ctx_count
    else:
        whole = jnp.roll(jnp.stack(chunks), ctx_index, axis=0)
        whole = whole.transpose(1, 0, 2).reshape(part_rows, width)
        flat.append(forward(whole, 0, 1))
        hidden = collect([0], 1)
        late_steps, spots = [], 1
    places = jnp.stack([ctx_index, exp_index])
    out = None
    for back in range(exp_count):
        operands = (
            [places]
            + [flat[step][back] for step in late_steps]
            + [hidden[back], all_ids[back], keep_counts.reshape(1, -1)]
            + [norm_gain.reshape(1, -1), router.T]
        )
        kept = [] if out is None else [out]
        out = pl.pallas_call(
            functools.partial(finish_kernel, late_steps, spots, back, exp_count),
            out_shape=jax.ShapeDtypeStruct((exp_count, experts_here, CAP, width), bf16),
            in_specs=[smem] + [vmem] * (len(operands) - 1) + [anywhere] * len(kept),
            out_specs=anywhere,
            scratch_shapes=[
                pltpu.VMEM((part_rows, width), f32),
                pltpu.VMEM((part_rows, width), bf16),
                pltpu.VMEM((experts_here, CAP, width), bf16),
                pltpu.SemaphoreType.DMA,
            ],
            input_output_aliases={len(operands): 0} if kept else {},
            compiler_params=params,
        )(*operands, *kept)
    return out


def solution(mesh):
    placed = (
        P(("groups", "exp"), "ctx", "tp", None),
        P(("groups", "exp"), "ctx", "tp", None),
        P(("groups", "exp"), "ctx", "tp", None),
        P(("groups", "exp"), "ctx"),
        P(("groups", "exp"), ("ctx", "tp"), None),
        P("tp", "ctx"),
        P(),
        P(None, "exp"),
        P(("groups", "exp"), ("ctx", "tp"), None),
        P("groups"),
    )
    return jax.shard_map(
        on_device,
        mesh=mesh,
        in_specs=placed,
        out_specs=P(("groups", "ctx", "tp"), "exp", None, None),
        check_vma=False,
    )
```

```python
import functools
import math

import jax
import jax.numpy as jnp
from jax import lax
from jax.experimental import pallas as pl
from jax.experimental.pallas import tpu as pltpu
from jax.sharding import PartitionSpec as P

CAP = 2
EPSILON = 1e-05
DOC_ROWS = 16
VMEM_LIMIT = 12 * 1024 * 1024
VMEM_MOST = 61 * 1024 * 1024
VMEM_MUCH = 52 * 1024 * 1024


def fetch(refs, buffers, sems):
    copies = [
        pltpu.make_async_copy(ref, buffer, sems.at[number])
        for number, (ref, buffer) in enumerate(zip(refs, buffers))
    ]
    for copy in copies:
        copy.start()
    return [copy.wait for copy in copies]


def pack_kernel(groups, key_ref, value_ref, doc_ref, out_ref, *scratch):
    buffers, sems = scratch[:-1], scratch[-1]
    for wait in fetch((key_ref, value_ref, doc_ref), buffers, sems):
        wait()
    key_ref, value_ref, doc_ref = buffers
    rows, head_size = key_ref.shape
    tokens = rows // groups
    token = lax.broadcasted_iota(jnp.int32, (tokens, rows), 0)
    row = lax.broadcasted_iota(jnp.int32, (tokens, rows), 1)
    for group in range(groups):
        pick = (row == token * groups + group).astype(jnp.bfloat16)
        for place, ref in enumerate((key_ref, value_ref)):
            first = (place * groups + group) * tokens
            out_ref[first : first + tokens, :] = jnp.dot(
                pick, ref[...], preferred_element_type=jnp.float32
            ).astype(jnp.bfloat16)
    out_ref[2 * rows :, :] = jnp.broadcast_to(
        (doc_ref[...] + 1).astype(jnp.float32), (DOC_ROWS, tokens)
    ).astype(jnp.bfloat16)


def stage_kernel(count, *refs):
    for wait in fetch(refs[:count], refs[count:-1], refs[-1]):
        wait()


def attention_kernel(ratio, groups, pair, place_ref, query_ref, *refs):
    pack_refs, out_refs = refs[:-pair], refs[-pair:]
    heads, tokens, head_size = query_ref.shape
    scale = 1.0 / math.sqrt(head_size)
    core = place_ref[0]
    part_rows = tokens // pair
    held_rows = groups * tokens
    rows = lax.broadcasted_iota(jnp.int32, (tokens, tokens), 0)
    columns = lax.broadcasted_iota(jnp.int32, (tokens, tokens), 1)
    docs = [ref[2 * held_rows : 2 * held_rows + 1, :].astype(jnp.float32) for ref in pack_refs]
    own_doc = jnp.sum(jnp.where(rows == columns, docs[0], 0.0), axis=1, keepdims=True)
    allowed = [(own_doc == docs[0]) & (columns <= rows)] + [own_doc == doc for doc in docs[1:]]
    allowed = jnp.concatenate(allowed, axis=1)
    for group in range(groups):
        first = group * tokens
        keys = jnp.concatenate([ref[first : first + tokens, :] for ref in pack_refs], axis=0)
        first = held_rows + group * tokens
        held = jnp.concatenate([ref[first : first + tokens, :] for ref in pack_refs], axis=0)
        for head in range(group * ratio, (group + 1) * ratio):
            scores = lax.dot_general(
                query_ref[head], keys, (((1,), (1,)), ((), ())), preferred_element_type=jnp.float32
            )
            scores = jnp.where(allowed, scores * scale, -1e30)
            weights = jnp.exp(scores - jnp.max(scores, axis=1, keepdims=True))
            totals = jnp.sum(weights, axis=1, keepdims=True)
            mixed = jnp.dot(
                weights.astype(jnp.bfloat16), held, preferred_element_type=jnp.float32
            )
            mixed = (mixed / totals).astype(jnp.bfloat16)
            parts = [mixed[i * part_rows : (i + 1) * part_rows] for i in range(pair)]
            for turn in range(pair):
                piece = parts[turn]
                for own in range(1, pair):
                    piece = jnp.where(core == own, parts[(own + turn) % pair], piece)
                out_refs[turn][:, head * head_size : (head + 1) * head_size] = piece


def project_kernel(pair, *refs):
    block_refs, weight_refs, out_ref = refs[:pair], refs[pair : 2 * pair], refs[2 * pair]
    total = None
    for block_ref, weight_ref in zip(block_refs, weight_refs):
        product = jnp.dot(block_ref[...], weight_ref[...], preferred_element_type=jnp.float32)
        total = product if total is None else total + product
    out_ref[...] = total.astype(out_ref.dtype)


def columns_of(chunk_ref, step, spots, ctx_index):
    columns = chunk_ref.shape[1]
    first = 0 if spots == 1 else lax.rem(ctx_index + step, spots) * columns
    return pl.ds(pl.multiple_of(first, 128), columns)


def hidden_kernel(step, spots, place_ref, residual_ref, chunk_ref, out_ref):
    part = columns_of(chunk_ref, step, spots, place_ref[0])
    out_ref[...] = (
        residual_ref[:, part].astype(jnp.float32) + chunk_ref[...].astype(jnp.float32)
    ).astype(out_ref.dtype)


def collect_kernel(steps, spots, exp_count, place_ref, *refs):
    count = len(steps)
    chunk_refs, out_refs = refs[:-exp_count], refs[-exp_count:]
    for back, out_ref in enumerate(out_refs):
        for step, chunk_ref in zip(steps, chunk_refs[back * count : (back + 1) * count]):
            out_ref[:, columns_of(chunk_ref, step, spots, place_ref[0])] = chunk_ref[...]


def finish_kernel(steps, spots, back, exp_count, place_ref, *refs):
    count = len(steps)
    chunk_refs = refs[:count]
    hidden_ref, id_ref, keep_ref, gain_ref, router_ref = refs[count : count + 5]
    out_ref, total_ref, normed_ref, result_ref, out_sem = refs[-5:]
    rows, width = hidden_ref.shape
    experts = keep_ref.shape[1]
    here = router_ref.shape[0]
    ctx_index, exp_index = place_ref[0], place_ref[1]
    keep = keep_ref[...].astype(jnp.float32)
    upper = (
        lax.broadcasted_iota(jnp.int32, (rows, rows), 0)
        < lax.broadcasted_iota(jnp.int32, (rows, rows), 1)
    ).astype(jnp.bfloat16)
    total_ref[...] = hidden_ref[...].astype(jnp.float32)
    for step, chunk_ref in zip(steps, chunk_refs):
        part = columns_of(chunk_ref, step, spots, ctx_index)
        total_ref[:, part] = chunk_ref[...].astype(jnp.float32)
    hidden = total_ref[...]
    power = jnp.sum(hidden * hidden, axis=1, keepdims=True)
    factor = lax.rsqrt(power / width + EPSILON)
    normed_ref[...] = (hidden * factor * gain_ref[...].astype(jnp.float32)).astype(jnp.bfloat16)
    ids = id_ref[...]
    onehot = (ids == lax.broadcasted_iota(jnp.int32, (experts, rows), 0)).astype(jnp.float32)
    earlier = jnp.dot(onehot.astype(jnp.bfloat16), upper, preferred_element_type=jnp.float32)
    ranking = jnp.sum(onehot * earlier, axis=0, keepdims=True)
    limits = jnp.dot(
        keep.astype(jnp.bfloat16),
        onehot.astype(jnp.bfloat16),
        preferred_element_type=jnp.float32,
    )
    local = ids - exp_index * here
    logits = lax.dot_general(
        router_ref[...],
        normed_ref[...],
        (((1,), (1,)), ((), ())),
        preferred_element_type=jnp.float32,
    )
    chosen = local == lax.broadcasted_iota(jnp.int32, (here, rows), 0)
    gates = jax.nn.sigmoid(jnp.sum(jnp.where(chosen, logits, 0.0), axis=0, keepdims=True))
    target = local * CAP + ranking.astype(jnp.int32)
    target = jnp.where((ranking < limits) & (local >= 0) & (local < here), target, -1)
    table = lax.broadcasted_iota(jnp.int32, (here * CAP, rows), 0) == target
    slot_gates = jnp.sum(jnp.where(table, gates, 0.0), axis=1, keepdims=True)
    slots = jnp.dot(
        table.astype(jnp.bfloat16), normed_ref[...], preferred_element_type=jnp.float32
    )
    result_ref[...] = (slots * slot_gates).astype(jnp.bfloat16).reshape(result_ref.shape)
    source = lax.rem(exp_index - back + exp_count, exp_count)
    copy = pltpu.make_async_copy(result_ref, out_ref.at[source], out_sem)
    copy.start()
    copy.wait()


def on_device(
    queries,
    key_states,
    values,
    doc_ids,
    residual,
    out_proj,
    norm_gain,
    router,
    expert_ids,
    keep_counts,
):
    _, tokens, heads, head_size = queries.shape
    groups = key_states.shape[2]
    ctx_count = lax.axis_size("ctx")
    pair = lax.axis_size("tp")
    exp_count = lax.axis_size("exp")
    part_rows = tokens // pair
    width = residual.shape[2]
    columns = out_proj.shape[1]
    experts_here = router.shape[1]
    ctx_index = lax.axis_index("ctx")
    core = lax.axis_index("tp")
    exp_index = lax.axis_index("exp")
    reach = -(-(ctx_count * tokens // 2 - 1) // tokens)
    vmem = pl.BlockSpec(memory_space=pltpu.VMEM)
    smem = pl.BlockSpec(memory_space=pltpu.SMEM)
    anywhere = pl.BlockSpec(memory_space=pl.ANY)
    params = pltpu.CompilerParams(vmem_limit_bytes=VMEM_LIMIT)
    most = pltpu.CompilerParams(vmem_limit_bytes=VMEM_MOST)
    much = pltpu.CompilerParams(vmem_limit_bytes=VMEM_MUCH)
    bf16, f32 = jnp.bfloat16, jnp.float32

    def over(array, axis, step):
        count = lax.axis_size(axis)
        if step % count == 0:
            return array
        return lax.ppermute(array, axis, [(i, (i + step) % count) for i in range(count)])

    def along(array, moves):
        return lax.ppermute(array, "ctx", moves)

    pack = pl.pallas_call(
        functools.partial(pack_kernel, groups),
        out_shape=jax.ShapeDtypeStruct((2 * groups * tokens + DOC_ROWS, head_size), bf16),
        in_specs=[anywhere] * 3,
        out_specs=vmem,
        scratch_shapes=[pltpu.VMEM((groups * tokens, head_size), bf16)] * 2
        + [pltpu.VMEM(doc_ids.shape, doc_ids.dtype), pltpu.SemaphoreType.DMA((3,))],
        compiler_params=most,
    )(
        key_states.reshape(groups * tokens, head_size),
        values.reshape(groups * tokens, head_size),
        doc_ids,
    )
    packs = [pack] + [
        lax.ppermute(pack, "ctx", [(i, i + step) for i in range(ctx_count - step)])
        for step in range(1, reach + 1)
    ]
    ids, own_residual = expert_ids[:, :, 0], residual[0]
    pack, own_queries, early_weights = lax.optimization_barrier(
        (pack, queries[0].transpose(1, 0, 2), out_proj)
    )
    weights = [out_proj] + [over(early_weights, "tp", turn) for turn in range(1, pair)]
    staged_queries, packs[0] = pl.pallas_call(
        functools.partial(stage_kernel, 2),
        out_shape=[
            jax.ShapeDtypeStruct(own_queries.shape, bf16),
            jax.ShapeDtypeStruct(pack.shape, bf16),
        ],
        in_specs=[anywhere] * 2,
        out_specs=[vmem] * 2,
        scratch_shapes=[pltpu.SemaphoreType.DMA((2,))],
        compiler_params=much,
    )(own_queries, pack)
    all_ids = [ids] + [over(ids, "exp", back) for back in range(1, exp_count)]
    staged_queries, all_ids = lax.optimization_barrier((staged_queries, all_ids))
    pieces = pl.pallas_call(
        functools.partial(attention_kernel, heads // groups, groups, pair),
        out_shape=[jax.ShapeDtypeStruct((part_rows, heads * head_size), bf16)] * pair,
        in_specs=[smem] + [vmem] * (1 + len(packs)),
        out_specs=[vmem] * pair,
        compiler_params=params,
    )(core.reshape(1), staged_queries, *packs)

    project = pl.pallas_call(
        functools.partial(project_kernel, pair),
        out_shape=jax.ShapeDtypeStruct((part_rows, columns), bf16),
        in_specs=[vmem] * (2 * pair),
        out_specs=vmem,
        compiler_params=params,
        cost_estimate=pl.CostEstimate(
            flops=2 * pair * part_rows * out_proj.size,
            bytes_accessed=2 * pair * out_proj.size,
            transcendentals=0,
        ),
    )
    block = [over(pieces[turn], "tp", turn) for turn in range(pair)]
    block[-1], swapped = lax.optimization_barrier((block[-1], weights[1:]))
    weights = weights[:1] + [*pl.pallas_call(
        functools.partial(stage_kernel, pair - 1),
        out_shape=[jax.ShapeDtypeStruct(out_proj.shape, bf16)] * (pair - 1),
        in_specs=[anywhere] * (pair - 1),
        out_specs=[vmem] * (pair - 1),
        scratch_shapes=[pltpu.SemaphoreType.DMA((pair - 1,))],
        compiler_params=params,
    )(*swapped)]

    aligned = columns % 128 == 0
    hidden = None

    def forward(chunk, step, spots):
        hidden = pl.pallas_call(
            functools.partial(hidden_kernel, step, spots),
            out_shape=jax.ShapeDtypeStruct(chunk.shape, bf16),
            in_specs=[smem] + [vmem] * 2,
            out_specs=vmem,
            compiler_params=params,
        )(ctx_index.reshape(1), own_residual, chunk)
        return [over(hidden, "exp", back) for back in range(exp_count)]

    def collect(steps, spots):
        arrays = [flat[step][back] for back in range(exp_count) for step in steps]
        return pl.pallas_call(
            functools.partial(collect_kernel, steps, spots, exp_count),
            out_shape=[jax.ShapeDtypeStruct((part_rows, width), bf16)] * exp_count,
            in_specs=[smem] + [vmem] * len(arrays),
            out_specs=[vmem] * exp_count,
            compiler_params=params,
        )(ctx_index.reshape(1), *arrays)

    chunks, flat = [], []
    late_from = max(1, ctx_count - 2)
    for step in range(ctx_count):
        last = step == ctx_count - 1
        following = None if last else [over(array, "ctx", 1) for array in block]
        if step == 2:
            block, chunks[1] = lax.optimization_barrier((block, chunks[1]))
        if step == 3 and aligned:
            block, flat[0] = lax.optimization_barrier((block, flat[0]))
        if last and aligned:
            hidden = collect(list(range(late_from)), ctx_count)
        total = project(*block, *weights)
        chunk = over(total, "ctx", ctx_count - step)
        if not last:
            block = [lax.optimization_barrier((array, total))[0] for array in following]
        if last and aligned:
            chunk, hidden = lax.optimization_barrier((chunk, hidden))
        chunks.append(chunk)
        if aligned:
            if step in (1, 2) and not last:
                first, _ = lax.optimization_barrier((chunks[step - 1], [total] + following[:1]))
                flat[step - 1] = forward(first, step - 1, ctx_count)
            flat.append(forward(chunk, step, ctx_count) if step > 1 or last else None)
    if aligned:
        late_steps, spots = list(range(late_from, ctx_count)), ctx_count
    else:
        whole = jnp.roll(jnp.stack(chunks), ctx_index, axis=0)
        whole = whole.transpose(1, 0, 2).reshape(part_rows, width)
        flat.append(forward(whole, 0, 1))
        hidden = collect([0], 1)
        late_steps, spots = [], 1
    places = jnp.stack([ctx_index, exp_index])
    out = None
    for back in range(exp_count):
        operands = (
            [places]
            + [flat[step][back] for step in late_steps]
            + [hidden[back], all_ids[back], keep_counts.reshape(1, -1)]
            + [norm_gain.reshape(1, -1), router.T]
        )
        kept = [] if out is None else [out]
        out = pl.pallas_call(
            functools.partial(finish_kernel, late_steps, spots, back, exp_count),
            out_shape=jax.ShapeDtypeStruct((exp_count, experts_here, CAP, width), bf16),
            in_specs=[smem] + [vmem] * (len(operands) - 1) + [anywhere] * len(kept),
            out_specs=anywhere,
            scratch_shapes=[
                pltpu.VMEM((part_rows, width), f32),
                pltpu.VMEM((part_rows, width), bf16),
                pltpu.VMEM((experts_here, CAP, width), bf16),
                pltpu.SemaphoreType.DMA,
            ],
            input_output_aliases={len(operands): 0} if kept else {},
            compiler_params=params,
        )(*operands, *kept)
    return out


def solution(mesh):
    placed = (
        P(("groups", "exp"), "ctx", "tp", None),
        P(("groups", "exp"), "ctx", "tp", None),
        P(("groups", "exp"), "ctx", "tp", None),
        P(("groups", "exp"), "ctx"),
        P(("groups", "exp"), ("ctx", "tp"), None),
        P("tp", "ctx"),
        P(),
        P(None, "exp"),
        P(("groups", "exp"), ("ctx", "tp"), None),
        P("groups"),
    )
    return jax.shard_map(
        on_device,
        mesh=mesh,
        in_specs=placed,
        out_specs=P(("groups", "ctx", "tp"), "exp", None, None),
        check_vma=False,
    )
```

```python
import functools
import math

import jax
import jax.numpy as jnp
from jax import lax
from jax.experimental import pallas as pl
from jax.experimental.pallas import tpu as pltpu
from jax.sharding import PartitionSpec as P

CAP = 2
EPSILON = 1e-05
DOC_ROWS = 16
VMEM_LIMIT = 8 * 1024 * 1024
VMEM_MOST = 61 * 1024 * 1024
VMEM_MUCH = 52 * 1024 * 1024


def fetch(refs, buffers, sems):
    copies = [
        pltpu.make_async_copy(ref, buffer, sems.at[number])
        for number, (ref, buffer) in enumerate(zip(refs, buffers))
    ]
    for copy in copies:
        copy.start()
    return [copy.wait for copy in copies]


def pack_kernel(groups, key_ref, value_ref, doc_ref, out_ref, *scratch):
    buffers, sems = scratch[:-1], scratch[-1]
    for wait in fetch((key_ref, value_ref, doc_ref), buffers, sems):
        wait()
    key_ref, value_ref, doc_ref = buffers
    rows, head_size = key_ref.shape
    tokens = rows // groups
    token = lax.broadcasted_iota(jnp.int32, (tokens, rows), 0)
    row = lax.broadcasted_iota(jnp.int32, (tokens, rows), 1)
    for group in range(groups):
        pick = (row == token * groups + group).astype(jnp.bfloat16)
        for place, ref in enumerate((key_ref, value_ref)):
            first = (place * groups + group) * tokens
            out_ref[first : first + tokens, :] = jnp.dot(
                pick, ref[...], preferred_element_type=jnp.float32
            ).astype(jnp.bfloat16)
    out_ref[2 * rows :, :] = jnp.broadcast_to(
        (doc_ref[...] + 1).astype(jnp.float32), (DOC_ROWS, tokens)
    ).astype(jnp.bfloat16)


def stage_kernel(count, *refs):
    for wait in fetch(refs[:count], refs[count:-1], refs[-1]):
        wait()


def attention_kernel(ratio, groups, pair, place_ref, query_ref, *refs):
    pack_refs, out_refs = refs[:-pair], refs[-pair:]
    heads, tokens, head_size = query_ref.shape
    scale = 1.0 / math.sqrt(head_size)
    core = place_ref[0]
    part_rows = tokens // pair
    held_rows = groups * tokens
    rows = lax.broadcasted_iota(jnp.int32, (tokens, tokens), 0)
    columns = lax.broadcasted_iota(jnp.int32, (tokens, tokens), 1)
    docs = [ref[2 * held_rows : 2 * held_rows + 1, :].astype(jnp.float32) for ref in pack_refs]
    own_doc = jnp.sum(jnp.where(rows == columns, docs[0], 0.0), axis=1, keepdims=True)
    allowed = [(own_doc == docs[0]) & (columns <= rows)] + [own_doc == doc for doc in docs[1:]]
    allowed = jnp.concatenate(allowed, axis=1)
    for group in range(groups):
        first = group * tokens
        keys = jnp.concatenate([ref[first : first + tokens, :] for ref in pack_refs], axis=0)
        first = held_rows + group * tokens
        held = jnp.concatenate([ref[first : first + tokens, :] for ref in pack_refs], axis=0)
        for head in range(group * ratio, (group + 1) * ratio):
            scores = lax.dot_general(
                query_ref[head], keys, (((1,), (1,)), ((), ())), preferred_element_type=jnp.float32
            )
            scores = jnp.where(allowed, scores * scale, -1e30)
            weights = jnp.exp(scores - jnp.max(scores, axis=1, keepdims=True))
            totals = jnp.sum(weights, axis=1, keepdims=True)
            mixed = jnp.dot(
                weights.astype(jnp.bfloat16), held, preferred_element_type=jnp.float32
            )
            mixed = (mixed / totals).astype(jnp.bfloat16)
            parts = [mixed[i * part_rows : (i + 1) * part_rows] for i in range(pair)]
            for turn in range(pair):
                piece = parts[turn]
                for own in range(1, pair):
                    piece = jnp.where(core == own, parts[(own + turn) % pair], piece)
                out_refs[turn][:, head * head_size : (head + 1) * head_size] = piece


def project_kernel(pair, *refs):
    block_refs, weight_refs, out_ref = refs[:pair], refs[pair : 2 * pair], refs[2 * pair]
    total = None
    for block_ref, weight_ref in zip(block_refs, weight_refs):
        product = jnp.dot(block_ref[...], weight_ref[...], preferred_element_type=jnp.float32)
        total = product if total is None else total + product
    out_ref[...] = total.astype(out_ref.dtype)


def columns_of(chunk_ref, step, spots, ctx_index):
    columns = chunk_ref.shape[1]
    first = 0 if spots == 1 else lax.rem(ctx_index + step, spots) * columns
    return pl.ds(pl.multiple_of(first, 128), columns)


def hidden_kernel(step, spots, place_ref, residual_ref, chunk_ref, out_ref):
    part = columns_of(chunk_ref, step, spots, place_ref[0])
    out_ref[...] = (
        residual_ref[:, part].astype(jnp.float32) + chunk_ref[...].astype(jnp.float32)
    ).astype(out_ref.dtype)


def collect_kernel(steps, spots, exp_count, place_ref, *refs):
    count = len(steps)
    chunk_refs, out_refs = refs[:-exp_count], refs[-exp_count:]
    for back, out_ref in enumerate(out_refs):
        for step, chunk_ref in zip(steps, chunk_refs[back * count : (back + 1) * count]):
            out_ref[:, columns_of(chunk_ref, step, spots, place_ref[0])] = chunk_ref[...]


def finish_kernel(steps, spots, back, exp_count, place_ref, *refs):
    count = len(steps)
    chunk_refs = refs[:count]
    hidden_ref, id_ref, keep_ref, gain_ref, router_ref = refs[count : count + 5]
    out_ref, total_ref, normed_ref, result_ref, out_sem = refs[-5:]
    rows, width = hidden_ref.shape
    experts = keep_ref.shape[1]
    here = router_ref.shape[0]
    ctx_index, exp_index = place_ref[0], place_ref[1]
    keep = keep_ref[...].astype(jnp.float32)
    upper = (
        lax.broadcasted_iota(jnp.int32, (rows, rows), 0)
        < lax.broadcasted_iota(jnp.int32, (rows, rows), 1)
    ).astype(jnp.bfloat16)
    total_ref[...] = hidden_ref[...].astype(jnp.float32)
    for step, chunk_ref in zip(steps, chunk_refs):
        part = columns_of(chunk_ref, step, spots, ctx_index)
        total_ref[:, part] = chunk_ref[...].astype(jnp.float32)
    hidden = total_ref[...]
    power = jnp.sum(hidden * hidden, axis=1, keepdims=True)
    factor = lax.rsqrt(power / width + EPSILON)
    normed_ref[...] = (hidden * factor * gain_ref[...].astype(jnp.float32)).astype(jnp.bfloat16)
    ids = id_ref[...]
    onehot = (ids == lax.broadcasted_iota(jnp.int32, (experts, rows), 0)).astype(jnp.float32)
    earlier = jnp.dot(onehot.astype(jnp.bfloat16), upper, preferred_element_type=jnp.float32)
    ranking = jnp.sum(onehot * earlier, axis=0, keepdims=True)
    limits = jnp.dot(
        keep.astype(jnp.bfloat16),
        onehot.astype(jnp.bfloat16),
        preferred_element_type=jnp.float32,
    )
    local = ids - exp_index * here
    logits = lax.dot_general(
        router_ref[...],
        normed_ref[...],
        (((1,), (1,)), ((), ())),
        preferred_element_type=jnp.float32,
    )
    chosen = local == lax.broadcasted_iota(jnp.int32, (here, rows), 0)
    gates = jax.nn.sigmoid(jnp.sum(jnp.where(chosen, logits, 0.0), axis=0, keepdims=True))
    target = local * CAP + ranking.astype(jnp.int32)
    target = jnp.where((ranking < limits) & (local >= 0) & (local < here), target, -1)
    table = lax.broadcasted_iota(jnp.int32, (here * CAP, rows), 0) == target
    slot_gates = jnp.sum(jnp.where(table, gates, 0.0), axis=1, keepdims=True)
    slots = jnp.dot(
        table.astype(jnp.bfloat16), normed_ref[...], preferred_element_type=jnp.float32
    )
    result_ref[...] = (slots * slot_gates).astype(jnp.bfloat16).reshape(result_ref.shape)
    source = lax.rem(exp_index - back + exp_count, exp_count)
    copy = pltpu.make_async_copy(result_ref, out_ref.at[source], out_sem)
    copy.start()
    copy.wait()


def on_device(
    queries,
    key_states,
    values,
    doc_ids,
    residual,
    out_proj,
    norm_gain,
    router,
    expert_ids,
    keep_counts,
):
    _, tokens, heads, head_size = queries.shape
    groups = key_states.shape[2]
    ctx_count = lax.axis_size("ctx")
    pair = lax.axis_size("tp")
    exp_count = lax.axis_size("exp")
    part_rows = tokens // pair
    width = residual.shape[2]
    columns = out_proj.shape[1]
    experts_here = router.shape[1]
    ctx_index = lax.axis_index("ctx")
    core = lax.axis_index("tp")
    exp_index = lax.axis_index("exp")
    reach = -(-(ctx_count * tokens // 2 - 1) // tokens)
    vmem = pl.BlockSpec(memory_space=pltpu.VMEM)
    smem = pl.BlockSpec(memory_space=pltpu.SMEM)
    anywhere = pl.BlockSpec(memory_space=pl.ANY)
    params = pltpu.CompilerParams(vmem_limit_bytes=VMEM_LIMIT)
    most = pltpu.CompilerParams(vmem_limit_bytes=VMEM_MOST)
    much = pltpu.CompilerParams(vmem_limit_bytes=VMEM_MUCH)
    bf16, f32 = jnp.bfloat16, jnp.float32

    def over(array, axis, step):
        count = lax.axis_size(axis)
        if step % count == 0:
            return array
        return lax.ppermute(array, axis, [(i, (i + step) % count) for i in range(count)])

    def along(array, moves):
        return lax.ppermute(array, "ctx", moves)

    pack = pl.pallas_call(
        functools.partial(pack_kernel, groups),
        out_shape=jax.ShapeDtypeStruct((2 * groups * tokens + DOC_ROWS, head_size), bf16),
        in_specs=[anywhere] * 3,
        out_specs=vmem,
        scratch_shapes=[pltpu.VMEM((groups * tokens, head_size), bf16)] * 2
        + [pltpu.VMEM(doc_ids.shape, doc_ids.dtype), pltpu.SemaphoreType.DMA((3,))],
        compiler_params=most,
    )(
        key_states.reshape(groups * tokens, head_size),
        values.reshape(groups * tokens, head_size),
        doc_ids,
    )
    packs = [pack] + [
        lax.ppermute(pack, "ctx", [(i, i + step) for i in range(ctx_count - step)])
        for step in range(1, reach + 1)
    ]
    ids, own_residual = expert_ids[:, :, 0], residual[0]
    pack, own_queries, early_weights = lax.optimization_barrier(
        (pack, queries[0].transpose(1, 0, 2), out_proj)
    )
    weights = [out_proj] + [over(early_weights, "tp", turn) for turn in range(1, pair)]
    staged_queries, packs[0] = pl.pallas_call(
        functools.partial(stage_kernel, 2),
        out_shape=[
            jax.ShapeDtypeStruct(own_queries.shape, bf16),
            jax.ShapeDtypeStruct(pack.shape, bf16),
        ],
        in_specs=[anywhere] * 2,
        out_specs=[vmem] * 2,
        scratch_shapes=[pltpu.SemaphoreType.DMA((2,))],
        compiler_params=much,
    )(own_queries, pack)
    all_ids = [ids] + [over(ids, "exp", back) for back in range(1, exp_count)]
    staged_queries, all_ids = lax.optimization_barrier((staged_queries, all_ids))
    pieces = pl.pallas_call(
        functools.partial(attention_kernel, heads // groups, groups, pair),
        out_shape=[jax.ShapeDtypeStruct((part_rows, heads * head_size), bf16)] * pair,
        in_specs=[smem] + [vmem] * (1 + len(packs)),
        out_specs=[vmem] * pair,
        compiler_params=params,
    )(core.reshape(1), staged_queries, *packs)

    project = pl.pallas_call(
        functools.partial(project_kernel, pair),
        out_shape=jax.ShapeDtypeStruct((part_rows, columns), bf16),
        in_specs=[vmem] * (2 * pair),
        out_specs=vmem,
        compiler_params=params,
        cost_estimate=pl.CostEstimate(
            flops=2 * pair * part_rows * out_proj.size,
            bytes_accessed=2 * pair * out_proj.size,
            transcendentals=0,
        ),
    )
    block = [over(pieces[turn], "tp", turn) for turn in range(pair)]
    block[-1], swapped = lax.optimization_barrier((block[-1], weights[1:]))
    weights = weights[:1] + [*pl.pallas_call(
        functools.partial(stage_kernel, pair - 1),
        out_shape=[jax.ShapeDtypeStruct(out_proj.shape, bf16)] * (pair - 1),
        in_specs=[anywhere] * (pair - 1),
        out_specs=[vmem] * (pair - 1),
        scratch_shapes=[pltpu.SemaphoreType.DMA((pair - 1,))],
        compiler_params=params,
    )(*swapped)]

    aligned = columns % 128 == 0
    hidden = None

    def forward(chunk, step, spots):
        hidden = pl.pallas_call(
            functools.partial(hidden_kernel, step, spots),
            out_shape=jax.ShapeDtypeStruct(chunk.shape, bf16),
            in_specs=[smem] + [vmem] * 2,
            out_specs=vmem,
            compiler_params=params,
        )(ctx_index.reshape(1), own_residual, chunk)
        return [over(hidden, "exp", back) for back in range(exp_count)]

    def collect(steps, spots):
        arrays = [flat[step][back] for back in range(exp_count) for step in steps]
        return pl.pallas_call(
            functools.partial(collect_kernel, steps, spots, exp_count),
            out_shape=[jax.ShapeDtypeStruct((part_rows, width), bf16)] * exp_count,
            in_specs=[smem] + [vmem] * len(arrays),
            out_specs=[vmem] * exp_count,
            compiler_params=params,
        )(ctx_index.reshape(1), *arrays)

    chunks, flat = [], []
    late_from = max(1, ctx_count - 2)
    for step in range(ctx_count):
        last = step == ctx_count - 1
        following = None if last else [over(array, "ctx", 1) for array in block]
        if step == 2:
            block, chunks[1] = lax.optimization_barrier((block, chunks[1]))
        if step == 3 and aligned:
            block, flat[0] = lax.optimization_barrier((block, flat[0]))
        if last and aligned:
            hidden = collect(list(range(late_from)), ctx_count)
        total = project(*block, *weights)
        chunk = over(total, "ctx", ctx_count - step)
        if not last:
            block = [lax.optimization_barrier((array, total))[0] for array in following]
        if last and aligned:
            chunk, hidden = lax.optimization_barrier((chunk, hidden))
        chunks.append(chunk)
        if aligned:
            if step in (1, 2) and not last:
                first, _ = lax.optimization_barrier((chunks[step - 1], [total] + following[:1]))
                flat[step - 1] = forward(first, step - 1, ctx_count)
            flat.append(forward(chunk, step, ctx_count) if step > 1 or last else None)
    if aligned:
        late_steps, spots = list(range(late_from, ctx_count)), ctx_count
    else:
        whole = jnp.roll(jnp.stack(chunks), ctx_index, axis=0)
        whole = whole.transpose(1, 0, 2).reshape(part_rows, width)
        flat.append(forward(whole, 0, 1))
        hidden = collect([0], 1)
        late_steps, spots = [], 1
    places = jnp.stack([ctx_index, exp_index])
    out = None
    for back in range(exp_count):
        operands = (
            [places]
            + [flat[step][back] for step in late_steps]
            + [hidden[back], all_ids[back], keep_counts.reshape(1, -1)]
            + [norm_gain.reshape(1, -1), router.T]
        )
        kept = [] if out is None else [out]
        out = pl.pallas_call(
            functools.partial(finish_kernel, late_steps, spots, back, exp_count),
            out_shape=jax.ShapeDtypeStruct((exp_count, experts_here, CAP, width), bf16),
            in_specs=[smem] + [vmem] * (len(operands) - 1) + [anywhere] * len(kept),
            out_specs=anywhere,
            scratch_shapes=[
                pltpu.VMEM((part_rows, width), f32),
                pltpu.VMEM((part_rows, width), bf16),
                pltpu.VMEM((experts_here, CAP, width), bf16),
                pltpu.SemaphoreType.DMA,
            ],
            input_output_aliases={len(operands): 0} if kept else {},
            compiler_params=params,
        )(*operands, *kept)
    return out


def solution(mesh):
    placed = (
        P(("groups", "exp"), "ctx", "tp", None),
        P(("groups", "exp"), "ctx", "tp", None),
        P(("groups", "exp"), "ctx", "tp", None),
        P(("groups", "exp"), "ctx"),
        P(("groups", "exp"), ("ctx", "tp"), None),
        P("tp", "ctx"),
        P(),
        P(None, "exp"),
        P(("groups", "exp"), ("ctx", "tp"), None),
        P("groups"),
    )
    return jax.shard_map(
        on_device,
        mesh=mesh,
        in_specs=placed,
        out_specs=P(("groups", "ctx", "tp"), "exp", None, None),
        check_vma=False,
    )
```

```python
import functools
import math

import jax
import jax.numpy as jnp
from jax import lax
from jax.experimental import pallas as pl
from jax.experimental.pallas import tpu as pltpu
from jax.sharding import PartitionSpec as P

CAP = 2
EPSILON = 1e-05
DOC_ROWS = 16
VMEM_LIMIT = 12 * 1024 * 1024
VMEM_MOST = 61 * 1024 * 1024
VMEM_MUCH = 52 * 1024 * 1024


def fetch(refs, buffers, sems):
    copies = [
        pltpu.make_async_copy(ref, buffer, sems.at[number])
        for number, (ref, buffer) in enumerate(zip(refs, buffers))
    ]
    for copy in copies:
        copy.start()
    return [copy.wait for copy in copies]


def pack_kernel(groups, key_ref, value_ref, doc_ref, out_ref, *scratch):
    buffers, sems = scratch[:-1], scratch[-1]
    for wait in fetch((key_ref, value_ref, doc_ref), buffers, sems):
        wait()
    key_ref, value_ref, doc_ref = buffers
    rows, head_size = key_ref.shape
    tokens = rows // groups
    token = lax.broadcasted_iota(jnp.int32, (tokens, rows), 0)
    row = lax.broadcasted_iota(jnp.int32, (tokens, rows), 1)
    for group in range(groups):
        pick = (row == token * groups + group).astype(jnp.bfloat16)
        for place, ref in enumerate((key_ref, value_ref)):
            first = (place * groups + group) * tokens
            out_ref[first : first + tokens, :] = jnp.dot(
                pick, ref[...], preferred_element_type=jnp.float32
            ).astype(jnp.bfloat16)
    out_ref[2 * rows :, :] = jnp.broadcast_to(
        (doc_ref[...] + 1).astype(jnp.float32), (DOC_ROWS, tokens)
    ).astype(jnp.bfloat16)


def stage_kernel(count, *refs):
    for wait in fetch(refs[:count], refs[count:-1], refs[-1]):
        wait()


def attention_kernel(ratio, groups, pair, place_ref, query_ref, *refs):
    pack_refs, out_refs = refs[:-pair], refs[-pair:]
    heads, tokens, head_size = query_ref.shape
    scale = 1.0 / math.sqrt(head_size)
    core = place_ref[0]
    part_rows = tokens // pair
    held_rows = groups * tokens
    rows = lax.broadcasted_iota(jnp.int32, (tokens, tokens), 0)
    columns = lax.broadcasted_iota(jnp.int32, (tokens, tokens), 1)
    docs = [ref[2 * held_rows : 2 * held_rows + 1, :].astype(jnp.float32) for ref in pack_refs]
    own_doc = jnp.sum(jnp.where(rows == columns, docs[0], 0.0), axis=1, keepdims=True)
    allowed = [(own_doc == docs[0]) & (columns <= rows)] + [own_doc == doc for doc in docs[1:]]
    allowed = jnp.concatenate(allowed, axis=1)
    for group in range(groups):
        first = group * tokens
        keys = jnp.concatenate([ref[first : first + tokens, :] for ref in pack_refs], axis=0)
        first = held_rows + group * tokens
        held = jnp.concatenate([ref[first : first + tokens, :] for ref in pack_refs], axis=0)
        for head in range(group * ratio, (group + 1) * ratio):
            scores = lax.dot_general(
                query_ref[head], keys, (((1,), (1,)), ((), ())), preferred_element_type=jnp.float32
            )
            scores = jnp.where(allowed, scores * scale, -1e30)
            weights = jnp.exp(scores - jnp.max(scores, axis=1, keepdims=True))
            totals = jnp.sum(weights, axis=1, keepdims=True)
            mixed = jnp.dot(
                weights.astype(jnp.bfloat16), held, preferred_element_type=jnp.float32
            )
            mixed = (mixed / totals).astype(jnp.bfloat16)
            parts = [mixed[i * part_rows : (i + 1) * part_rows] for i in range(pair)]
            for turn in range(pair):
                piece = parts[turn]
                for own in range(1, pair):
                    piece = jnp.where(core == own, parts[(own + turn) % pair], piece)
                out_refs[turn][:, head * head_size : (head + 1) * head_size] = piece


def project_kernel(pair, *refs):
    block_refs, weight_refs, out_ref = refs[:pair], refs[pair : 2 * pair], refs[2 * pair]
    total = None
    for block_ref, weight_ref in zip(block_refs, weight_refs):
        product = jnp.dot(block_ref[...], weight_ref[...], preferred_element_type=jnp.float32)
        total = product if total is None else total + product
    out_ref[...] = total.astype(out_ref.dtype)


def columns_of(chunk_ref, step, spots, ctx_index):
    columns = chunk_ref.shape[1]
    first = 0 if spots == 1 else lax.rem(ctx_index + step, spots) * columns
    return pl.ds(pl.multiple_of(first, 128), columns)


def hidden_kernel(step, spots, place_ref, residual_ref, chunk_ref, out_ref):
    part = columns_of(chunk_ref, step, spots, place_ref[0])
    out_ref[...] = (
        residual_ref[:, part].astype(jnp.float32) + chunk_ref[...].astype(jnp.float32)
    ).astype(out_ref.dtype)


def collect_kernel(steps, spots, exp_count, place_ref, *refs):
    count = len(steps)
    chunk_refs, out_refs = refs[:-exp_count], refs[-exp_count:]
    for back, out_ref in enumerate(out_refs):
        for step, chunk_ref in zip(steps, chunk_refs[back * count : (back + 1) * count]):
            out_ref[:, columns_of(chunk_ref, step, spots, place_ref[0])] = chunk_ref[...]


def finish_kernel(steps, spots, back, exp_count, place_ref, *refs):
    count = len(steps)
    chunk_refs = refs[:count]
    hidden_ref, id_ref, keep_ref, gain_ref, router_ref = refs[count : count + 5]
    out_ref, total_ref, normed_ref, result_ref, out_sem = refs[-5:]
    rows, width = hidden_ref.shape
    experts = keep_ref.shape[1]
    here = router_ref.shape[0]
    ctx_index, exp_index = place_ref[0], place_ref[1]
    keep = keep_ref[...].astype(jnp.float32)
    upper = (
        lax.broadcasted_iota(jnp.int32, (rows, rows), 0)
        < lax.broadcasted_iota(jnp.int32, (rows, rows), 1)
    ).astype(jnp.bfloat16)
    total_ref[...] = hidden_ref[...].astype(jnp.float32)
    for step, chunk_ref in zip(steps, chunk_refs):
        part = columns_of(chunk_ref, step, spots, ctx_index)
        total_ref[:, part] = chunk_ref[...].astype(jnp.float32)
    hidden = total_ref[...]
    power = jnp.sum(hidden * hidden, axis=1, keepdims=True)
    factor = lax.rsqrt(power / width + EPSILON)
    normed_ref[...] = (hidden * factor * gain_ref[...].astype(jnp.float32)).astype(jnp.bfloat16)
    ids = id_ref[...]
    onehot = (ids == lax.broadcasted_iota(jnp.int32, (experts, rows), 0)).astype(jnp.float32)
    earlier = jnp.dot(onehot.astype(jnp.bfloat16), upper, preferred_element_type=jnp.float32)
    ranking = jnp.sum(onehot * earlier, axis=0, keepdims=True)
    limits = jnp.dot(
        keep.astype(jnp.bfloat16),
        onehot.astype(jnp.bfloat16),
        preferred_element_type=jnp.float32,
    )
    local = ids - exp_index * here
    logits = lax.dot_general(
        router_ref[...],
        normed_ref[...],
        (((1,), (1,)), ((), ())),
        preferred_element_type=jnp.float32,
    )
    chosen = local == lax.broadcasted_iota(jnp.int32, (here, rows), 0)
    gates = jax.nn.sigmoid(jnp.sum(jnp.where(chosen, logits, 0.0), axis=0, keepdims=True))
    target = local * CAP + ranking.astype(jnp.int32)
    target = jnp.where((ranking < limits) & (local >= 0) & (local < here), target, -1)
    table = lax.broadcasted_iota(jnp.int32, (here * CAP, rows), 0) == target
    slot_gates = jnp.sum(jnp.where(table, gates, 0.0), axis=1, keepdims=True)
    slots = jnp.dot(
        table.astype(jnp.bfloat16), normed_ref[...], preferred_element_type=jnp.float32
    )
    result_ref[...] = (slots * slot_gates).astype(jnp.bfloat16).reshape(result_ref.shape)
    source = lax.rem(exp_index - back + exp_count, exp_count)
    copy = pltpu.make_async_copy(result_ref, out_ref.at[source], out_sem)
    copy.start()
    copy.wait()


def on_device(
    queries,
    key_states,
    values,
    doc_ids,
    residual,
    out_proj,
    norm_gain,
    router,
    expert_ids,
    keep_counts,
):
    _, tokens, heads, head_size = queries.shape
    groups = key_states.shape[2]
    ctx_count = lax.axis_size("ctx")
    pair = lax.axis_size("tp")
    exp_count = lax.axis_size("exp")
    part_rows = tokens // pair
    width = residual.shape[2]
    columns = out_proj.shape[1]
    experts_here = router.shape[1]
    ctx_index = lax.axis_index("ctx")
    core = lax.axis_index("tp")
    exp_index = lax.axis_index("exp")
    reach = -(-(ctx_count * tokens // 2 - 1) // tokens)
    vmem = pl.BlockSpec(memory_space=pltpu.VMEM)
    smem = pl.BlockSpec(memory_space=pltpu.SMEM)
    anywhere = pl.BlockSpec(memory_space=pl.ANY)
    params = pltpu.CompilerParams(vmem_limit_bytes=VMEM_LIMIT)
    most = pltpu.CompilerParams(vmem_limit_bytes=VMEM_MOST)
    much = pltpu.CompilerParams(vmem_limit_bytes=VMEM_MUCH)
    bf16, f32 = jnp.bfloat16, jnp.float32

    def over(array, axis, step):
        count = lax.axis_size(axis)
        if step % count == 0:
            return array
        return lax.ppermute(array, axis, [(i, (i + step) % count) for i in range(count)])

    def along(array, moves):
        return lax.ppermute(array, "ctx", moves)

    pack = pl.pallas_call(
        functools.partial(pack_kernel, groups),
        out_shape=jax.ShapeDtypeStruct((2 * groups * tokens + DOC_ROWS, head_size), bf16),
        in_specs=[anywhere] * 3,
        out_specs=vmem,
        scratch_shapes=[pltpu.VMEM((groups * tokens, head_size), bf16)] * 2
        + [pltpu.VMEM(doc_ids.shape, doc_ids.dtype), pltpu.SemaphoreType.DMA((3,))],
        compiler_params=most,
    )(
        key_states.reshape(groups * tokens, head_size),
        values.reshape(groups * tokens, head_size),
        doc_ids,
    )
    packs = [pack] + [
        lax.ppermute(pack, "ctx", [(i, i + step) for i in range(ctx_count - step)])
        for step in range(1, reach + 1)
    ]
    ids, own_residual = expert_ids[:, :, 0], residual[0]
    weights = [over(out_proj, "tp", turn) for turn in range(pair)]
    pack, own_queries = lax.optimization_barrier((pack, queries[0].transpose(1, 0, 2)))
    staged_queries, packs[0] = pl.pallas_call(
        functools.partial(stage_kernel, 2),
        out_shape=[
            jax.ShapeDtypeStruct(own_queries.shape, bf16),
            jax.ShapeDtypeStruct(pack.shape, bf16),
        ],
        in_specs=[anywhere] * 2,
        out_specs=[vmem] * 2,
        scratch_shapes=[pltpu.SemaphoreType.DMA((2,))],
        compiler_params=much,
    )(own_queries, pack)
    all_ids = [ids] + [over(ids, "exp", back) for back in range(1, exp_count)]
    staged_queries, all_ids = lax.optimization_barrier((staged_queries, all_ids))
    pieces = pl.pallas_call(
        functools.partial(attention_kernel, heads // groups, groups, pair),
        out_shape=[jax.ShapeDtypeStruct((part_rows, heads * head_size), bf16)] * pair,
        in_specs=[smem] + [vmem] * (1 + len(packs)),
        out_specs=[vmem] * pair,
        compiler_params=params,
    )(core.reshape(1), staged_queries, *packs)

    project = pl.pallas_call(
        functools.partial(project_kernel, pair),
        out_shape=jax.ShapeDtypeStruct((part_rows, columns), bf16),
        in_specs=[vmem] * (2 * pair),
        out_specs=vmem,
        compiler_params=params,
        cost_estimate=pl.CostEstimate(
            flops=2 * pair * part_rows * out_proj.size,
            bytes_accessed=2 * pair * out_proj.size,
            transcendentals=0,
        ),
    )
    block = [over(pieces[turn], "tp", turn) for turn in range(pair)]
    block[-1], weights = lax.optimization_barrier((block[-1], weights))
    weights = pl.pallas_call(
        functools.partial(stage_kernel, pair),
        out_shape=[jax.ShapeDtypeStruct(out_proj.shape, bf16)] * pair,
        in_specs=[anywhere] * pair,
        out_specs=[vmem] * pair,
        scratch_shapes=[pltpu.SemaphoreType.DMA((pair,))],
        compiler_params=params,
    )(*weights)

    aligned = columns % 128 == 0
    hidden = None

    def forward(chunk, step, spots):
        hidden = pl.pallas_call(
            functools.partial(hidden_kernel, step, spots),
            out_shape=jax.ShapeDtypeStruct(chunk.shape, bf16),
            in_specs=[smem] + [vmem] * 2,
            out_specs=vmem,
            compiler_params=params,
        )(ctx_index.reshape(1), own_residual, chunk)
        return [over(hidden, "exp", back) for back in range(exp_count)]

    def collect(steps, spots):
        arrays = [flat[step][back] for back in range(exp_count) for step in steps]
        return pl.pallas_call(
            functools.partial(collect_kernel, steps, spots, exp_count),
            out_shape=[jax.ShapeDtypeStruct((part_rows, width), bf16)] * exp_count,
            in_specs=[smem] + [vmem] * len(arrays),
            out_specs=[vmem] * exp_count,
            compiler_params=params,
        )(ctx_index.reshape(1), *arrays)

    chunks, flat = [], []
    late_from = max(1, ctx_count - 2)
    for step in range(ctx_count):
        last = step == ctx_count - 1
        following = None if last else [over(array, "ctx", 1) for array in block]
        if step == 2:
            block, chunks[1] = lax.optimization_barrier((block, chunks[1]))
        if step == 3 and aligned:
            block, flat[0] = lax.optimization_barrier((block, flat[0]))
        if last and aligned:
            hidden = collect(list(range(late_from)), ctx_count)
        total = project(*block, *weights)
        chunk = over(total, "ctx", ctx_count - step)
        if not last:
            block = [lax.optimization_barrier((array, total))[0] for array in following]
        if last and aligned:
            chunk, hidden = lax.optimization_barrier((chunk, hidden))
        chunks.append(chunk)
        if aligned:
            if step in (1, 2) and not last:
                first, _ = lax.optimization_barrier((chunks[step - 1], [total] + following[:1]))
                flat[step - 1] = forward(first, step - 1, ctx_count)
            flat.append(forward(chunk, step, ctx_count) if step > 1 or last else None)
    if aligned:
        late_steps, spots = list(range(late_from, ctx_count)), ctx_count
    else:
        whole = jnp.roll(jnp.stack(chunks), ctx_index, axis=0)
        whole = whole.transpose(1, 0, 2).reshape(part_rows, width)
        flat.append(forward(whole, 0, 1))
        hidden = collect([0], 1)
        late_steps, spots = [], 1
    places = jnp.stack([ctx_index, exp_index])
    out = None
    for back in range(exp_count):
        operands = (
            [places]
            + [flat[step][back] for step in late_steps]
            + [hidden[back], all_ids[back], keep_counts.reshape(1, -1)]
            + [norm_gain.reshape(1, -1), router.T]
        )
        kept = [] if out is None else [out]
        out = pl.pallas_call(
            functools.partial(finish_kernel, late_steps, spots, back, exp_count),
            out_shape=jax.ShapeDtypeStruct((exp_count, experts_here, CAP, width), bf16),
            in_specs=[smem] + [vmem] * (len(operands) - 1) + [anywhere] * len(kept),
            out_specs=anywhere,
            scratch_shapes=[
                pltpu.VMEM((part_rows, width), f32),
                pltpu.VMEM((part_rows, width), bf16),
                pltpu.VMEM((experts_here, CAP, width), bf16),
                pltpu.SemaphoreType.DMA,
            ],
            input_output_aliases={len(operands): 0} if kept else {},
            compiler_params=params,
        )(*operands, *kept)
    return out


def solution(mesh):
    placed = (
        P(("groups", "exp"), "ctx", "tp", None),
        P(("groups", "exp"), "ctx", "tp", None),
        P(("groups", "exp"), "ctx", "tp", None),
        P(("groups", "exp"), "ctx"),
        P(("groups", "exp"), ("ctx", "tp"), None),
        P("tp", "ctx"),
        P(),
        P(None, "exp"),
        P(("groups", "exp"), ("ctx", "tp"), None),
        P("groups"),
    )
    return jax.shard_map(
        on_device,
        mesh=mesh,
        in_specs=placed,
        out_specs=P(("groups", "ctx", "tp"), "exp", None, None),
        check_vma=False,
    )
```

```python
import functools
import math

import jax
import jax.numpy as jnp
from jax import lax
from jax.experimental import pallas as pl
from jax.experimental.pallas import tpu as pltpu
from jax.sharding import PartitionSpec as P

CAP = 2
EPSILON = 1e-05
DOC_ROWS = 16
VMEM_LIMIT = 12 * 1024 * 1024
VMEM_MOST = 61 * 1024 * 1024
VMEM_MUCH = 52 * 1024 * 1024


def fetch(refs, buffers, sems):
    copies = [
        pltpu.make_async_copy(ref, buffer, sems.at[number])
        for number, (ref, buffer) in enumerate(zip(refs, buffers))
    ]
    for copy in copies:
        copy.start()
    return [copy.wait for copy in copies]


def pack_kernel(groups, key_ref, value_ref, doc_ref, out_ref, *scratch):
    buffers, sems = scratch[:-1], scratch[-1]
    for wait in fetch((key_ref, value_ref, doc_ref), buffers, sems):
        wait()
    key_ref, value_ref, doc_ref = buffers
    rows, head_size = key_ref.shape
    tokens = rows // groups
    token = lax.broadcasted_iota(jnp.int32, (tokens, rows), 0)
    row = lax.broadcasted_iota(jnp.int32, (tokens, rows), 1)
    for group in range(groups):
        pick = (row == token * groups + group).astype(jnp.bfloat16)
        for place, ref in enumerate((key_ref, value_ref)):
            first = (place * groups + group) * tokens
            out_ref[first : first + tokens, :] = jnp.dot(
                pick, ref[...], preferred_element_type=jnp.float32
            ).astype(jnp.bfloat16)
    out_ref[2 * rows :, :] = jnp.broadcast_to(
        (doc_ref[...] + 1).astype(jnp.float32), (DOC_ROWS, tokens)
    ).astype(jnp.bfloat16)


def stage_kernel(count, *refs):
    for wait in fetch(refs[:count], refs[count:-1], refs[-1]):
        wait()


def attention_kernel(ratio, groups, pair, place_ref, query_ref, *refs):
    pack_refs, out_refs = refs[:-pair], refs[-pair:]
    heads, tokens, head_size = query_ref.shape
    scale = 1.0 / math.sqrt(head_size)
    core, ctx_index = place_ref[0], place_ref[1]
    part_rows = tokens // pair
    held_rows = groups * tokens
    rows = lax.broadcasted_iota(jnp.int32, (tokens, tokens), 0)
    columns = lax.broadcasted_iota(jnp.int32, (tokens, tokens), 1)
    docs = [ref[2 * held_rows : 2 * held_rows + 1, :].astype(jnp.float32) for ref in pack_refs]
    own_doc = jnp.sum(jnp.where(rows == columns, docs[0], 0.0), axis=1, keepdims=True)
    allowed = [(own_doc == docs[0]) & (columns <= rows)]
    for step, doc in enumerate(docs[1:], 1):
        allowed.append((own_doc == doc) & (ctx_index >= step))
    allowed = jnp.concatenate(allowed, axis=1)
    for group in range(groups):
        first = group * tokens
        keys = jnp.concatenate([ref[first : first + tokens, :] for ref in pack_refs], axis=0)
        first = held_rows + group * tokens
        held = jnp.concatenate([ref[first : first + tokens, :] for ref in pack_refs], axis=0)
        for head in range(group * ratio, (group + 1) * ratio):
            scores = lax.dot_general(
                query_ref[head], keys, (((1,), (1,)), ((), ())), preferred_element_type=jnp.float32
            )
            scores = jnp.where(allowed, scores * scale, -1e30)
            weights = jnp.exp(scores - jnp.max(scores, axis=1, keepdims=True))
            totals = jnp.sum(weights, axis=1, keepdims=True)
            mixed = jnp.dot(
                weights.astype(jnp.bfloat16), held, preferred_element_type=jnp.float32
            )
            mixed = (mixed / totals).astype(jnp.bfloat16)
            parts = [mixed[i * part_rows : (i + 1) * part_rows] for i in range(pair)]
            for turn in range(pair):
                piece = parts[turn]
                for own in range(1, pair):
                    piece = jnp.where(core == own, parts[(own + turn) % pair], piece)
                out_refs[turn][:, head * head_size : (head + 1) * head_size] = piece


def project_kernel(pair, *refs):
    block_refs, weight_refs, out_ref = refs[:pair], refs[pair : 2 * pair], refs[2 * pair]
    total = None
    for block_ref, weight_ref in zip(block_refs, weight_refs):
        product = jnp.dot(block_ref[...], weight_ref[...], preferred_element_type=jnp.float32)
        total = product if total is None else total + product
    out_ref[...] = total.astype(out_ref.dtype)


def columns_of(chunk_ref, step, spots, ctx_index):
    columns = chunk_ref.shape[1]
    first = 0 if spots == 1 else lax.rem(ctx_index + step, spots) * columns
    return pl.ds(pl.multiple_of(first, 128), columns)


def hidden_kernel(step, spots, place_ref, residual_ref, chunk_ref, out_ref):
    part = columns_of(chunk_ref, step, spots, place_ref[0])
    out_ref[...] = (
        residual_ref[:, part].astype(jnp.float32) + chunk_ref[...].astype(jnp.float32)
    ).astype(out_ref.dtype)


def collect_kernel(steps, spots, exp_count, place_ref, *refs):
    count = len(steps)
    chunk_refs, out_refs = refs[:-exp_count], refs[-exp_count:]
    for back, out_ref in enumerate(out_refs):
        for step, chunk_ref in zip(steps, chunk_refs[back * count : (back + 1) * count]):
            out_ref[:, columns_of(chunk_ref, step, spots, place_ref[0])] = chunk_ref[...]


def finish_kernel(steps, spots, back, exp_count, place_ref, *refs):
    count = len(steps)
    chunk_refs = refs[:count]
    hidden_ref, id_ref, keep_ref, gain_ref, router_ref = refs[count : count + 5]
    out_ref, total_ref, normed_ref, result_ref, out_sem = refs[-5:]
    rows, width = hidden_ref.shape
    experts = keep_ref.shape[1]
    here = router_ref.shape[0]
    ctx_index, exp_index = place_ref[0], place_ref[1]
    keep = keep_ref[...].astype(jnp.float32)
    upper = (
        lax.broadcasted_iota(jnp.int32, (rows, rows), 0)
        < lax.broadcasted_iota(jnp.int32, (rows, rows), 1)
    ).astype(jnp.bfloat16)
    total_ref[...] = hidden_ref[...].astype(jnp.float32)
    for step, chunk_ref in zip(steps, chunk_refs):
        part = columns_of(chunk_ref, step, spots, ctx_index)
        total_ref[:, part] = chunk_ref[...].astype(jnp.float32)
    hidden = total_ref[...]
    power = jnp.sum(hidden * hidden, axis=1, keepdims=True)
    factor = lax.rsqrt(power / width + EPSILON)
    normed_ref[...] = (hidden * factor * gain_ref[...].astype(jnp.float32)).astype(jnp.bfloat16)
    ids = id_ref[...]
    onehot = (ids == lax.broadcasted_iota(jnp.int32, (experts, rows), 0)).astype(jnp.float32)
    earlier = jnp.dot(onehot.astype(jnp.bfloat16), upper, preferred_element_type=jnp.float32)
    ranking = jnp.sum(onehot * earlier, axis=0, keepdims=True)
    limits = jnp.dot(
        keep.astype(jnp.bfloat16),
        onehot.astype(jnp.bfloat16),
        preferred_element_type=jnp.float32,
    )
    local = ids - exp_index * here
    logits = lax.dot_general(
        router_ref[...],
        normed_ref[...],
        (((1,), (1,)), ((), ())),
        preferred_element_type=jnp.float32,
    )
    chosen = local == lax.broadcasted_iota(jnp.int32, (here, rows), 0)
    gates = jax.nn.sigmoid(jnp.sum(jnp.where(chosen, logits, 0.0), axis=0, keepdims=True))
    target = local * CAP + ranking.astype(jnp.int32)
    target = jnp.where((ranking < limits) & (local >= 0) & (local < here), target, -1)
    table = lax.broadcasted_iota(jnp.int32, (here * CAP, rows), 0) == target
    slot_gates = jnp.sum(jnp.where(table, gates, 0.0), axis=1, keepdims=True)
    slots = jnp.dot(
        table.astype(jnp.bfloat16), normed_ref[...], preferred_element_type=jnp.float32
    )
    result_ref[...] = (slots * slot_gates).astype(jnp.bfloat16).reshape(result_ref.shape)
    source = lax.rem(exp_index - back + exp_count, exp_count)
    copy = pltpu.make_async_copy(result_ref, out_ref.at[source], out_sem)
    copy.start()
    copy.wait()


def on_device(
    queries,
    key_states,
    values,
    doc_ids,
    residual,
    out_proj,
    norm_gain,
    router,
    expert_ids,
    keep_counts,
):
    _, tokens, heads, head_size = queries.shape
    groups = key_states.shape[2]
    ctx_count = lax.axis_size("ctx")
    pair = lax.axis_size("tp")
    exp_count = lax.axis_size("exp")
    part_rows = tokens // pair
    width = residual.shape[2]
    columns = out_proj.shape[1]
    experts_here = router.shape[1]
    ctx_index = lax.axis_index("ctx")
    core = lax.axis_index("tp")
    exp_index = lax.axis_index("exp")
    reach = -(-(ctx_count * tokens // 2 - 1) // tokens)
    vmem = pl.BlockSpec(memory_space=pltpu.VMEM)
    smem = pl.BlockSpec(memory_space=pltpu.SMEM)
    anywhere = pl.BlockSpec(memory_space=pl.ANY)
    params = pltpu.CompilerParams(vmem_limit_bytes=VMEM_LIMIT)
    most = pltpu.CompilerParams(vmem_limit_bytes=VMEM_MOST)
    much = pltpu.CompilerParams(vmem_limit_bytes=VMEM_MUCH)
    bf16, f32 = jnp.bfloat16, jnp.float32

    def over(array, axis, step):
        count = lax.axis_size(axis)
        if step % count == 0:
            return array
        return lax.ppermute(array, axis, [(i, (i + step) % count) for i in range(count)])

    def along(array, moves):
        return lax.ppermute(array, "ctx", moves)

    pack = pl.pallas_call(
        functools.partial(pack_kernel, groups),
        out_shape=jax.ShapeDtypeStruct((2 * groups * tokens + DOC_ROWS, head_size), bf16),
        in_specs=[anywhere] * 3,
        out_specs=vmem,
        scratch_shapes=[pltpu.VMEM((groups * tokens, head_size), bf16)] * 2
        + [pltpu.VMEM(doc_ids.shape, doc_ids.dtype), pltpu.SemaphoreType.DMA((3,))],
        compiler_params=most,
    )(
        key_states.reshape(groups * tokens, head_size),
        values.reshape(groups * tokens, head_size),
        doc_ids,
    )
    packs = [pack] + [
        lax.ppermute(
            pack,
            "ctx",
            [
                (i, (i + step) % ctx_count)
                for i in range(ctx_count if step == 1 else ctx_count - step)
            ],
        )
        for step in range(1, reach + 1)
    ]
    ids, own_residual = expert_ids[:, :, 0], residual[0]
    weights = [over(out_proj, "tp", turn) for turn in range(pair)]
    pack, own_queries = lax.optimization_barrier((pack, queries[0].transpose(1, 0, 2)))
    staged_queries, packs[0] = pl.pallas_call(
        functools.partial(stage_kernel, 2),
        out_shape=[
            jax.ShapeDtypeStruct(own_queries.shape, bf16),
            jax.ShapeDtypeStruct(pack.shape, bf16),
        ],
        in_specs=[anywhere] * 2,
        out_specs=[vmem] * 2,
        scratch_shapes=[pltpu.SemaphoreType.DMA((2,))],
        compiler_params=much,
    )(own_queries, pack)
    all_ids = [ids] + [over(ids, "exp", back) for back in range(1, exp_count)]
    staged_queries, all_ids = lax.optimization_barrier((staged_queries, all_ids))
    pieces = pl.pallas_call(
        functools.partial(attention_kernel, heads // groups, groups, pair),
        out_shape=[jax.ShapeDtypeStruct((part_rows, heads * head_size), bf16)] * pair,
        in_specs=[smem] + [vmem] * (1 + len(packs)),
        out_specs=[vmem] * pair,
        compiler_params=params,
    )(jnp.stack([core, ctx_index]), staged_queries, *packs)

    project = pl.pallas_call(
        functools.partial(project_kernel, pair),
        out_shape=jax.ShapeDtypeStruct((part_rows, columns), bf16),
        in_specs=[vmem] * (2 * pair),
        out_specs=vmem,
        compiler_params=params,
        cost_estimate=pl.CostEstimate(
            flops=2 * pair * part_rows * out_proj.size,
            bytes_accessed=2 * pair * out_proj.size,
            transcendentals=0,
        ),
    )
    block = [over(pieces[turn], "tp", turn) for turn in range(pair)]
    block[-1], weights = lax.optimization_barrier((block[-1], weights))
    weights = pl.pallas_call(
        functools.partial(stage_kernel, pair),
        out_shape=[jax.ShapeDtypeStruct(out_proj.shape, bf16)] * pair,
        in_specs=[anywhere] * pair,
        out_specs=[vmem] * pair,
        scratch_shapes=[pltpu.SemaphoreType.DMA((pair,))],
        compiler_params=params,
    )(*weights)

    aligned = columns % 128 == 0
    hidden = None

    def forward(chunk, step, spots):
        hidden = pl.pallas_call(
            functools.partial(hidden_kernel, step, spots),
            out_shape=jax.ShapeDtypeStruct(chunk.shape, bf16),
            in_specs=[smem] + [vmem] * 2,
            out_specs=vmem,
            compiler_params=params,
        )(ctx_index.reshape(1), own_residual, chunk)
        return [over(hidden, "exp", back) for back in range(exp_count)]

    def collect(steps, spots):
        arrays = [flat[step][back] for back in range(exp_count) for step in steps]
        return pl.pallas_call(
            functools.partial(collect_kernel, steps, spots, exp_count),
            out_shape=[jax.ShapeDtypeStruct((part_rows, width), bf16)] * exp_count,
            in_specs=[smem] + [vmem] * len(arrays),
            out_specs=[vmem] * exp_count,
            compiler_params=params,
        )(ctx_index.reshape(1), *arrays)

    chunks, flat = [], []
    late_from = max(1, ctx_count - 2)
    for step in range(ctx_count):
        last = step == ctx_count - 1
        following = None if last else [over(array, "ctx", 1) for array in block]
        if step == 2:
            block, chunks[1] = lax.optimization_barrier((block, chunks[1]))
        if step == 3 and aligned:
            block, flat[0] = lax.optimization_barrier((block, flat[0]))
        if last and aligned:
            hidden = collect(list(range(late_from)), ctx_count)
        total = project(*block, *weights)
        chunk = over(total, "ctx", ctx_count - step)
        if not last:
            block = [lax.optimization_barrier((array, total))[0] for array in following]
        if last and aligned:
            chunk, hidden = lax.optimization_barrier((chunk, hidden))
        chunks.append(chunk)
        if aligned:
            if step in (1, 2) and not last:
                first, _ = lax.optimization_barrier((chunks[step - 1], [total] + following[:1]))
                flat[step - 1] = forward(first, step - 1, ctx_count)
            flat.append(forward(chunk, step, ctx_count) if step > 1 or last else None)
    if aligned:
        late_steps, spots = list(range(late_from, ctx_count)), ctx_count
    else:
        whole = jnp.roll(jnp.stack(chunks), ctx_index, axis=0)
        whole = whole.transpose(1, 0, 2).reshape(part_rows, width)
        flat.append(forward(whole, 0, 1))
        hidden = collect([0], 1)
        late_steps, spots = [], 1
    places = jnp.stack([ctx_index, exp_index])
    out = None
    for back in range(exp_count):
        operands = (
            [places]
            + [flat[step][back] for step in late_steps]
            + [hidden[back], all_ids[back], keep_counts.reshape(1, -1)]
            + [norm_gain.reshape(1, -1), router.T]
        )
        kept = [] if out is None else [out]
        out = pl.pallas_call(
            functools.partial(finish_kernel, late_steps, spots, back, exp_count),
            out_shape=jax.ShapeDtypeStruct((exp_count, experts_here, CAP, width), bf16),
            in_specs=[smem] + [vmem] * (len(operands) - 1) + [anywhere] * len(kept),
            out_specs=anywhere,
            scratch_shapes=[
                pltpu.VMEM((part_rows, width), f32),
                pltpu.VMEM((part_rows, width), bf16),
                pltpu.VMEM((experts_here, CAP, width), bf16),
                pltpu.SemaphoreType.DMA,
            ],
            input_output_aliases={len(operands): 0} if kept else {},
            compiler_params=params,
        )(*operands, *kept)
    return out


def solution(mesh):
    placed = (
        P(("groups", "exp"), "ctx", "tp", None),
        P(("groups", "exp"), "ctx", "tp", None),
        P(("groups", "exp"), "ctx", "tp", None),
        P(("groups", "exp"), "ctx"),
        P(("groups", "exp"), ("ctx", "tp"), None),
        P("tp", "ctx"),
        P(),
        P(None, "exp"),
        P(("groups", "exp"), ("ctx", "tp"), None),
        P("groups"),
    )
    return jax.shard_map(
        on_device,
        mesh=mesh,
        in_specs=placed,
        out_specs=P(("groups", "ctx", "tp"), "exp", None, None),
        check_vma=False,
    )
```

```python
import functools
import math

import jax
import jax.numpy as jnp
from jax import lax
from jax.experimental import pallas as pl
from jax.experimental.pallas import tpu as pltpu
from jax.sharding import PartitionSpec as P

CAP = 2
EPSILON = 1e-05
DOC_ROWS = 16
VMEM_LIMIT = 12 * 1024 * 1024
VMEM_MOST = 61 * 1024 * 1024
VMEM_MUCH = 52 * 1024 * 1024


def fetch(refs, buffers, sems):
    copies = [
        pltpu.make_async_copy(ref, buffer, sems.at[number])
        for number, (ref, buffer) in enumerate(zip(refs, buffers))
    ]
    for copy in copies:
        copy.start()
    return [copy.wait for copy in copies]


def pack_kernel(groups, key_ref, value_ref, doc_ref, out_ref, *scratch):
    buffers, sems = scratch[:-1], scratch[-1]
    for wait in fetch((key_ref, value_ref, doc_ref), buffers, sems):
        wait()
    key_ref, value_ref, doc_ref = buffers
    rows, head_size = key_ref.shape
    tokens = rows // groups
    token = lax.broadcasted_iota(jnp.int32, (tokens, rows), 0)
    row = lax.broadcasted_iota(jnp.int32, (tokens, rows), 1)
    for group in range(groups):
        pick = (row == token * groups + group).astype(jnp.bfloat16)
        for place, ref in enumerate((key_ref, value_ref)):
            first = (place * groups + group) * tokens
            out_ref[first : first + tokens, :] = jnp.dot(
                pick, ref[...], preferred_element_type=jnp.float32
            ).astype(jnp.bfloat16)
    out_ref[2 * rows :, :] = jnp.broadcast_to(
        (doc_ref[...] + 1).astype(jnp.float32), (DOC_ROWS, tokens)
    ).astype(jnp.bfloat16)


def stage_kernel(count, *refs):
    for wait in fetch(refs[:count], refs[count:-1], refs[-1]):
        wait()


def attention_kernel(ratio, groups, pair, place_ref, query_ref, *refs):
    pack_refs, out_refs = refs[:-pair], refs[-pair:]
    heads, tokens, head_size = query_ref.shape
    scale = 1.0 / math.sqrt(head_size)
    core, ctx_index = place_ref[0], place_ref[1]
    part_rows = tokens // pair
    held_rows = groups * tokens
    rows = lax.broadcasted_iota(jnp.int32, (tokens, tokens), 0)
    columns = lax.broadcasted_iota(jnp.int32, (tokens, tokens), 1)
    docs = [ref[2 * held_rows : 2 * held_rows + 1, :].astype(jnp.float32) for ref in pack_refs]
    own_doc = jnp.sum(jnp.where(rows == columns, docs[0], 0.0), axis=1, keepdims=True)
    allowed = [(own_doc == docs[0]) & (columns <= rows)]
    for step, doc in enumerate(docs[1:], 1):
        allowed.append((own_doc == doc) & (ctx_index >= step))
    allowed = jnp.concatenate(allowed, axis=1)
    for group in range(groups):
        first = group * tokens
        keys = jnp.concatenate([ref[first : first + tokens, :] for ref in pack_refs], axis=0)
        first = held_rows + group * tokens
        held = jnp.concatenate([ref[first : first + tokens, :] for ref in pack_refs], axis=0)
        for head in range(group * ratio, (group + 1) * ratio):
            scores = lax.dot_general(
                query_ref[head], keys, (((1,), (1,)), ((), ())), preferred_element_type=jnp.float32
            )
            scores = jnp.where(allowed, scores * scale, -1e30)
            weights = jnp.exp(scores - jnp.max(scores, axis=1, keepdims=True))
            totals = jnp.sum(weights, axis=1, keepdims=True)
            mixed = jnp.dot(
                weights.astype(jnp.bfloat16), held, preferred_element_type=jnp.float32
            )
            mixed = (mixed / totals).astype(jnp.bfloat16)
            parts = [mixed[i * part_rows : (i + 1) * part_rows] for i in range(pair)]
            for turn in range(pair):
                piece = parts[turn]
                for own in range(1, pair):
                    piece = jnp.where(core == own, parts[(own + turn) % pair], piece)
                out_refs[turn][:, head * head_size : (head + 1) * head_size] = piece


def project_kernel(pair, *refs):
    block_refs, weight_refs, out_ref = refs[:pair], refs[pair : 2 * pair], refs[2 * pair]
    total = None
    for block_ref, weight_ref in zip(block_refs, weight_refs):
        product = jnp.dot(block_ref[...], weight_ref[...], preferred_element_type=jnp.float32)
        total = product if total is None else total + product
    out_ref[...] = total.astype(out_ref.dtype)


def columns_of(chunk_ref, step, spots, ctx_index):
    columns = chunk_ref.shape[1]
    first = 0 if spots == 1 else lax.rem(ctx_index + step, spots) * columns
    return pl.ds(pl.multiple_of(first, 128), columns)


def hidden_kernel(step, spots, place_ref, residual_ref, chunk_ref, out_ref):
    part = columns_of(chunk_ref, step, spots, place_ref[0])
    out_ref[...] = (
        residual_ref[:, part].astype(jnp.float32) + chunk_ref[...].astype(jnp.float32)
    ).astype(out_ref.dtype)


def collect_kernel(steps, spots, exp_count, place_ref, *refs):
    count = len(steps)
    chunk_refs, out_refs = refs[:-exp_count], refs[-exp_count:]
    for back, out_ref in enumerate(out_refs):
        for step, chunk_ref in zip(steps, chunk_refs[back * count : (back + 1) * count]):
            out_ref[:, columns_of(chunk_ref, step, spots, place_ref[0])] = chunk_ref[...]


def finish_kernel(steps, spots, back, exp_count, place_ref, *refs):
    count = len(steps)
    chunk_refs = refs[:count]
    hidden_ref, id_ref, keep_ref, gain_ref, router_ref = refs[count : count + 5]
    out_ref, total_ref, normed_ref, result_ref, out_sem = refs[-5:]
    rows, width = hidden_ref.shape
    experts = keep_ref.shape[1]
    here = router_ref.shape[0]
    ctx_index, exp_index = place_ref[0], place_ref[1]
    keep = keep_ref[...].astype(jnp.float32)
    upper = (
        lax.broadcasted_iota(jnp.int32, (rows, rows), 0)
        < lax.broadcasted_iota(jnp.int32, (rows, rows), 1)
    ).astype(jnp.bfloat16)
    total_ref[...] = hidden_ref[...]
    for step, chunk_ref in zip(steps, chunk_refs):
        total_ref[:, columns_of(chunk_ref, step, spots, ctx_index)] = chunk_ref[...]
    pieces = out_sem.shape[0]
    piece = width // pieces
    parts = [slice(number * piece, (number + 1) * piece) for number in range(pieces)]
    power = jnp.zeros((rows, 1), jnp.float32)
    for part in parts:
        hidden = total_ref[:, part].astype(jnp.float32)
        power = power + jnp.sum(hidden * hidden, axis=1, keepdims=True)
    factor = lax.rsqrt(power / width + EPSILON)
    for part in parts:
        gain = gain_ref[:, part].astype(jnp.float32)
        hidden = total_ref[:, part].astype(jnp.float32)
        normed_ref[:, part] = (hidden * factor * gain).astype(jnp.bfloat16)
    ids = id_ref[...]
    onehot = (ids == lax.broadcasted_iota(jnp.int32, (experts, rows), 0)).astype(jnp.float32)
    earlier = jnp.dot(onehot.astype(jnp.bfloat16), upper, preferred_element_type=jnp.float32)
    ranking = jnp.sum(onehot * earlier, axis=0, keepdims=True)
    limits = jnp.dot(
        keep.astype(jnp.bfloat16),
        onehot.astype(jnp.bfloat16),
        preferred_element_type=jnp.float32,
    )
    local = ids - exp_index * here
    logits = lax.dot_general(
        router_ref[...],
        normed_ref[...],
        (((1,), (1,)), ((), ())),
        preferred_element_type=jnp.float32,
    )
    chosen = local == lax.broadcasted_iota(jnp.int32, (here, rows), 0)
    gates = jax.nn.sigmoid(jnp.sum(jnp.where(chosen, logits, 0.0), axis=0, keepdims=True))
    target = local * CAP + ranking.astype(jnp.int32)
    target = jnp.where((ranking < limits) & (local >= 0) & (local < here), target, -1)
    table = lax.broadcasted_iota(jnp.int32, (here * CAP, rows), 0) == target
    slot_gates = jnp.sum(jnp.where(table, gates, 0.0), axis=1, keepdims=True)
    table = table.astype(jnp.bfloat16)
    source = lax.rem(exp_index - back + exp_count, exp_count)
    copies = []
    for number, part in enumerate(parts):
        slots = jnp.dot(table, normed_ref[:, part], preferred_element_type=jnp.float32)
        result_ref[:, :, part] = (
            (slots * slot_gates).astype(jnp.bfloat16).reshape(here, CAP, piece)
        )
        copy = pltpu.make_async_copy(
            result_ref.at[:, :, part], out_ref.at[source, :, :, part], out_sem.at[number]
        )
        copy.start()
        copies.append(copy)
    for copy in copies:
        copy.wait()


def on_device(
    queries,
    key_states,
    values,
    doc_ids,
    residual,
    out_proj,
    norm_gain,
    router,
    expert_ids,
    keep_counts,
):
    _, tokens, heads, head_size = queries.shape
    groups = key_states.shape[2]
    ctx_count = lax.axis_size("ctx")
    pair = lax.axis_size("tp")
    exp_count = lax.axis_size("exp")
    part_rows = tokens // pair
    width = residual.shape[2]
    columns = out_proj.shape[1]
    experts_here = router.shape[1]
    ctx_index = lax.axis_index("ctx")
    core = lax.axis_index("tp")
    exp_index = lax.axis_index("exp")
    reach = -(-(ctx_count * tokens // 2 - 1) // tokens)
    vmem = pl.BlockSpec(memory_space=pltpu.VMEM)
    smem = pl.BlockSpec(memory_space=pltpu.SMEM)
    anywhere = pl.BlockSpec(memory_space=pl.ANY)
    params = pltpu.CompilerParams(vmem_limit_bytes=VMEM_LIMIT)
    most = pltpu.CompilerParams(vmem_limit_bytes=VMEM_MOST)
    much = pltpu.CompilerParams(vmem_limit_bytes=VMEM_MUCH)
    bf16, f32 = jnp.bfloat16, jnp.float32

    def over(array, axis, step):
        count = lax.axis_size(axis)
        if step % count == 0:
            return array
        return lax.ppermute(array, axis, [(i, (i + step) % count) for i in range(count)])

    def along(array, moves):
        return lax.ppermute(array, "ctx", moves)

    pack = pl.pallas_call(
        functools.partial(pack_kernel, groups),
        out_shape=jax.ShapeDtypeStruct((2 * groups * tokens + DOC_ROWS, head_size), bf16),
        in_specs=[anywhere] * 3,
        out_specs=vmem,
        scratch_shapes=[pltpu.VMEM((groups * tokens, head_size), bf16)] * 2
        + [pltpu.VMEM(doc_ids.shape, doc_ids.dtype), pltpu.SemaphoreType.DMA((3,))],
        compiler_params=most,
    )(
        key_states.reshape(groups * tokens, head_size),
        values.reshape(groups * tokens, head_size),
        doc_ids,
    )
    packs = [pack] + [
        lax.ppermute(
            pack,
            "ctx",
            [
                (i, (i + step) % ctx_count)
                for i in range(ctx_count if step == 1 else ctx_count - step)
            ],
        )
        for step in range(1, reach + 1)
    ]
    ids, own_residual = expert_ids[:, :, 0], residual[0]
    weights = [over(out_proj, "tp", turn) for turn in range(pair)]
    pack, own_queries = lax.optimization_barrier((pack, queries[0].transpose(1, 0, 2)))
    staged_queries, packs[0] = pl.pallas_call(
        functools.partial(stage_kernel, 2),
        out_shape=[
            jax.ShapeDtypeStruct(own_queries.shape, bf16),
            jax.ShapeDtypeStruct(pack.shape, bf16),
        ],
        in_specs=[anywhere] * 2,
        out_specs=[vmem] * 2,
        scratch_shapes=[pltpu.SemaphoreType.DMA((2,))],
        compiler_params=much,
    )(own_queries, pack)
    all_ids = [ids] + [over(ids, "exp", back) for back in range(1, exp_count)]
    staged_queries, all_ids = lax.optimization_barrier((staged_queries, all_ids))
    pieces = pl.pallas_call(
        functools.partial(attention_kernel, heads // groups, groups, pair),
        out_shape=[jax.ShapeDtypeStruct((part_rows, heads * head_size), bf16)] * pair,
        in_specs=[smem] + [vmem] * (1 + len(packs)),
        out_specs=[vmem] * pair,
        compiler_params=params,
    )(jnp.stack([core, ctx_index]), staged_queries, *packs)

    project = pl.pallas_call(
        functools.partial(project_kernel, pair),
        out_shape=jax.ShapeDtypeStruct((part_rows, columns), bf16),
        in_specs=[vmem] * (2 * pair),
        out_specs=vmem,
        compiler_params=params,
        cost_estimate=pl.CostEstimate(
            flops=2 * pair * part_rows * out_proj.size,
            bytes_accessed=2 * pair * out_proj.size,
            transcendentals=0,
        ),
    )
    block = [over(pieces[turn], "tp", turn) for turn in range(pair)]
    block[-1], weights = lax.optimization_barrier((block[-1], weights))
    weights = pl.pallas_call(
        functools.partial(stage_kernel, pair),
        out_shape=[jax.ShapeDtypeStruct(out_proj.shape, bf16)] * pair,
        in_specs=[anywhere] * pair,
        out_specs=[vmem] * pair,
        scratch_shapes=[pltpu.SemaphoreType.DMA((pair,))],
        compiler_params=params,
    )(*weights)

    aligned = columns % 128 == 0
    hidden = None

    def forward(chunk, step, spots):
        hidden = pl.pallas_call(
            functools.partial(hidden_kernel, step, spots),
            out_shape=jax.ShapeDtypeStruct(chunk.shape, bf16),
            in_specs=[smem] + [vmem] * 2,
            out_specs=vmem,
            compiler_params=params,
        )(ctx_index.reshape(1), own_residual, chunk)
        return [over(hidden, "exp", back) for back in range(exp_count)]

    def collect(steps, spots):
        arrays = [flat[step][back] for back in range(exp_count) for step in steps]
        return pl.pallas_call(
            functools.partial(collect_kernel, steps, spots, exp_count),
            out_shape=[jax.ShapeDtypeStruct((part_rows, width), bf16)] * exp_count,
            in_specs=[smem] + [vmem] * len(arrays),
            out_specs=[vmem] * exp_count,
            compiler_params=params,
        )(ctx_index.reshape(1), *arrays)

    chunks, flat = [], []
    late_from = max(1, ctx_count - 2)
    for step in range(ctx_count):
        last = step == ctx_count - 1
        following = None if last else [over(array, "ctx", 1) for array in block]
        if step == 2:
            block, chunks[1] = lax.optimization_barrier((block, chunks[1]))
        if step == 3 and aligned:
            block, flat[0] = lax.optimization_barrier((block, flat[0]))
        if last and aligned:
            hidden = collect(list(range(late_from)), ctx_count)
        total = project(*block, *weights)
        chunk = over(total, "ctx", ctx_count - step)
        if not last:
            block = [lax.optimization_barrier((array, total))[0] for array in following]
        if last and aligned:
            chunk, hidden = lax.optimization_barrier((chunk, hidden))
        chunks.append(chunk)
        if aligned:
            if step in (1, 2) and not last:
                first, _ = lax.optimization_barrier((chunks[step - 1], [total] + following[:1]))
                flat[step - 1] = forward(first, step - 1, ctx_count)
            flat.append(forward(chunk, step, ctx_count) if step > 1 or last else None)
    if aligned:
        late_steps, spots = list(range(late_from, ctx_count)), ctx_count
    else:
        whole = jnp.roll(jnp.stack(chunks), ctx_index, axis=0)
        whole = whole.transpose(1, 0, 2).reshape(part_rows, width)
        flat.append(forward(whole, 0, 1))
        hidden = collect([0], 1)
        late_steps, spots = [], 1
    places = jnp.stack([ctx_index, exp_index])
    out = None
    for back in range(exp_count):
        operands = (
            [places]
            + [flat[step][back] for step in late_steps]
            + [hidden[back], all_ids[back], keep_counts.reshape(1, -1)]
            + [norm_gain.reshape(1, -1), router.T]
        )
        kept = [] if out is None else [out]
        out = pl.pallas_call(
            functools.partial(finish_kernel, late_steps, spots, back, exp_count),
            out_shape=jax.ShapeDtypeStruct((exp_count, experts_here, CAP, width), bf16),
            in_specs=[smem] + [vmem] * (len(operands) - 1) + [anywhere] * len(kept),
            out_specs=anywhere,
            scratch_shapes=[
                pltpu.VMEM((part_rows, width), bf16),
                pltpu.VMEM((part_rows, width), bf16),
                pltpu.VMEM((experts_here, CAP, width), bf16),
                pltpu.SemaphoreType.DMA((5 if width % (5 * 128) == 0 else 1,)),
            ],
            input_output_aliases={len(operands): 0} if kept else {},
            compiler_params=params,
        )(*operands, *kept)
    return out


def solution(mesh):
    placed = (
        P(("groups", "exp"), "ctx", "tp", None),
        P(("groups", "exp"), "ctx", "tp", None),
        P(("groups", "exp"), "ctx", "tp", None),
        P(("groups", "exp"), "ctx"),
        P(("groups", "exp"), ("ctx", "tp"), None),
        P("tp", "ctx"),
        P(),
        P(None, "exp"),
        P(("groups", "exp"), ("ctx", "tp"), None),
        P("groups"),
    )
    return jax.shard_map(
        on_device,
        mesh=mesh,
        in_specs=placed,
        out_specs=P(("groups", "ctx", "tp"), "exp", None, None),
        check_vma=False,
    )
```

```python
import functools
import math

import jax
import jax.numpy as jnp
from jax import lax
from jax.experimental import pallas as pl
from jax.experimental.pallas import tpu as pltpu
from jax.sharding import PartitionSpec as P

CAP = 2
EPSILON = 1e-05
DOC_ROWS = 16
VMEM_LIMIT = 12 * 1024 * 1024
VMEM_ATTENTION = 16 * 1024 * 1024
VMEM_MOST = 61 * 1024 * 1024
VMEM_MUCH = 52 * 1024 * 1024


def fetch(refs, buffers, sems):
    copies = [
        pltpu.make_async_copy(ref, buffer, sems.at[number])
        for number, (ref, buffer) in enumerate(zip(refs, buffers))
    ]
    for copy in copies:
        copy.start()
    return [copy.wait for copy in copies]


def pack_kernel(groups, key_ref, value_ref, doc_ref, out_ref, *scratch):
    buffers, sems = scratch[:-1], scratch[-1]
    for wait in fetch((key_ref, value_ref, doc_ref), buffers, sems):
        wait()
    key_ref, value_ref, doc_ref = buffers
    rows, head_size = key_ref.shape
    tokens = rows // groups
    token = lax.broadcasted_iota(jnp.int32, (tokens, rows), 0)
    row = lax.broadcasted_iota(jnp.int32, (tokens, rows), 1)
    for group in range(groups):
        pick = (row == token * groups + group).astype(jnp.bfloat16)
        for place, ref in enumerate((key_ref, value_ref)):
            first = (place * groups + group) * tokens
            out_ref[first : first + tokens, :] = jnp.dot(
                pick, ref[...], preferred_element_type=jnp.float32
            ).astype(jnp.bfloat16)
    out_ref[2 * rows :, :] = jnp.broadcast_to(
        (doc_ref[...] + 1).astype(jnp.float32), (DOC_ROWS, tokens)
    ).astype(jnp.bfloat16)


def stage_kernel(count, *refs):
    for wait in fetch(refs[:count], refs[count:-1], refs[-1]):
        wait()


def attention_kernel(ratio, groups, pair, place_ref, query_ref, *refs):
    pack_refs, out_refs = refs[:-pair], refs[-pair:]
    heads, tokens, head_size = query_ref.shape
    scale = 1.0 / math.sqrt(head_size)
    core, ctx_index = place_ref[0], place_ref[1]
    part_rows = tokens // pair
    held_rows = groups * tokens
    rows = lax.broadcasted_iota(jnp.int32, (tokens, tokens), 0)
    columns = lax.broadcasted_iota(jnp.int32, (tokens, tokens), 1)
    docs = [ref[2 * held_rows : 2 * held_rows + 1, :].astype(jnp.float32) for ref in pack_refs]
    own_doc = jnp.sum(jnp.where(rows == columns, docs[0], 0.0), axis=1, keepdims=True)
    allowed = [(own_doc == docs[0]) & (columns <= rows)]
    for step, doc in enumerate(docs[1:], 1):
        allowed.append((own_doc == doc) & (ctx_index >= step))
    allowed = jnp.concatenate(allowed, axis=1)
    for group in range(groups):
        first = group * tokens
        keys = jnp.concatenate([ref[first : first + tokens, :] for ref in pack_refs], axis=0)
        first = held_rows + group * tokens
        held = jnp.concatenate([ref[first : first + tokens, :] for ref in pack_refs], axis=0)
        for head in range(group * ratio, (group + 1) * ratio):
            scores = lax.dot_general(
                query_ref[head], keys, (((1,), (1,)), ((), ())), preferred_element_type=jnp.float32
            )
            scores = jnp.where(allowed, scores * scale, -1e30)
            weights = jnp.exp(scores - jnp.max(scores, axis=1, keepdims=True))
            totals = jnp.sum(weights, axis=1, keepdims=True)
            mixed = jnp.dot(
                weights.astype(jnp.bfloat16), held, preferred_element_type=jnp.float32
            )
            mixed = (mixed / totals).astype(jnp.bfloat16)
            parts = [mixed[i * part_rows : (i + 1) * part_rows] for i in range(pair)]
            for turn in range(pair):
                piece = parts[turn]
                for own in range(1, pair):
                    piece = jnp.where(core == own, parts[(own + turn) % pair], piece)
                out_refs[turn][:, head * head_size : (head + 1) * head_size] = piece


def project_kernel(pair, *refs):
    block_refs, weight_refs, out_ref = refs[:pair], refs[pair : 2 * pair], refs[2 * pair]
    total = None
    for block_ref, weight_ref in zip(block_refs, weight_refs):
        product = jnp.dot(block_ref[...], weight_ref[...], preferred_element_type=jnp.float32)
        total = product if total is None else total + product
    out_ref[...] = total.astype(out_ref.dtype)


def columns_of(chunk_ref, step, spots, ctx_index):
    columns = chunk_ref.shape[1]
    first = 0 if spots == 1 else lax.rem(ctx_index + step, spots) * columns
    return pl.ds(pl.multiple_of(first, 128), columns)


def hidden_kernel(step, spots, place_ref, residual_ref, chunk_ref, out_ref):
    part = columns_of(chunk_ref, step, spots, place_ref[0])
    out_ref[...] = (
        residual_ref[:, part].astype(jnp.float32) + chunk_ref[...].astype(jnp.float32)
    ).astype(out_ref.dtype)


def collect_kernel(steps, spots, exp_count, place_ref, *refs):
    count = len(steps)
    chunk_refs, out_refs = refs[:-exp_count], refs[-exp_count:]
    for back, out_ref in enumerate(out_refs):
        for step, chunk_ref in zip(steps, chunk_refs[back * count : (back + 1) * count]):
            out_ref[:, columns_of(chunk_ref, step, spots, place_ref[0])] = chunk_ref[...]


def finish_kernel(steps, spots, back, exp_count, place_ref, *refs):
    count = len(steps)
    chunk_refs = refs[:count]
    hidden_ref, id_ref, keep_ref, gain_ref, router_ref = refs[count : count + 5]
    out_ref, total_ref, normed_ref, result_ref, out_sem = refs[-5:]
    rows, width = hidden_ref.shape
    experts = keep_ref.shape[1]
    here = router_ref.shape[0]
    ctx_index, exp_index = place_ref[0], place_ref[1]
    keep = keep_ref[...].astype(jnp.float32)
    upper = (
        lax.broadcasted_iota(jnp.int32, (rows, rows), 0)
        < lax.broadcasted_iota(jnp.int32, (rows, rows), 1)
    ).astype(jnp.bfloat16)
    total_ref[...] = hidden_ref[...].astype(jnp.float32)
    for step, chunk_ref in zip(steps, chunk_refs):
        part = columns_of(chunk_ref, step, spots, ctx_index)
        total_ref[:, part] = chunk_ref[...].astype(jnp.float32)
    hidden = total_ref[...]
    power = jnp.sum(hidden * hidden, axis=1, keepdims=True)
    factor = lax.rsqrt(power / width + EPSILON)
    normed_ref[...] = (hidden * factor * gain_ref[...].astype(jnp.float32)).astype(jnp.bfloat16)
    ids = id_ref[...]
    onehot = (ids == lax.broadcasted_iota(jnp.int32, (experts, rows), 0)).astype(jnp.float32)
    earlier = jnp.dot(onehot.astype(jnp.bfloat16), upper, preferred_element_type=jnp.float32)
    ranking = jnp.sum(onehot * earlier, axis=0, keepdims=True)
    limits = jnp.dot(
        keep.astype(jnp.bfloat16),
        onehot.astype(jnp.bfloat16),
        preferred_element_type=jnp.float32,
    )
    local = ids - exp_index * here
    logits = lax.dot_general(
        router_ref[...],
        normed_ref[...],
        (((1,), (1,)), ((), ())),
        preferred_element_type=jnp.float32,
    )
    chosen = local == lax.broadcasted_iota(jnp.int32, (here, rows), 0)
    gates = jax.nn.sigmoid(jnp.sum(jnp.where(chosen, logits, 0.0), axis=0, keepdims=True))
    target = local * CAP + ranking.astype(jnp.int32)
    target = jnp.where((ranking < limits) & (local >= 0) & (local < here), target, -1)
    table = lax.broadcasted_iota(jnp.int32, (here * CAP, rows), 0) == target
    slot_gates = jnp.sum(jnp.where(table, gates, 0.0), axis=1, keepdims=True)
    slots = jnp.dot(
        table.astype(jnp.bfloat16), normed_ref[...], preferred_element_type=jnp.float32
    )
    result_ref[...] = (slots * slot_gates).astype(jnp.bfloat16).reshape(result_ref.shape)
    source = lax.rem(exp_index - back + exp_count, exp_count)
    copy = pltpu.make_async_copy(result_ref, out_ref.at[source], out_sem)
    copy.start()
    copy.wait()


def on_device(
    queries,
    key_states,
    values,
    doc_ids,
    residual,
    out_proj,
    norm_gain,
    router,
    expert_ids,
    keep_counts,
):
    _, tokens, heads, head_size = queries.shape
    groups = key_states.shape[2]
    ctx_count = lax.axis_size("ctx")
    pair = lax.axis_size("tp")
    exp_count = lax.axis_size("exp")
    part_rows = tokens // pair
    width = residual.shape[2]
    columns = out_proj.shape[1]
    experts_here = router.shape[1]
    ctx_index = lax.axis_index("ctx")
    core = lax.axis_index("tp")
    exp_index = lax.axis_index("exp")
    reach = -(-(ctx_count * tokens // 2 - 1) // tokens)
    vmem = pl.BlockSpec(memory_space=pltpu.VMEM)
    smem = pl.BlockSpec(memory_space=pltpu.SMEM)
    anywhere = pl.BlockSpec(memory_space=pl.ANY)
    params = pltpu.CompilerParams(vmem_limit_bytes=VMEM_LIMIT)
    most = pltpu.CompilerParams(vmem_limit_bytes=VMEM_MOST)
    much = pltpu.CompilerParams(vmem_limit_bytes=VMEM_MUCH)
    bf16, f32 = jnp.bfloat16, jnp.float32

    def over(array, axis, step):
        count = lax.axis_size(axis)
        if step % count == 0:
            return array
        return lax.ppermute(array, axis, [(i, (i + step) % count) for i in range(count)])

    def along(array, moves):
        return lax.ppermute(array, "ctx", moves)

    pack = pl.pallas_call(
        functools.partial(pack_kernel, groups),
        out_shape=jax.ShapeDtypeStruct((2 * groups * tokens + DOC_ROWS, head_size), bf16),
        in_specs=[anywhere] * 3,
        out_specs=vmem,
        scratch_shapes=[pltpu.VMEM((groups * tokens, head_size), bf16)] * 2
        + [pltpu.VMEM(doc_ids.shape, doc_ids.dtype), pltpu.SemaphoreType.DMA((3,))],
        compiler_params=most,
    )(
        key_states.reshape(groups * tokens, head_size),
        values.reshape(groups * tokens, head_size),
        doc_ids,
    )
    packs = [pack] + [
        lax.ppermute(
            pack,
            "ctx",
            [
                (i, (i + step) % ctx_count)
                for i in range(ctx_count if step == 1 else ctx_count - step)
            ],
        )
        for step in range(1, reach + 1)
    ]
    ids, own_residual = expert_ids[:, :, 0], residual[0]
    weights = [over(out_proj, "tp", turn) for turn in range(pair)]
    pack, own_queries = lax.optimization_barrier((pack, queries[0].transpose(1, 0, 2)))
    staged_queries, packs[0] = pl.pallas_call(
        functools.partial(stage_kernel, 2),
        out_shape=[
            jax.ShapeDtypeStruct(own_queries.shape, bf16),
            jax.ShapeDtypeStruct(pack.shape, bf16),
        ],
        in_specs=[anywhere] * 2,
        out_specs=[vmem] * 2,
        scratch_shapes=[pltpu.SemaphoreType.DMA((2,))],
        compiler_params=much,
    )(own_queries, pack)
    all_ids = [ids] + [over(ids, "exp", back) for back in range(1, exp_count)]
    staged_queries, all_ids = lax.optimization_barrier((staged_queries, all_ids))
    pieces = pl.pallas_call(
        functools.partial(attention_kernel, heads // groups, groups, pair),
        out_shape=[jax.ShapeDtypeStruct((part_rows, heads * head_size), bf16)] * pair,
        in_specs=[smem] + [vmem] * (1 + len(packs)),
        out_specs=[vmem] * pair,
        compiler_params=pltpu.CompilerParams(vmem_limit_bytes=VMEM_ATTENTION),
    )(jnp.stack([core, ctx_index]), staged_queries, *packs)

    project = pl.pallas_call(
        functools.partial(project_kernel, pair),
        out_shape=jax.ShapeDtypeStruct((part_rows, columns), bf16),
        in_specs=[vmem] * (2 * pair),
        out_specs=vmem,
        compiler_params=params,
        cost_estimate=pl.CostEstimate(
            flops=2 * pair * part_rows * out_proj.size,
            bytes_accessed=2 * pair * out_proj.size,
            transcendentals=0,
        ),
    )
    block = [over(pieces[turn], "tp", turn) for turn in range(pair)]
    block[-1], weights = lax.optimization_barrier((block[-1], weights))
    weights = pl.pallas_call(
        functools.partial(stage_kernel, pair),
        out_shape=[jax.ShapeDtypeStruct(out_proj.shape, bf16)] * pair,
        in_specs=[anywhere] * pair,
        out_specs=[vmem] * pair,
        scratch_shapes=[pltpu.SemaphoreType.DMA((pair,))],
        compiler_params=params,
    )(*weights)

    aligned = columns % 128 == 0
    hidden = None

    def forward(chunk, step, spots):
        hidden = pl.pallas_call(
            functools.partial(hidden_kernel, step, spots),
            out_shape=jax.ShapeDtypeStruct(chunk.shape, bf16),
            in_specs=[smem] + [vmem] * 2,
            out_specs=vmem,
            compiler_params=params,
        )(ctx_index.reshape(1), own_residual, chunk)
        return [over(hidden, "exp", back) for back in range(exp_count)]

    def collect(steps, spots):
        arrays = [flat[step][back] for back in range(exp_count) for step in steps]
        return pl.pallas_call(
            functools.partial(collect_kernel, steps, spots, exp_count),
            out_shape=[jax.ShapeDtypeStruct((part_rows, width), bf16)] * exp_count,
            in_specs=[smem] + [vmem] * len(arrays),
            out_specs=[vmem] * exp_count,
            compiler_params=params,
        )(ctx_index.reshape(1), *arrays)

    chunks, flat = [], []
    late_from = max(1, ctx_count - 2)
    for step in range(ctx_count):
        last = step == ctx_count - 1
        following = None if last else [over(array, "ctx", 1) for array in block]
        if step == 2:
            block, chunks[1] = lax.optimization_barrier((block, chunks[1]))
        if step == 3 and aligned:
            block, flat[0] = lax.optimization_barrier((block, flat[0]))
        if last and aligned:
            hidden = collect(list(range(late_from)), ctx_count)
        total = project(*block, *weights)
        chunk = over(total, "ctx", ctx_count - step)
        if not last:
            block = [lax.optimization_barrier((array, total))[0] for array in following]
        if last and aligned:
            chunk, hidden = lax.optimization_barrier((chunk, hidden))
        chunks.append(chunk)
        if aligned:
            if step in (1, 2) and not last:
                first, _ = lax.optimization_barrier((chunks[step - 1], [total] + following[:1]))
                flat[step - 1] = forward(first, step - 1, ctx_count)
            flat.append(forward(chunk, step, ctx_count) if step > 1 or last else None)
    if aligned:
        late_steps, spots = list(range(late_from, ctx_count)), ctx_count
    else:
        whole = jnp.roll(jnp.stack(chunks), ctx_index, axis=0)
        whole = whole.transpose(1, 0, 2).reshape(part_rows, width)
        flat.append(forward(whole, 0, 1))
        hidden = collect([0], 1)
        late_steps, spots = [], 1
    places = jnp.stack([ctx_index, exp_index])
    out = None
    for back in range(exp_count):
        operands = (
            [places]
            + [flat[step][back] for step in late_steps]
            + [hidden[back], all_ids[back], keep_counts.reshape(1, -1)]
            + [norm_gain.reshape(1, -1), router.T]
        )
        kept = [] if out is None else [out]
        out = pl.pallas_call(
            functools.partial(finish_kernel, late_steps, spots, back, exp_count),
            out_shape=jax.ShapeDtypeStruct((exp_count, experts_here, CAP, width), bf16),
            in_specs=[smem] + [vmem] * (len(operands) - 1) + [anywhere] * len(kept),
            out_specs=anywhere,
            scratch_shapes=[
                pltpu.VMEM((part_rows, width), f32),
                pltpu.VMEM((part_rows, width), bf16),
                pltpu.VMEM((experts_here, CAP, width), bf16),
                pltpu.SemaphoreType.DMA,
            ],
            input_output_aliases={len(operands): 0} if kept else {},
            compiler_params=params,
        )(*operands, *kept)
    return out


def solution(mesh):
    placed = (
        P(("groups", "exp"), "ctx", "tp", None),
        P(("groups", "exp"), "ctx", "tp", None),
        P(("groups", "exp"), "ctx", "tp", None),
        P(("groups", "exp"), "ctx"),
        P(("groups", "exp"), ("ctx", "tp"), None),
        P("tp", "ctx"),
        P(),
        P(None, "exp"),
        P(("groups", "exp"), ("ctx", "tp"), None),
        P("groups"),
    )
    return jax.shard_map(
        on_device,
        mesh=mesh,
        in_specs=placed,
        out_specs=P(("groups", "ctx", "tp"), "exp", None, None),
        check_vma=False,
    )
```

```python
import functools
import math

import jax
import jax.numpy as jnp
from jax import lax
from jax.experimental import pallas as pl
from jax.experimental.pallas import tpu as pltpu
from jax.sharding import PartitionSpec as P

CAP = 2
EPSILON = 1e-05
DOC_ROWS = 16
VMEM_LIMIT = 12 * 1024 * 1024
VMEM_ATTENTION = 16 * 1024 * 1024
VMEM_MOST = 61 * 1024 * 1024
VMEM_MUCH = 52 * 1024 * 1024


def fetch(refs, buffers, sems):
    copies = [
        pltpu.make_async_copy(ref, buffer, sems.at[number])
        for number, (ref, buffer) in enumerate(zip(refs, buffers))
    ]
    for copy in copies:
        copy.start()
    return [copy.wait for copy in copies]


def pack_kernel(groups, key_ref, value_ref, doc_ref, out_ref, *scratch):
    buffers, sems = scratch[:-1], scratch[-1]
    for wait in fetch((key_ref, value_ref, doc_ref), buffers, sems):
        wait()
    key_ref, value_ref, doc_ref = buffers
    rows, head_size = key_ref.shape
    tokens = rows // groups
    token = lax.broadcasted_iota(jnp.int32, (tokens, rows), 0)
    row = lax.broadcasted_iota(jnp.int32, (tokens, rows), 1)
    for group in range(groups):
        pick = (row == token * groups + group).astype(jnp.bfloat16)
        for place, ref in enumerate((key_ref, value_ref)):
            first = (place * groups + group) * tokens
            out_ref[first : first + tokens, :] = jnp.dot(
                pick, ref[...], preferred_element_type=jnp.float32
            ).astype(jnp.bfloat16)
    out_ref[2 * rows :, :] = jnp.broadcast_to(
        (doc_ref[...] + 1).astype(jnp.float32), (DOC_ROWS, tokens)
    ).astype(jnp.bfloat16)


def stage_kernel(count, *refs):
    for wait in fetch(refs[:count], refs[count:-1], refs[-1]):
        wait()


def attention_kernel(ratio, groups, pair, place_ref, query_ref, *refs):
    pack_refs, out_refs = refs[:-pair], refs[-pair:]
    heads, tokens, head_size = query_ref.shape
    scale = 1.0 / math.sqrt(head_size)
    core, ctx_index = place_ref[0], place_ref[1]
    part_rows = tokens // pair
    held_rows = groups * tokens
    rows = lax.broadcasted_iota(jnp.int32, (tokens, tokens), 0)
    columns = lax.broadcasted_iota(jnp.int32, (tokens, tokens), 1)
    docs = [ref[2 * held_rows : 2 * held_rows + 1, :].astype(jnp.float32) for ref in pack_refs]
    own_doc = jnp.sum(jnp.where(rows == columns, docs[0], 0.0), axis=1, keepdims=True)
    allowed = [(own_doc == docs[0]) & (columns <= rows)]
    for step, doc in enumerate(docs[1:], 1):
        allowed.append((own_doc == doc) & (ctx_index >= step))
    allowed = jnp.concatenate(allowed, axis=1)
    for group in range(groups):
        first = group * tokens
        keys = jnp.concatenate([ref[first : first + tokens, :] for ref in pack_refs], axis=0)
        first = held_rows + group * tokens
        held = jnp.concatenate([ref[first : first + tokens, :] for ref in pack_refs], axis=0)
        for head in range(group * ratio, (group + 1) * ratio):
            scores = lax.dot_general(
                query_ref[head], keys, (((1,), (1,)), ((), ())), preferred_element_type=jnp.float32
            )
            scores = jnp.where(allowed, scores * scale, -1e30)
            weights = jnp.exp(scores - jnp.max(scores, axis=1, keepdims=True))
            totals = jnp.sum(weights, axis=1, keepdims=True)
            mixed = jnp.dot(
                weights.astype(jnp.bfloat16), held, preferred_element_type=jnp.float32
            )
            mixed = (mixed / totals).astype(jnp.bfloat16)
            parts = [mixed[i * part_rows : (i + 1) * part_rows] for i in range(pair)]
            for turn in range(pair):
                piece = parts[turn]
                for own in range(1, pair):
                    piece = jnp.where(core == own, parts[(own + turn) % pair], piece)
                out_refs[turn][:, head * head_size : (head + 1) * head_size] = piece


def project_kernel(pair, *refs):
    block_refs, weight_refs, out_ref = refs[:pair], refs[pair : 2 * pair], refs[2 * pair]
    total = None
    for block_ref, weight_ref in zip(block_refs, weight_refs):
        product = jnp.dot(block_ref[...], weight_ref[...], preferred_element_type=jnp.float32)
        total = product if total is None else total + product
    out_ref[...] = total.astype(out_ref.dtype)


def columns_of(chunk_ref, step, spots, ctx_index):
    columns = chunk_ref.shape[1]
    first = 0 if spots == 1 else lax.rem(ctx_index + spots - step, spots) * columns
    return pl.ds(pl.multiple_of(first, 128), columns)


def hidden_kernel(step, spots, place_ref, residual_ref, chunk_ref, out_ref):
    part = columns_of(chunk_ref, step, spots, place_ref[0])
    out_ref[...] = (
        residual_ref[:, part].astype(jnp.float32) + chunk_ref[...].astype(jnp.float32)
    ).astype(out_ref.dtype)


def collect_kernel(steps, spots, exp_count, place_ref, *refs):
    count = len(steps)
    chunk_refs, out_refs = refs[:-exp_count], refs[-exp_count:]
    for back, out_ref in enumerate(out_refs):
        for step, chunk_ref in zip(steps, chunk_refs[back * count : (back + 1) * count]):
            out_ref[:, columns_of(chunk_ref, step, spots, place_ref[0])] = chunk_ref[...]


def finish_kernel(steps, spots, back, exp_count, place_ref, *refs):
    count = len(steps)
    chunk_refs = refs[:count]
    hidden_ref, id_ref, keep_ref, gain_ref, router_ref = refs[count : count + 5]
    out_ref, total_ref, normed_ref, result_ref, out_sem = refs[-5:]
    rows, width = hidden_ref.shape
    experts = keep_ref.shape[1]
    here = router_ref.shape[0]
    ctx_index, exp_index = place_ref[0], place_ref[1]
    keep = keep_ref[...].astype(jnp.float32)
    upper = (
        lax.broadcasted_iota(jnp.int32, (rows, rows), 0)
        < lax.broadcasted_iota(jnp.int32, (rows, rows), 1)
    ).astype(jnp.bfloat16)
    total_ref[...] = hidden_ref[...].astype(jnp.float32)
    for step, chunk_ref in zip(steps, chunk_refs):
        part = columns_of(chunk_ref, step, spots, ctx_index)
        total_ref[:, part] = chunk_ref[...].astype(jnp.float32)
    hidden = total_ref[...]
    power = jnp.sum(hidden * hidden, axis=1, keepdims=True)
    factor = lax.rsqrt(power / width + EPSILON)
    normed_ref[...] = (hidden * factor * gain_ref[...].astype(jnp.float32)).astype(jnp.bfloat16)
    ids = id_ref[...]
    onehot = (ids == lax.broadcasted_iota(jnp.int32, (experts, rows), 0)).astype(jnp.float32)
    earlier = jnp.dot(onehot.astype(jnp.bfloat16), upper, preferred_element_type=jnp.float32)
    ranking = jnp.sum(onehot * earlier, axis=0, keepdims=True)
    limits = jnp.dot(
        keep.astype(jnp.bfloat16),
        onehot.astype(jnp.bfloat16),
        preferred_element_type=jnp.float32,
    )
    local = ids - exp_index * here
    logits = lax.dot_general(
        router_ref[...],
        normed_ref[...],
        (((1,), (1,)), ((), ())),
        preferred_element_type=jnp.float32,
    )
    chosen = local == lax.broadcasted_iota(jnp.int32, (here, rows), 0)
    gates = jax.nn.sigmoid(jnp.sum(jnp.where(chosen, logits, 0.0), axis=0, keepdims=True))
    target = local * CAP + ranking.astype(jnp.int32)
    target = jnp.where((ranking < limits) & (local >= 0) & (local < here), target, -1)
    table = lax.broadcasted_iota(jnp.int32, (here * CAP, rows), 0) == target
    slot_gates = jnp.sum(jnp.where(table, gates, 0.0), axis=1, keepdims=True)
    slots = jnp.dot(
        table.astype(jnp.bfloat16), normed_ref[...], preferred_element_type=jnp.float32
    )
    result_ref[...] = (slots * slot_gates).astype(jnp.bfloat16).reshape(result_ref.shape)
    source = lax.rem(exp_index - back + exp_count, exp_count)
    copy = pltpu.make_async_copy(result_ref, out_ref.at[source], out_sem)
    copy.start()
    copy.wait()


def on_device(
    queries,
    key_states,
    values,
    doc_ids,
    residual,
    out_proj,
    norm_gain,
    router,
    expert_ids,
    keep_counts,
):
    _, tokens, heads, head_size = queries.shape
    groups = key_states.shape[2]
    ctx_count = lax.axis_size("ctx")
    pair = lax.axis_size("tp")
    exp_count = lax.axis_size("exp")
    part_rows = tokens // pair
    width = residual.shape[2]
    columns = out_proj.shape[1]
    experts_here = router.shape[1]
    ctx_index = lax.axis_index("ctx")
    core = lax.axis_index("tp")
    exp_index = lax.axis_index("exp")
    reach = -(-(ctx_count * tokens // 2 - 1) // tokens)
    vmem = pl.BlockSpec(memory_space=pltpu.VMEM)
    smem = pl.BlockSpec(memory_space=pltpu.SMEM)
    anywhere = pl.BlockSpec(memory_space=pl.ANY)
    params = pltpu.CompilerParams(vmem_limit_bytes=VMEM_LIMIT)
    most = pltpu.CompilerParams(vmem_limit_bytes=VMEM_MOST)
    much = pltpu.CompilerParams(vmem_limit_bytes=VMEM_MUCH)
    bf16, f32 = jnp.bfloat16, jnp.float32

    def over(array, axis, step):
        count = lax.axis_size(axis)
        if step % count == 0:
            return array
        return lax.ppermute(array, axis, [(i, (i + step) % count) for i in range(count)])

    def along(array, moves):
        return lax.ppermute(array, "ctx", moves)

    pack = pl.pallas_call(
        functools.partial(pack_kernel, groups),
        out_shape=jax.ShapeDtypeStruct((2 * groups * tokens + DOC_ROWS, head_size), bf16),
        in_specs=[anywhere] * 3,
        out_specs=vmem,
        scratch_shapes=[pltpu.VMEM((groups * tokens, head_size), bf16)] * 2
        + [pltpu.VMEM(doc_ids.shape, doc_ids.dtype), pltpu.SemaphoreType.DMA((3,))],
        compiler_params=most,
    )(
        key_states.reshape(groups * tokens, head_size),
        values.reshape(groups * tokens, head_size),
        doc_ids,
    )
    packs = [pack] + [
        lax.ppermute(
            pack,
            "ctx",
            [
                (i, (i + step) % ctx_count)
                for i in range(ctx_count if step == 1 else ctx_count - step)
            ],
        )
        for step in range(1, reach + 1)
    ]
    ids, own_residual = expert_ids[:, :, 0], residual[0]
    weights = [over(out_proj, "tp", turn) for turn in range(pair)]
    pack, own_queries = lax.optimization_barrier((pack, queries[0].transpose(1, 0, 2)))
    staged_queries, packs[0] = pl.pallas_call(
        functools.partial(stage_kernel, 2),
        out_shape=[
            jax.ShapeDtypeStruct(own_queries.shape, bf16),
            jax.ShapeDtypeStruct(pack.shape, bf16),
        ],
        in_specs=[anywhere] * 2,
        out_specs=[vmem] * 2,
        scratch_shapes=[pltpu.SemaphoreType.DMA((2,))],
        compiler_params=much,
    )(own_queries, pack)
    all_ids = [ids] + [over(ids, "exp", back) for back in range(1, exp_count)]
    staged_queries, all_ids = lax.optimization_barrier((staged_queries, all_ids))
    pieces = pl.pallas_call(
        functools.partial(attention_kernel, heads // groups, groups, pair),
        out_shape=[jax.ShapeDtypeStruct((part_rows, heads * head_size), bf16)] * pair,
        in_specs=[smem] + [vmem] * (1 + len(packs)),
        out_specs=[vmem] * pair,
        compiler_params=pltpu.CompilerParams(vmem_limit_bytes=VMEM_ATTENTION),
    )(jnp.stack([core, ctx_index]), staged_queries, *packs)

    project = pl.pallas_call(
        functools.partial(project_kernel, pair),
        out_shape=jax.ShapeDtypeStruct((part_rows, columns), bf16),
        in_specs=[vmem] * (2 * pair),
        out_specs=vmem,
        compiler_params=params,
        cost_estimate=pl.CostEstimate(
            flops=2 * pair * part_rows * out_proj.size,
            bytes_accessed=2 * pair * out_proj.size,
            transcendentals=0,
        ),
    )
    block = [over(pieces[turn], "tp", turn) for turn in range(pair)]
    block[-1], weights = lax.optimization_barrier((block[-1], weights))
    weights = pl.pallas_call(
        functools.partial(stage_kernel, pair),
        out_shape=[jax.ShapeDtypeStruct(out_proj.shape, bf16)] * pair,
        in_specs=[anywhere] * pair,
        out_specs=[vmem] * pair,
        scratch_shapes=[pltpu.SemaphoreType.DMA((pair,))],
        compiler_params=params,
    )(*weights)

    aligned = columns % 128 == 0
    hidden = None

    def forward(chunk, step, spots):
        hidden = pl.pallas_call(
            functools.partial(hidden_kernel, step, spots),
            out_shape=jax.ShapeDtypeStruct(chunk.shape, bf16),
            in_specs=[smem] + [vmem] * 2,
            out_specs=vmem,
            compiler_params=params,
        )(ctx_index.reshape(1), own_residual, chunk)
        return [over(hidden, "exp", back) for back in range(exp_count)]

    def collect(steps, spots):
        arrays = [flat[step][back] for back in range(exp_count) for step in steps]
        return pl.pallas_call(
            functools.partial(collect_kernel, steps, spots, exp_count),
            out_shape=[jax.ShapeDtypeStruct((part_rows, width), bf16)] * exp_count,
            in_specs=[smem] + [vmem] * len(arrays),
            out_specs=[vmem] * exp_count,
            compiler_params=params,
        )(ctx_index.reshape(1), *arrays)

    chunks, flat = [], []
    late_from = max(1, ctx_count - 2)
    for step in range(ctx_count):
        last = step == ctx_count - 1
        following = None if last else [over(array, "ctx", -1) for array in block]
        if step == 2:
            block, chunks[1] = lax.optimization_barrier((block, chunks[1]))
        if step == 3 and aligned:
            block, flat[0] = lax.optimization_barrier((block, flat[0]))
        if last and aligned:
            hidden = collect(list(range(late_from)), ctx_count)
        total = project(*block, *weights)
        chunk = over(total, "ctx", step)
        if not last:
            block = [lax.optimization_barrier((array, total))[0] for array in following]
        if last and aligned:
            chunk, hidden = lax.optimization_barrier((chunk, hidden))
        chunks.append(chunk)
        if aligned:
            if step in (1, 2) and not last:
                first, _ = lax.optimization_barrier((chunks[step - 1], [total] + following[:1]))
                flat[step - 1] = forward(first, step - 1, ctx_count)
            flat.append(forward(chunk, step, ctx_count) if step > 1 or last else None)
    if aligned:
        late_steps, spots = list(range(late_from, ctx_count)), ctx_count
    else:
        whole = jnp.roll(jnp.stack(chunks[:1] + chunks[:0:-1]), ctx_index, axis=0)
        whole = whole.transpose(1, 0, 2).reshape(part_rows, width)
        flat.append(forward(whole, 0, 1))
        hidden = collect([0], 1)
        late_steps, spots = [], 1
    places = jnp.stack([ctx_index, exp_index])
    out = None
    for back in range(exp_count):
        operands = (
            [places]
            + [flat[step][back] for step in late_steps]
            + [hidden[back], all_ids[back], keep_counts.reshape(1, -1)]
            + [norm_gain.reshape(1, -1), router.T]
        )
        kept = [] if out is None else [out]
        out = pl.pallas_call(
            functools.partial(finish_kernel, late_steps, spots, back, exp_count),
            out_shape=jax.ShapeDtypeStruct((exp_count, experts_here, CAP, width), bf16),
            in_specs=[smem] + [vmem] * (len(operands) - 1) + [anywhere] * len(kept),
            out_specs=anywhere,
            scratch_shapes=[
                pltpu.VMEM((part_rows, width), f32),
                pltpu.VMEM((part_rows, width), bf16),
                pltpu.VMEM((experts_here, CAP, width), bf16),
                pltpu.SemaphoreType.DMA,
            ],
            input_output_aliases={len(operands): 0} if kept else {},
            compiler_params=params,
        )(*operands, *kept)
    return out


def solution(mesh):
    placed = (
        P(("groups", "exp"), "ctx", "tp", None),
        P(("groups", "exp"), "ctx", "tp", None),
        P(("groups", "exp"), "ctx", "tp", None),
        P(("groups", "exp"), "ctx"),
        P(("groups", "exp"), ("ctx", "tp"), None),
        P("tp", "ctx"),
        P(),
        P(None, "exp"),
        P(("groups", "exp"), ("ctx", "tp"), None),
        P("groups"),
    )
    return jax.shard_map(
        on_device,
        mesh=mesh,
        in_specs=placed,
        out_specs=P(("groups", "ctx", "tp"), "exp", None, None),
        check_vma=False,
    )
```

```python
import functools
import math

import jax
import jax.numpy as jnp
from jax import lax
from jax.experimental import pallas as pl
from jax.experimental.pallas import tpu as pltpu
from jax.sharding import PartitionSpec as P

CAP = 2
EPSILON = 1e-05
DOC_ROWS = 16
VMEM_LIMIT = 12 * 1024 * 1024
VMEM_ATTENTION = 16 * 1024 * 1024
VMEM_MOST = 61 * 1024 * 1024
VMEM_MUCH = 52 * 1024 * 1024


def fetch(refs, buffers, sems):
    copies = [
        pltpu.make_async_copy(ref, buffer, sems.at[number])
        for number, (ref, buffer) in enumerate(zip(refs, buffers))
    ]
    for copy in copies:
        copy.start()
    return [copy.wait for copy in copies]


def pack_kernel(groups, key_ref, value_ref, doc_ref, out_ref, *scratch):
    buffers, sems = scratch[:-1], scratch[-1]
    for wait in fetch((key_ref, value_ref, doc_ref), buffers, sems):
        wait()
    key_ref, value_ref, doc_ref = buffers
    rows, head_size = key_ref.shape
    tokens = rows // groups
    token = lax.broadcasted_iota(jnp.int32, (tokens, rows), 0)
    row = lax.broadcasted_iota(jnp.int32, (tokens, rows), 1)
    for group in range(groups):
        pick = (row == token * groups + group).astype(jnp.bfloat16)
        for place, ref in enumerate((key_ref, value_ref)):
            first = (place * groups + group) * tokens
            out_ref[first : first + tokens, :] = jnp.dot(
                pick, ref[...], preferred_element_type=jnp.float32
            ).astype(jnp.bfloat16)
    out_ref[2 * rows :, :] = jnp.broadcast_to(
        (doc_ref[...] + 1).astype(jnp.float32), (DOC_ROWS, tokens)
    ).astype(jnp.bfloat16)


def stage_kernel(count, *refs):
    for wait in fetch(refs[:count], refs[count:-1], refs[-1]):
        wait()


def attention_kernel(ratio, groups, pair, place_ref, query_ref, *refs):
    pack_refs, out_refs = refs[:-pair], refs[-pair:]
    heads, tokens, head_size = query_ref.shape
    scale = 1.0 / math.sqrt(head_size)
    core, ctx_index = place_ref[0], place_ref[1]
    part_rows = tokens // pair
    held_rows = groups * tokens
    rows = lax.broadcasted_iota(jnp.int32, (tokens, tokens), 0)
    columns = lax.broadcasted_iota(jnp.int32, (tokens, tokens), 1)
    docs = [ref[2 * held_rows : 2 * held_rows + 1, :].astype(jnp.float32) for ref in pack_refs]
    own_doc = jnp.sum(jnp.where(rows == columns, docs[0], 0.0), axis=1, keepdims=True)
    allowed = [(own_doc == docs[0]) & (columns <= rows)]
    for step, doc in enumerate(docs[1:], 1):
        allowed.append((own_doc == doc) & (ctx_index >= step))
    allowed = jnp.concatenate(allowed, axis=1)
    for group in range(groups):
        first = group * tokens
        keys = jnp.concatenate([ref[first : first + tokens, :] for ref in pack_refs], axis=0)
        first = held_rows + group * tokens
        held = jnp.concatenate([ref[first : first + tokens, :] for ref in pack_refs], axis=0)
        for head in range(group * ratio, (group + 1) * ratio):
            scores = lax.dot_general(
                query_ref[head], keys, (((1,), (1,)), ((), ())), preferred_element_type=jnp.float32
            )
            scores = jnp.where(allowed, scores * scale, -1e30)
            weights = jnp.exp(scores - jnp.max(scores, axis=1, keepdims=True))
            totals = jnp.sum(weights, axis=1, keepdims=True)
            mixed = jnp.dot(
                weights.astype(jnp.bfloat16), held, preferred_element_type=jnp.float32
            )
            mixed = (mixed / totals).astype(jnp.bfloat16)
            parts = [mixed[i * part_rows : (i + 1) * part_rows] for i in range(pair)]
            for turn in range(pair):
                piece = parts[turn]
                for own in range(1, pair):
                    piece = jnp.where(core == own, parts[(own + turn) % pair], piece)
                out_refs[turn][:, head * head_size : (head + 1) * head_size] = piece


def project_kernel(pair, *refs):
    block_refs, weight_refs, out_ref = refs[:pair], refs[pair : 2 * pair], refs[2 * pair]
    total = None
    for block_ref, weight_ref in zip(block_refs, weight_refs):
        product = jnp.dot(block_ref[...], weight_ref[...], preferred_element_type=jnp.float32)
        total = product if total is None else total + product
    out_ref[...] = total.astype(out_ref.dtype)


def columns_of(chunk_ref, step, spots, ctx_index):
    columns = chunk_ref.shape[1]
    first = 0 if spots == 1 else lax.rem(ctx_index + spots - step, spots) * columns
    return pl.ds(pl.multiple_of(first, 128), columns)


def hidden_kernel(step, spots, place_ref, residual_ref, chunk_ref, out_ref):
    part = columns_of(chunk_ref, step, spots, place_ref[0])
    out_ref[...] = (
        residual_ref[:, part].astype(jnp.float32) + chunk_ref[...].astype(jnp.float32)
    ).astype(out_ref.dtype)


def collect_kernel(steps, spots, exp_count, place_ref, *refs):
    count = len(steps)
    chunk_refs, out_refs = refs[:-exp_count], refs[-exp_count:]
    for back, out_ref in enumerate(out_refs):
        for step, chunk_ref in zip(steps, chunk_refs[back * count : (back + 1) * count]):
            out_ref[:, columns_of(chunk_ref, step, spots, place_ref[0])] = chunk_ref[...]


def finish_kernel(steps, spots, back, exp_count, place_ref, *refs):
    count = len(steps)
    chunk_refs = refs[:count]
    hidden_ref, id_ref, keep_ref, gain_ref, router_ref = refs[count : count + 5]
    out_ref, total_ref, normed_ref, result_ref, out_sem = refs[-5:]
    rows, width = hidden_ref.shape
    experts = keep_ref.shape[1]
    here = router_ref.shape[0]
    ctx_index, exp_index = place_ref[0], place_ref[1]
    keep = keep_ref[...].astype(jnp.float32)
    upper = (
        lax.broadcasted_iota(jnp.int32, (rows, rows), 0)
        < lax.broadcasted_iota(jnp.int32, (rows, rows), 1)
    ).astype(jnp.bfloat16)
    total_ref[...] = hidden_ref[...]
    for step, chunk_ref in zip(steps, chunk_refs):
        total_ref[:, columns_of(chunk_ref, step, spots, ctx_index)] = chunk_ref[...]
    pieces = out_sem.shape[0]
    piece = width // pieces
    parts = [slice(number * piece, (number + 1) * piece) for number in range(pieces)]
    power = jnp.zeros((rows, 1), jnp.float32)
    for part in parts:
        hidden = total_ref[:, part].astype(jnp.float32)
        power = power + jnp.sum(hidden * hidden, axis=1, keepdims=True)
    factor = lax.rsqrt(power / width + EPSILON)
    for part in parts:
        gain = gain_ref[:, part].astype(jnp.float32)
        hidden = total_ref[:, part].astype(jnp.float32)
        normed_ref[:, part] = (hidden * factor * gain).astype(jnp.bfloat16)
    ids = id_ref[...]
    onehot = (ids == lax.broadcasted_iota(jnp.int32, (experts, rows), 0)).astype(jnp.float32)
    earlier = jnp.dot(onehot.astype(jnp.bfloat16), upper, preferred_element_type=jnp.float32)
    ranking = jnp.sum(onehot * earlier, axis=0, keepdims=True)
    limits = jnp.dot(
        keep.astype(jnp.bfloat16),
        onehot.astype(jnp.bfloat16),
        preferred_element_type=jnp.float32,
    )
    local = ids - exp_index * here
    logits = lax.dot_general(
        router_ref[...],
        normed_ref[...],
        (((1,), (1,)), ((), ())),
        preferred_element_type=jnp.float32,
    )
    chosen = local == lax.broadcasted_iota(jnp.int32, (here, rows), 0)
    gates = jax.nn.sigmoid(jnp.sum(jnp.where(chosen, logits, 0.0), axis=0, keepdims=True))
    target = local * CAP + ranking.astype(jnp.int32)
    target = jnp.where((ranking < limits) & (local >= 0) & (local < here), target, -1)
    table = lax.broadcasted_iota(jnp.int32, (here * CAP, rows), 0) == target
    slot_gates = jnp.sum(jnp.where(table, gates, 0.0), axis=1, keepdims=True)
    table = table.astype(jnp.bfloat16)
    source = lax.rem(exp_index - back + exp_count, exp_count)
    copies = []
    for number, part in enumerate(parts):
        slots = jnp.dot(table, normed_ref[:, part], preferred_element_type=jnp.float32)
        result_ref[:, :, part] = (
            (slots * slot_gates).astype(jnp.bfloat16).reshape(here, CAP, piece)
        )
        copy = pltpu.make_async_copy(
            result_ref.at[:, :, part], out_ref.at[source, :, :, part], out_sem.at[number]
        )
        copy.start()
        copies.append(copy)
    for copy in copies:
        copy.wait()


def on_device(
    queries,
    key_states,
    values,
    doc_ids,
    residual,
    out_proj,
    norm_gain,
    router,
    expert_ids,
    keep_counts,
):
    _, tokens, heads, head_size = queries.shape
    groups = key_states.shape[2]
    ctx_count = lax.axis_size("ctx")
    pair = lax.axis_size("tp")
    exp_count = lax.axis_size("exp")
    part_rows = tokens // pair
    width = residual.shape[2]
    columns = out_proj.shape[1]
    experts_here = router.shape[1]
    ctx_index = lax.axis_index("ctx")
    core = lax.axis_index("tp")
    exp_index = lax.axis_index("exp")
    reach = -(-(ctx_count * tokens // 2 - 1) // tokens)
    vmem = pl.BlockSpec(memory_space=pltpu.VMEM)
    smem = pl.BlockSpec(memory_space=pltpu.SMEM)
    anywhere = pl.BlockSpec(memory_space=pl.ANY)
    params = pltpu.CompilerParams(vmem_limit_bytes=VMEM_LIMIT)
    most = pltpu.CompilerParams(vmem_limit_bytes=VMEM_MOST)
    much = pltpu.CompilerParams(vmem_limit_bytes=VMEM_MUCH)
    bf16, f32 = jnp.bfloat16, jnp.float32

    def over(array, axis, step):
        count = lax.axis_size(axis)
        if step % count == 0:
            return array
        return lax.ppermute(array, axis, [(i, (i + step) % count) for i in range(count)])

    def along(array, moves):
        return lax.ppermute(array, "ctx", moves)

    pack = pl.pallas_call(
        functools.partial(pack_kernel, groups),
        out_shape=jax.ShapeDtypeStruct((2 * groups * tokens + DOC_ROWS, head_size), bf16),
        in_specs=[anywhere] * 3,
        out_specs=vmem,
        scratch_shapes=[pltpu.VMEM((groups * tokens, head_size), bf16)] * 2
        + [pltpu.VMEM(doc_ids.shape, doc_ids.dtype), pltpu.SemaphoreType.DMA((3,))],
        compiler_params=most,
    )(
        key_states.reshape(groups * tokens, head_size),
        values.reshape(groups * tokens, head_size),
        doc_ids,
    )
    packs = [pack] + [
        lax.ppermute(
            pack,
            "ctx",
            [
                (i, (i + step) % ctx_count)
                for i in range(ctx_count if step == 1 else ctx_count - step)
            ],
        )
        for step in range(1, reach + 1)
    ]
    ids, own_residual = expert_ids[:, :, 0], residual[0]
    weights = [over(out_proj, "tp", turn) for turn in range(pair)]
    pack, own_queries = lax.optimization_barrier((pack, queries[0].transpose(1, 0, 2)))
    staged_queries, packs[0] = pl.pallas_call(
        functools.partial(stage_kernel, 2),
        out_shape=[
            jax.ShapeDtypeStruct(own_queries.shape, bf16),
            jax.ShapeDtypeStruct(pack.shape, bf16),
        ],
        in_specs=[anywhere] * 2,
        out_specs=[vmem] * 2,
        scratch_shapes=[pltpu.SemaphoreType.DMA((2,))],
        compiler_params=much,
    )(own_queries, pack)
    all_ids = [ids] + [over(ids, "exp", back) for back in range(1, exp_count)]
    staged_queries, all_ids = lax.optimization_barrier((staged_queries, all_ids))
    pieces = pl.pallas_call(
        functools.partial(attention_kernel, heads // groups, groups, pair),
        out_shape=[jax.ShapeDtypeStruct((part_rows, heads * head_size), bf16)] * pair,
        in_specs=[smem] + [vmem] * (1 + len(packs)),
        out_specs=[vmem] * pair,
        compiler_params=pltpu.CompilerParams(vmem_limit_bytes=VMEM_ATTENTION),
    )(jnp.stack([core, ctx_index]), staged_queries, *packs)

    project = pl.pallas_call(
        functools.partial(project_kernel, pair),
        out_shape=jax.ShapeDtypeStruct((part_rows, columns), bf16),
        in_specs=[vmem] * (2 * pair),
        out_specs=vmem,
        compiler_params=params,
        cost_estimate=pl.CostEstimate(
            flops=2 * pair * part_rows * out_proj.size,
            bytes_accessed=2 * pair * out_proj.size,
            transcendentals=0,
        ),
    )
    block = [over(pieces[turn], "tp", turn) for turn in range(pair)]
    block[-1], weights = lax.optimization_barrier((block[-1], weights))
    weights = pl.pallas_call(
        functools.partial(stage_kernel, pair),
        out_shape=[jax.ShapeDtypeStruct(out_proj.shape, bf16)] * pair,
        in_specs=[anywhere] * pair,
        out_specs=[vmem] * pair,
        scratch_shapes=[pltpu.SemaphoreType.DMA((pair,))],
        compiler_params=params,
    )(*weights)

    aligned = columns % 128 == 0
    hidden = None

    def forward(chunk, step, spots):
        hidden = pl.pallas_call(
            functools.partial(hidden_kernel, step, spots),
            out_shape=jax.ShapeDtypeStruct(chunk.shape, bf16),
            in_specs=[smem] + [vmem] * 2,
            out_specs=vmem,
            compiler_params=params,
        )(ctx_index.reshape(1), own_residual, chunk)
        return [over(hidden, "exp", back) for back in range(exp_count)]

    def collect(steps, spots):
        arrays = [flat[step][back] for back in range(exp_count) for step in steps]
        return pl.pallas_call(
            functools.partial(collect_kernel, steps, spots, exp_count),
            out_shape=[jax.ShapeDtypeStruct((part_rows, width), bf16)] * exp_count,
            in_specs=[smem] + [vmem] * len(arrays),
            out_specs=[vmem] * exp_count,
            compiler_params=params,
        )(ctx_index.reshape(1), *arrays)

    chunks, flat = [], []
    late_from = max(1, ctx_count - 2)
    for step in range(ctx_count):
        last = step == ctx_count - 1
        following = None if last else [over(array, "ctx", -1) for array in block]
        if step == 2:
            block, chunks[1] = lax.optimization_barrier((block, chunks[1]))
        if step == 3 and aligned:
            block, flat[0] = lax.optimization_barrier((block, flat[0]))
        if last and aligned:
            hidden = collect(list(range(late_from)), ctx_count)
        total = project(*block, *weights)
        chunk = over(total, "ctx", step)
        if not last:
            block = [lax.optimization_barrier((array, total))[0] for array in following]
        if last and aligned:
            chunk, hidden = lax.optimization_barrier((chunk, hidden))
        chunks.append(chunk)
        if aligned:
            if step in (1, 2) and not last:
                first, _ = lax.optimization_barrier((chunks[step - 1], [total] + following[:1]))
                flat[step - 1] = forward(first, step - 1, ctx_count)
            flat.append(forward(chunk, step, ctx_count) if step > 1 or last else None)
    if aligned:
        late_steps, spots = list(range(late_from, ctx_count)), ctx_count
    else:
        whole = jnp.roll(jnp.stack(chunks[:1] + chunks[:0:-1]), ctx_index, axis=0)
        whole = whole.transpose(1, 0, 2).reshape(part_rows, width)
        flat.append(forward(whole, 0, 1))
        hidden = collect([0], 1)
        late_steps, spots = [], 1
    places = jnp.stack([ctx_index, exp_index])
    out = None
    for back in range(exp_count):
        operands = (
            [places]
            + [flat[step][back] for step in late_steps]
            + [hidden[back], all_ids[back], keep_counts.reshape(1, -1)]
            + [norm_gain.reshape(1, -1), router.T]
        )
        kept = [] if out is None else [out]
        out = pl.pallas_call(
            functools.partial(finish_kernel, late_steps, spots, back, exp_count),
            out_shape=jax.ShapeDtypeStruct((exp_count, experts_here, CAP, width), bf16),
            in_specs=[smem] + [vmem] * (len(operands) - 1) + [anywhere] * len(kept),
            out_specs=anywhere,
            scratch_shapes=[
                pltpu.VMEM((part_rows, width), bf16),
                pltpu.VMEM((part_rows, width), bf16),
                pltpu.VMEM((experts_here, CAP, width), bf16),
                pltpu.SemaphoreType.DMA((5 if width % (5 * 128) == 0 else 1,)),
            ],
            input_output_aliases={len(operands): 0} if kept else {},
            compiler_params=params,
        )(*operands, *kept)
    return out


def solution(mesh):
    placed = (
        P(("groups", "exp"), "ctx", "tp", None),
        P(("groups", "exp"), "ctx", "tp", None),
        P(("groups", "exp"), "ctx", "tp", None),
        P(("groups", "exp"), "ctx"),
        P(("groups", "exp"), ("ctx", "tp"), None),
        P("tp", "ctx"),
        P(),
        P(None, "exp"),
        P(("groups", "exp"), ("ctx", "tp"), None),
        P("groups"),
    )
    return jax.shard_map(
        on_device,
        mesh=mesh,
        in_specs=placed,
        out_specs=P(("groups", "ctx", "tp"), "exp", None, None),
        check_vma=False,
    )
```
